32 devices in a mesh: replica: 4 (over x, core), fsdp: 4 (over z), tensor: 2 (over y).
Axes of the slice: x: 2, y: 2, z: 4, core: 2. Of those that a mesh axis runs over, the one named last changes fastest.
Arguments:
- images: bfloat16 [96, 729, 1152], P(('replica', 'fsdp')), may hold values from -6 to 6
- live: int32 [96], P(('replica', 'fsdp')), may hold values 0 or 1
- cotangent: bfloat16 [96, 729, 1152], P(('replica', 'fsdp')), may hold values from -6 to 6
- ln1_gain: float32 [1152], replicated, may hold values from 0.1 to 1.9
- ln1_bias: float32 [1152], replicated, may hold values from -3 to 3
- q_weight: float32 [1152, 1152], P('fsdp', 'tensor'), may hold values from -0.25 to 0.25
- q_bias: float32 [1152], replicated, may hold values from -3 to 3
- k_weight: float32 [1152, 1152], P('fsdp', 'tensor'), may hold values from -0.25 to 0.25
- v_weight: float32 [1152, 1152], P('fsdp', 'tensor'), may hold values from -0.1875 to 0.1875
- v_bias: float32 [1152], replicated, may hold values from -3 to 3
- o_weight: float32 [1152, 1152], P('tensor', 'fsdp'), may hold values from -0.75 to 0.75
- o_bias: float32 [1152], replicated, may hold values from -3 to 3
- ln2_gain: float32 [1152], replicated, may hold values from 0.1 to 1.9
- ln2_bias: float32 [1152], replicated, may hold values from -3 to 3
- fc1_weight: float32 [1152, 4304], P('fsdp', 'tensor'), may hold values from -1 to 1
- fc1_bias: float32 [4304], replicated, may hold values from -3 to 3
- fc2_weight: float32 [4304, 1152], P('tensor', 'fsdp'), may hold values from -0.09375 to 0.09375
- fc2_bias: float32 [1152], replicated, may hold values from -3 to 3
Outputs:
- output: bfloat16 [96, 729, 1152], P(('replica', 'fsdp'))
- input_grad: bfloat16 [96, 729, 1152], P(('replica', 'fsdp'))
- ln1_gain_grad: float32 [1152], P('tensor')
- ln1_bias_grad: float32 [1152], P('tensor')
- q_weight_grad: float32 [1152, 1152], P('fsdp', 'tensor')
- q_bias_grad: float32 [1152], P('tensor')
- k_weight_grad: float32 [1152, 1152], P('fsdp', 'tensor')
- v_weight_grad: float32 [1152, 1152], P('fsdp', 'tensor')
- v_bias_grad: float32 [1152], P('tensor')
- o_weight_grad: float32 [1152, 1152], P('tensor', 'fsdp')
- o_bias_grad: float32 [1152], P('tensor')
- ln2_gain_grad: float32 [1152], P('tensor')
- ln2_bias_grad: float32 [1152], P('tensor')
- fc1_weight_grad: float32 [1152, 4304], P('fsdp', 'tensor')
- fc1_bias_grad: float32 [4304], P('tensor')
- fc2_weight_grad: float32 [4304, 1152], P('tensor', 'fsdp')
- fc2_bias_grad: float32 [1152], P('tensor')
The draws below stay inside these ranges and needn't reach their ends.
Inputs may be any that keep to these rules, and one draw needn't show every extreme that they name: `live`: 1 marks a slot that holds an image, 0 an empty slot.
All inputs are finite; a program needn't handle non-finite values. No bound on the sum of `live` on one device may be relied on, other than what follows from the above.
Results may differ from the reference program's by a relative error of at most 0.018.
Values may be sent and summed in bfloat16 or wider, within the bound.
No kernel may reach another device: no remote copies, remote signals or barrier semaphores. Data moves between devices by JAX's collectives and lax.ppermute only.
A program may use at most 640 MiB of HBM per device.

```python
import jax
import jax.numpy as jnp
from jax import lax

D = 1152
HEADS = 16
HEAD = 72
FF = 4304
SEQ = 729
SLOTS = 3
IMAGES = 96


def draw_fc1_weight(key, part):
    entry_key = jax.random.fold_in(key, 11)
    column_key = jax.random.fold_in(key, 12)
    scale_value = D ** (-0.5)
    entries = jax.random.truncated_normal(entry_key, -4.0, 4.0, (D, FF), jnp.float32)
    columns = jax.random.truncated_normal(column_key, -4.0, 4.0, (FF,), jnp.float32)
    return (entries * scale_value + columns[None, :] * scale_value).astype(jnp.float32)


def touch_ends(values, rng, smallest, largest):
    extent = values.shape
    index_at = [jax.random.randint(jax.random.fold_in(rng, axis), (), 0, extent[axis]) for axis in range(len(extent))]
    values = values.at[tuple(index_at)].set(smallest)
    longest = extent.index(max(extent))
    index_at[longest] = (index_at[longest] + 1) % extent[longest]
    return values.at[tuple(index_at)].set(largest)


def steps_of(own_key, shape, shards, low, top_value):
    def one(axis_at, shards_of):
        draws = jax.random.uniform(jax.random.fold_in(jax.random.fold_in(own_key, 6), axis_at), (shards_of,), jnp.float32, low / len(shards), top_value / len(shards))
        return jnp.repeat(jnp.exp(draws), shape[axis_at] // shards_of).reshape((-1,) + (1,) * (len(shape) - axis_at - 1))

    loudness = one(*shards[0])
    for cut in shards[1:]:
        loudness = loudness * one(*cut)
    return loudness


def scatter_about(own_key, dims, scale, bound, cuts=(), held_as=jnp.bfloat16):
    values = jax.random.normal(own_key, dims, jnp.float32) * scale
    if len(cuts) > 0:
        values = steps_of(own_key, dims, cuts, -0.22, 0.18) * values
    return jnp.clip(values, min=-bound, max=bound).astype(held_as)


def setup_inputs(seed: int = 0) -> dict:
    keys = jax.random.split(jax.random.key(seed), 19)
    images = scatter_about(keys[0], (IMAGES, SEQ, D), 1.0, 6.0, ((0, 16),))
    live = touch_ends((jax.random.randint(keys[1], (IMAGES,), 0, 4) < 3).astype(jnp.int32), jax.random.fold_in(keys[1], 1), 0, 1)
    cotangent = scatter_about(keys[2], (IMAGES, SEQ, D), 1.0, 6.0, ((0, 16),))
    ln1_gain = jnp.clip(1.0 + 0.18 * jax.random.normal(keys[3], (D,), jnp.float32), 0.1, 1.9)
    ln1_bias = scatter_about(keys[4], (D,), 0.3, 3.0, (), jnp.float32)
    q_weight = scatter_about(keys[5], (D, HEADS * HEAD), (D // 2) ** -0.5, 0.25, ((0, 4), (1, 2)), jnp.float32)
    q_bias = scatter_about(keys[6], (HEADS * HEAD,), 0.5, 3.0, (), jnp.float32)
    k_weight = scatter_about(keys[7], (D, HEADS * HEAD), (D // 2) ** -0.5, 0.25, ((0, 4), (1, 2)), jnp.float32)
    v_weight = scatter_about(keys[8], (D, HEADS * HEAD), D ** -0.5, 0.1875, ((0, 4), (1, 2)), jnp.float32)
    v_bias = scatter_about(keys[9], (HEADS * HEAD,), 0.5, 3.0, (), jnp.float32)
    o_weight = scatter_about(keys[10], (HEADS * HEAD, D), (HEADS * HEAD // 16) ** -0.5, 0.75, ((0, 2), (1, 4)), jnp.float32)
    o_bias = scatter_about(keys[11], (D,), 0.5, 3.0, (), jnp.float32)
    ln2_gain = jnp.clip(1.0 + 0.18 * jax.random.normal(keys[12], (D,), jnp.float32), 0.1, 1.9)
    ln2_bias = scatter_about(keys[13], (D,), 0.3, 3.0, (), jnp.float32)
    fc1_weight = draw_fc1_weight(jax.random.fold_in(keys[18], 71), 0)
    fc1_bias = scatter_about(keys[15], (FF,), 0.5, 3.0, (), jnp.float32)
    fc2_weight = scatter_about(keys[16], (FF, D), FF ** -0.5, 0.09375, ((0, 2), (1, 4)), jnp.float32)
    fc2_bias = scatter_about(keys[17], (D,), 0.5, 3.0, (), jnp.float32)
    return dict(images=images, live=live, cotangent=cotangent, ln1_gain=ln1_gain, ln1_bias=ln1_bias, q_weight=q_weight, q_bias=q_bias, k_weight=k_weight, v_weight=v_weight, v_bias=v_bias, o_weight=o_weight, o_bias=o_bias, ln2_gain=ln2_gain, ln2_bias=ln2_bias, fc1_weight=fc1_weight, fc1_bias=fc1_bias, fc2_weight=fc2_weight, fc2_bias=fc2_bias)


EPSILON = 1e-06
HIGHEST = lax.Precision.HIGHEST

@jax.custom_vjp
def low(v):
    return lax.optimization_barrier(v.astype(jnp.bfloat16)).astype(jnp.float32)

@jax.custom_vjp
def low_back(v):
    return v

def low_keep(v):
    return (low(v), None)

def low_pass(kept, grad):
    return (grad,)

def back_keep(v):
    return (v, None)

def back_low(kept, grad):
    return (low(grad),)
low.defvjp(low_keep, low_pass)
low_back.defvjp(back_keep, back_low)

def matmul(first_op, second_op):
    return jnp.dot(first_op, second_op, precision=HIGHEST, preferred_element_type=jnp.float32)

def layer_norm(values, gain_vec, shift_vec):
    center = lax.optimization_barrier(jnp.mean(values, axis=-1, keepdims=True))
    spread = lax.optimization_barrier(jnp.mean(values * values, axis=-1, keepdims=True)) - center * center
    return (values - center) * lax.rsqrt(spread + EPSILON) * gain_vec + shift_vec

def encoder_layer(tokens, params):
    gain_one, shift_one, q_weight, q_bias, k_weight, v_weight, v_bias, o_weight, o_bias, gain_two, shift_two, up_weight, up_bias, down_weight, down_bias = params
    blocks, length, width_all = tokens.shape
    row_count = blocks * length
    resid = tokens.reshape(row_count, width_all)
    first = low(layer_norm(resid, gain_one, shift_one))
    shape_four = (blocks, length, HEADS, HEAD)
    queries = low(low_back(matmul(first, low(q_weight)) + q_bias) * HEAD ** (-0.5)).reshape(shape_four)
    key_rows = low(low_back(matmul(first, low(k_weight)))).reshape(shape_four)
    value_rows = low(low_back(matmul(first, low(v_weight)) + v_bias)).reshape(shape_four)
    scores = low_back(jnp.einsum('bqhd,bkhd->bhqk', queries, key_rows, precision=HIGHEST))
    probs_low = low(jax.nn.softmax(scores, axis=-1))
    mixed_rows = low(low_back(jnp.einsum('bhqk,bkhd->bqhd', probs_low, value_rows, precision=HIGHEST)))
    mixed_rows = mixed_rows.reshape(row_count, HEADS * HEAD)
    middle = resid + low_back(matmul(mixed_rows, low(o_weight)) + o_bias)
    second = low(layer_norm(middle, gain_two, shift_two))
    upper_pre = low_back(matmul(second, low(up_weight)) + up_bias)
    hidden = low(jax.nn.gelu(upper_pre, approximate=True))
    result = middle + low_back(matmul(hidden, low(down_weight)) + down_bias)
    return result.reshape(blocks, length, width_all)

def reference(images, live, cotangent, ln1_gain, ln1_bias, q_weight, q_bias, k_weight, v_weight, v_bias, o_weight, o_bias, ln2_gain, ln2_bias, fc1_weight, fc1_bias, fc2_weight, fc2_bias):
    params = (ln1_gain, ln1_bias, q_weight, q_bias, k_weight, v_weight, v_bias, o_weight, o_bias, ln2_gain, ln2_bias, fc1_weight, fc1_bias, fc2_weight, fc2_bias)
    groups = images.shape[0] // SLOTS
    shape_five = (groups, SLOTS, SEQ, D)
    mask_all = live.astype(jnp.float32)[:, None, None]
    inputs = images.astype(jnp.float32).reshape(shape_five)
    cot_rows = (cotangent.astype(jnp.float32) * mask_all).reshape(shape_five)
    mask_groups = mask_all.reshape(groups, SLOTS, 1, 1)

    def step_group(carry, item):
        tokens, cot_group, mask_group = item
        result, pull = jax.vjp(encoder_layer, tokens, params)
        token_grad, param_grads = pull(cot_group)
        carry = jax.tree.map(jnp.add, carry, param_grads)
        return (carry, ((result * mask_group).astype(jnp.bfloat16), token_grad.astype(jnp.bfloat16)))
    zeros = jax.tree.map(jnp.zeros_like, params)
    totals, (outputs, grads_in) = lax.scan(step_group, zeros, (inputs, cot_rows, mask_groups))
    return (outputs.reshape(images.shape), grads_in.reshape(images.shape), totals[0], totals[1], totals[2], totals[3], totals[4], totals[5], totals[6], totals[7], totals[8], totals[9], totals[10], totals[11], totals[12], totals[13], totals[14])
```

```python
import functools

import jax
import jax.numpy as jnp
from jax import lax
from jax.experimental import pallas as pl
from jax.experimental.pallas import tpu as pltpu
from jax.sharding import PartitionSpec as P

HEAD = 72
MB = 2
SLOTS = 3


EPSILON = 1e-06


def matmul(first_op, second_op):
    return jnp.dot(first_op, second_op, preferred_element_type=jnp.float32)


def matmul_tn(first_op, second_op):
    return lax.dot_general(
        first_op, second_op, (((0,), (0,)), ((), ())), preferred_element_type=jnp.float32
    )


def matmul_nt(first_op, second_op):
    return lax.dot_general(
        first_op, second_op, (((1,), (1,)), ((), ())), preferred_element_type=jnp.float32
    )


def gelu_tanh(values):
    return jax.nn.gelu(values, approximate=True)


def row_totals(first_sum, second_sum):
    return lax.psum((first_sum, second_sum), "tensor")


def spread_whole(rounded):
    return lax.all_gather(rounded, "tensor", axis=1, tiled=True)


def combine_parts(partial_value):
    return lax.psum_scatter(partial_value, "tensor", scatter_dimension=1, tiled=True)


def normalize(stream, gain_vec, shift_vec):
    full_width = stream.shape[1] * lax.axis_size("tensor")
    totals = row_totals(
        jnp.sum(stream, axis=1, keepdims=True), jnp.sum(stream * stream, axis=1, keepdims=True)
    )
    center = totals[0] / full_width
    spread = totals[1] / full_width - center * center
    scale_inv = lax.rsqrt(spread + EPSILON)
    normed = (stream - center) * scale_inv
    rounded = (normed * gain_vec + shift_vec).astype(jnp.bfloat16)
    return (spread_whole(rounded), normed, scale_inv)


def norm_back(grad_part, normed, scale_inv, gain_vec):
    scaled = grad_part * gain_vec
    full_width = grad_part.shape[1] * lax.axis_size("tensor")
    totals = row_totals(
        jnp.sum(scaled, axis=1, keepdims=True), jnp.sum(scaled * normed, axis=1, keepdims=True)
    )
    mean_one = totals[0] / full_width
    mean_two = totals[1] / full_width
    return scale_inv * (scaled - mean_one - normed * mean_two)


def score_block(queries, key_rows):
    return jnp.einsum("bqhd,bkhd->bhqk", queries, key_rows, preferred_element_type=jnp.float32)


def forward_pass(stream, row_mask, weights, vectors, sizes_info):
    q_full, k_full, v_full, o_full, up_full, down_full = weights
    gain_one, shift_one, q_shift, v_shift, o_shift, gain_two, shift_two, up_shift, down_shift = (
        vectors
    )
    blocks, length, row_count, padded_rows = sizes_info
    head_count = q_shift.shape[0] // HEAD
    shape_four = (blocks, length, head_count, HEAD)
    first, normed_one, inv_one = normalize(stream, gain_one, shift_one)
    queries = (
        ((matmul(first, q_full) + q_shift) * HEAD ** (-0.5))
        .astype(jnp.bfloat16)
        .reshape(shape_four)
    )
    key_rows = matmul(first, k_full).astype(jnp.bfloat16).reshape(shape_four)
    value_rows = (matmul(first, v_full) + v_shift).astype(jnp.bfloat16).reshape(shape_four)
    scores = score_block(queries, key_rows)
    top_score = jnp.max(scores, axis=-1, keepdims=True)
    log_total = top_score + jnp.log(jnp.sum(jnp.exp(scores - top_score), axis=-1, keepdims=True))
    probs_bf = jnp.exp(scores - log_total).astype(jnp.bfloat16)
    attended = jnp.einsum(
        "bhqk,bkhd->bqhd", probs_bf, value_rows, preferred_element_type=jnp.float32
    )
    attended_bf = attended.reshape(row_count, head_count * HEAD).astype(jnp.bfloat16)
    middle = stream + combine_parts(matmul(attended_bf, o_full)) + o_shift
    second, normed_two, inv_two = normalize(middle, gain_two, shift_two)
    upper_pre = matmul(second, up_full) + up_shift
    hidden = gelu_tanh(upper_pre).astype(jnp.bfloat16)
    result = middle + combine_parts(matmul(hidden, down_full)) + down_shift
    output = (result * row_mask).astype(jnp.bfloat16)
    kept_state = (
        first,
        normed_one,
        inv_one,
        queries,
        key_rows,
        value_rows,
        log_total,
        attended_bf,
        normed_two,
        inv_two,
        second,
        upper_pre,
        hidden,
    )
    return (output, kept_state)


def backward_pass(cot_stream, row_mask, weights, vectors, kept_state, sizes_info):
    q_full, k_full, v_full, o_full, up_full, down_full = weights
    gain_one, shift_one, q_shift, v_shift, o_shift, gain_two, shift_two, up_shift, down_shift = (
        vectors
    )
    (
        first,
        normed_one,
        inv_one,
        queries,
        key_rows,
        value_rows,
        log_total,
        attended_bf,
        normed_two,
        inv_two,
        second,
        upper_pre,
        hidden,
    ) = kept_state
    blocks, length, row_count, padded_rows = sizes_info
    shape_four = queries.shape
    out_grad = cot_stream.astype(jnp.float32) * row_mask
    out_whole = spread_whole(out_grad.astype(jnp.bfloat16))
    down_grad = matmul_tn(hidden, out_whole)
    hidden_grad = matmul_nt(out_whole, down_full)
    upper_grad = jax.vjp(gelu_tanh, upper_pre)[1](hidden_grad)[0].astype(jnp.bfloat16)
    up_grad = matmul_tn(second, upper_grad)
    second_grad = combine_parts(matmul_nt(upper_grad, up_full))
    middle_grad = out_grad + norm_back(second_grad, normed_two, inv_two, gain_two)
    middle_bf = middle_grad.astype(jnp.bfloat16)
    middle_whole = spread_whole(middle_bf)
    o_grad = matmul_tn(attended_bf, middle_whole)
    attended_grad = matmul_nt(middle_whole, o_full).astype(jnp.bfloat16).reshape(shape_four)
    scores = score_block(queries, key_rows)
    probs = jnp.exp(scores - log_total)
    probs_bf = probs.astype(jnp.bfloat16)
    prob_grad = jnp.einsum(
        "bqhd,bkhd->bhqk", attended_grad, value_rows, preferred_element_type=jnp.float32
    )
    value_grad = jnp.einsum(
        "bhqk,bqhd->bkhd", probs_bf, attended_grad, preferred_element_type=jnp.float32
    )
    value_grad = value_grad.reshape(row_count, -1).astype(jnp.bfloat16)
    row_dot = jnp.sum(prob_grad * probs, axis=-1, keepdims=True)
    score_grad = (probs * (prob_grad - row_dot)).astype(jnp.bfloat16)
    query_grad = jnp.einsum(
        "bhqk,bkhd->bqhd", score_grad, key_rows, preferred_element_type=jnp.float32
    )
    query_grad = (query_grad.reshape(row_count, -1) * HEAD ** (-0.5)).astype(jnp.bfloat16)
    key_grad = jnp.einsum(
        "bhqk,bqhd->bkhd", score_grad, queries, preferred_element_type=jnp.float32
    )
    key_grad = key_grad.reshape(row_count, -1).astype(jnp.bfloat16)
    first_grad = combine_parts(
        matmul_nt(query_grad, q_full) + matmul_nt(key_grad, k_full) + matmul_nt(value_grad, v_full)
    )
    input_grad = middle_grad + norm_back(first_grad, normed_one, inv_one, gain_one)
    matrices = (
        matmul_tn(first, query_grad),
        matmul_tn(first, key_grad),
        matmul_tn(first, value_grad),
        o_grad,
        up_grad,
        down_grad,
    )
    vector_grads = (
        jnp.sum(first_grad * normed_one, axis=0),
        jnp.sum(first_grad, axis=0),
        jnp.sum(query_grad, axis=0, dtype=jnp.float32),
        jnp.sum(value_grad, axis=0, dtype=jnp.float32),
        jnp.sum(middle_bf, axis=0, dtype=jnp.float32),
        jnp.sum(second_grad * normed_two, axis=0),
        jnp.sum(second_grad, axis=0),
        jnp.sum(upper_grad, axis=0, dtype=jnp.float32),
        jnp.sum(out_grad, axis=0),
    )
    return (input_grad.astype(jnp.bfloat16), matrices, vector_grads)


def split_heads_body(
    images,
    live,
    cotangent,
    ln1_gain,
    ln1_bias,
    q_weight,
    q_bias,
    k_weight,
    v_weight,
    v_bias,
    o_weight,
    o_bias,
    ln2_gain,
    ln2_bias,
    fc1_weight,
    fc1_bias,
    fc2_weight,
    fc2_bias,
):
    tensor_count = lax.axis_size("tensor")
    tensor_rank = lax.axis_index("tensor")
    length = images.shape[1]
    full_width = images.shape[2]
    part_width = full_width // tensor_count
    feature_start = tensor_rank * part_width
    head_width = q_bias.shape[0] // tensor_count
    head_start = tensor_rank * head_width
    unit_width = fc1_bias.shape[0] // tensor_count
    unit_start = tensor_rank * unit_width
    row_count = SLOTS * length
    row_share = (row_count + tensor_count - 1) // tensor_count
    padded_rows = row_share * tensor_count
    sizes_info = (SLOTS, length, row_count, padded_rows)
    q_shift = lax.dynamic_slice_in_dim(q_bias, head_start, head_width, 0)
    v_shift = lax.dynamic_slice_in_dim(v_bias, head_start, head_width, 0)
    up_shift = lax.dynamic_slice_in_dim(fc1_bias, unit_start, unit_width, 0)
    gain_one, shift_one, o_shift, gain_two, shift_two, down_shift = tuple(
        (
            lax.dynamic_slice_in_dim(vector, feature_start, part_width, 0)
            for vector in (ln1_gain, ln1_bias, o_bias, ln2_gain, ln2_bias, fc2_bias)
        )
    )
    vectors = (
        gain_one,
        shift_one,
        q_shift,
        v_shift,
        o_shift,
        gain_two,
        shift_two,
        up_shift,
        down_shift,
    )
    q_low = q_weight.astype(jnp.bfloat16)
    k_low = k_weight.astype(jnp.bfloat16)
    v_low = v_weight.astype(jnp.bfloat16)
    o_low = o_weight.astype(jnp.bfloat16)
    up_low = fc1_weight.astype(jnp.bfloat16)
    down_low = fc2_weight.astype(jnp.bfloat16)
    slot_mask = live.astype(jnp.float32)
    outputs = []
    input_grads = []
    matrix_sums = None
    vector_sums = None
    for micro_batch in range(MB):
        slot_start = micro_batch * SLOTS
        batch_tokens = images[slot_start : slot_start + SLOTS].reshape(row_count, full_width)
        batch_cot = cotangent[slot_start : slot_start + SLOTS].reshape(row_count, full_width)
        mask_rows = jnp.broadcast_to(
            slot_mask[slot_start : slot_start + SLOTS, None], (SLOTS, length)
        ).reshape(-1, 1)
        stream = lax.dynamic_slice_in_dim(batch_tokens, feature_start, part_width, 1).astype(
            jnp.float32
        )
        cot_stream = lax.dynamic_slice_in_dim(batch_cot, feature_start, part_width, 1)
        forward_weights = (
            lax.all_gather(q_low, "fsdp", axis=0, tiled=True),
            lax.all_gather(k_low, "fsdp", axis=0, tiled=True),
            lax.all_gather(v_low, "fsdp", axis=0, tiled=True),
            lax.all_gather(o_low, "fsdp", axis=1, tiled=True),
            lax.all_gather(up_low, "fsdp", axis=0, tiled=True),
            lax.all_gather(down_low, "fsdp", axis=1, tiled=True),
        )
        output, kept_state = forward_pass(stream, mask_rows, forward_weights, vectors, sizes_info)
        backward_weights = (
            lax.all_gather(q_low, "fsdp", axis=0, tiled=True),
            lax.all_gather(k_low, "fsdp", axis=0, tiled=True),
            lax.all_gather(v_low, "fsdp", axis=0, tiled=True),
            lax.all_gather(o_low, "fsdp", axis=1, tiled=True),
            lax.all_gather(up_low, "fsdp", axis=0, tiled=True),
            lax.all_gather(down_low, "fsdp", axis=1, tiled=True),
        )
        grad_in, matrices, vector_grads = backward_pass(
            cot_stream, mask_rows, backward_weights, vectors, kept_state, sizes_info
        )
        whole_out, whole_grad = (
            lax.all_gather(output, "tensor", axis=1, tiled=True),
            lax.all_gather(grad_in, "tensor", axis=1, tiled=True),
        )
        outputs.append(whole_out.reshape(SLOTS, length, full_width))
        input_grads.append(whole_grad.reshape(SLOTS, length, full_width))
        vector_sums = (
            vector_grads
            if vector_sums is None
            else jax.tree.map(jnp.add, vector_sums, vector_grads)
        )
        matrix_sums = (
            matrices if matrix_sums is None else jax.tree.map(jnp.add, matrix_sums, matrices)
        )
    total_wq, total_wk, total_wv, total_wo, total_up, total_down = matrix_sums
    shard_wq, shard_wk, shard_wv, shard_wo, shard_up, shard_down = (
        lax.psum_scatter(
            total_wq.astype(jnp.bfloat16), "fsdp", scatter_dimension=0, tiled=True
        ).astype(jnp.float32),
        lax.psum_scatter(
            total_wk.astype(jnp.bfloat16), "fsdp", scatter_dimension=0, tiled=True
        ).astype(jnp.float32),
        lax.psum_scatter(
            total_wv.astype(jnp.bfloat16), "fsdp", scatter_dimension=0, tiled=True
        ).astype(jnp.float32),
        lax.psum_scatter(
            total_wo.astype(jnp.bfloat16), "fsdp", scatter_dimension=1, tiled=True
        ).astype(jnp.float32),
        lax.psum_scatter(
            total_up.astype(jnp.bfloat16), "fsdp", scatter_dimension=0, tiled=True
        ).astype(jnp.float32),
        lax.psum_scatter(
            total_down.astype(jnp.bfloat16), "fsdp", scatter_dimension=1, tiled=True
        ).astype(jnp.float32),
    )
    final_wq, final_wk, final_wv, final_wo, final_up, final_down = (
        lax.psum(shard_wq.astype(jnp.bfloat16), "replica").astype(jnp.float32),
        lax.psum(shard_wk.astype(jnp.bfloat16), "replica").astype(jnp.float32),
        lax.psum(shard_wv.astype(jnp.bfloat16), "replica").astype(jnp.float32),
        lax.psum(shard_wo.astype(jnp.bfloat16), "replica").astype(jnp.float32),
        lax.psum(shard_up.astype(jnp.bfloat16), "replica").astype(jnp.float32),
        lax.psum(shard_down.astype(jnp.bfloat16), "replica").astype(jnp.float32),
    )
    (
        sum_gain_one,
        sum_shift_one,
        sum_q_shift,
        sum_v_shift,
        sum_o_shift,
        sum_gain_two,
        sum_shift_two,
        sum_up_shift,
        sum_down_shift,
    ) = vector_sums
    summed = lax.psum(
        (
            sum_gain_one,
            sum_shift_one,
            sum_q_shift,
            sum_v_shift,
            sum_o_shift,
            sum_gain_two,
            sum_shift_two,
            sum_up_shift,
            sum_down_shift,
        ),
        ("replica", "fsdp"),
    )
    (
        grad_gain_one,
        grad_shift_one,
        grad_q_shift,
        grad_v_shift,
        grad_o_shift,
        grad_gain_two,
        grad_shift_two,
        grad_up_shift,
        grad_down_shift,
    ) = summed
    return (
        jnp.concatenate(outputs, axis=0),
        jnp.concatenate(input_grads, axis=0),
        grad_gain_one,
        grad_shift_one,
        final_wq,
        grad_q_shift,
        final_wk,
        final_wv,
        grad_v_shift,
        final_wo,
        grad_o_shift,
        grad_gain_two,
        grad_shift_two,
        final_up,
        grad_up_shift,
        final_down,
        grad_down_shift,
    )


WINDOW = 256
LANES = 128
SHIFT = 64
VMEM = 60 * 2**20
GELU = 0.7978845608
EVERY = ("tensor", "fsdp", "replica")


def ceil_to(value, step):
    return -(-value // step) * step


def call(kernel, name, grid, scalars, ins, outs, flops=0, scratch=(), aliases=None):
    total = sum(array.size * array.dtype.itemsize for array, _ in ins)
    return pl.pallas_call(
        kernel,
        grid_spec=pltpu.PrefetchScalarGridSpec(
            num_scalar_prefetch=1,
            grid=grid,
            in_specs=[spec for _, spec in ins],
            out_specs=[spec for _, _, spec in outs],
            scratch_shapes=list(scratch),
        ),
        out_shape=[jax.ShapeDtypeStruct(shape, dtype) for shape, dtype, _ in outs],
        input_output_aliases=aliases or {},
        compiler_params=pltpu.CompilerParams(vmem_limit_bytes=VMEM),
        cost_estimate=pl.CostEstimate(flops=flops, bytes_accessed=total, transcendentals=0),
        name=name,
    )(scalars, *(array for array, _ in ins))


def fixed(shape, index):
    return pl.BlockSpec(shape, index, pipeline_mode=pl.Buffered(1))


def head_window(offset, base, rows):
    start = (offset + base) // LANES * LANES
    lane = lax.broadcasted_iota(jnp.int32, (rows, WINDOW), 1) + start
    inside = (lane >= offset + base) & (lane < offset + base + HEAD)
    return pl.ds(pl.multiple_of(start, LANES), WINDOW), inside


def attention(qvk, length, rows, width, group):
    heads = width // HEAD
    count = qvk.shape[0] // rows
    steps = heads // group
    out_width = ceil_to(width + SHIFT, WINDOW)

    def kernel(none_ref, qvk_ref, mixed_ref, probs_ref):
        @pl.when(pl.program_id(1) == 0)
        def _():
            mixed_ref[...] = jnp.zeros_like(mixed_ref)

        real = lax.broadcasted_iota(jnp.int32, (rows, rows), 1) < length
        for item in range(group):
            offset = (pl.program_id(1) * group + item) * HEAD
            at_q, _ = head_window(offset, 0, rows)
            at_v, in_v = head_window(offset, width, rows)
            at_k, in_k = head_window(offset, 2 * width, rows)
            at_o, in_o = head_window(offset, SHIFT, rows)
            key_rows = jnp.where(in_k, qvk_ref[:, at_k], 0)
            value_rows = jnp.where(in_v, qvk_ref[:, at_v], 0)
            scores = jnp.where(real, matmul_nt(qvk_ref[:, at_q], key_rows), -1e30)
            powers = jnp.exp(scores - jnp.max(scores, axis=1, keepdims=True))
            total = jnp.sum(powers, axis=1, keepdims=True)
            probs = (powers * (1.0 / total)).astype(jnp.bfloat16)
            probs_ref[item] = probs
            mixed = matmul(probs, value_rows).astype(jnp.bfloat16)
            mixed_ref[:, at_o] = jnp.where(in_o, mixed, mixed_ref[:, at_o])

    return call(
        kernel,
        "attention",
        (count, steps),
        jnp.zeros((1,), jnp.int32),
        [(qvk, pl.BlockSpec((rows, qvk.shape[1]), lambda i, g, s: (i, 0)))],
        [
            ((count * rows, out_width), jnp.bfloat16, pl.BlockSpec((rows, out_width), lambda i, g, s: (i, 0))),
            (
                (count * heads, rows, rows),
                jnp.bfloat16,
                pl.BlockSpec((group, rows, rows), lambda i, g, s: (i * steps + g, 0, 0)),
            ),
        ],
        flops=4 * count * heads * rows * rows * WINDOW,
    )


def attention_back(qvk, mixed, grad, probs, images, kept, rows, width, group):
    heads = width // HEAD
    steps = heads // group
    at = images.start
    count = len(images)

    def kernel(none_ref, qvk_ref, mixed_ref, grad_ref, probs_ref, *refs):
        out_ref, sums_ref = refs[-2:]

        @pl.when(pl.program_id(1) == 0)
        def _():
            out_ref[...] = jnp.zeros_like(out_ref)

        for item in range(group):
            offset = (pl.program_id(1) * group + item) * HEAD
            at_q, in_q = head_window(offset, 0, rows)
            at_v, in_v = head_window(offset, width, rows)
            at_k, in_k = head_window(offset, 2 * width, rows)
            at_o, in_o = head_window(offset, SHIFT, rows)
            grad = jnp.where(in_o, grad_ref[:, at_o], 0)
            query_rows = jnp.where(in_q, qvk_ref[:, at_q], 0)
            key_rows = jnp.where(in_k, qvk_ref[:, at_k], 0)
            probs = probs_ref[item]
            row_dot = jnp.sum(
                grad.astype(jnp.float32) * mixed_ref[:, at_o].astype(jnp.float32), axis=1, keepdims=True
            )
            prob_grad = matmul_nt(grad, qvk_ref[:, at_v])
            score_grad = (probs.astype(jnp.float32) * (prob_grad - row_dot)).astype(jnp.bfloat16)
            value_grad = matmul_tn(probs, grad).astype(jnp.bfloat16)
            query_grad = (matmul(score_grad, key_rows) * HEAD ** (-0.5)).astype(jnp.bfloat16)
            key_grad = matmul_tn(score_grad, query_rows).astype(jnp.bfloat16)
            out_ref[:, at_q] = jnp.where(in_q, query_grad, out_ref[:, at_q])
            out_ref[:, at_v] = jnp.where(in_v, value_grad, out_ref[:, at_v])
            out_ref[:, at_k] = jnp.where(in_k, key_grad, out_ref[:, at_k])

        @pl.when(pl.program_id(1) == steps - 1)
        def _():
            total = jnp.sum(out_ref[...].astype(jnp.float32), axis=0, keepdims=True)
            sums_ref[0] = jnp.broadcast_to(total, sums_ref.shape[1:])

    ins = [
        (qvk, pl.BlockSpec((rows, qvk.shape[1]), lambda i, g, s: (at + i, 0))),
        (mixed, pl.BlockSpec((rows, mixed.shape[1]), lambda i, g, s: (at + i, 0))),
        (grad, pl.BlockSpec((rows, mixed.shape[1]), lambda i, g, s: (at + i, 0))),
        (probs, pl.BlockSpec((group, rows, rows), lambda i, g, s: ((at + i) * steps + g, 0, 0))),
    ]
    if kept is not None:
        ins.append((kept, pl.BlockSpec(memory_space=pl.ANY)))
    grads, sums = call(
        kernel,
        "attention_back",
        (count, steps),
        jnp.zeros((1,), jnp.int32),
        ins,
        [
            (qvk.shape, jnp.bfloat16, pl.BlockSpec((rows, qvk.shape[1]), lambda i, g, s: (at + i, 0))),
            ((count, 8, qvk.shape[1]), jnp.float32, pl.BlockSpec((1, 8, qvk.shape[1]), lambda i, g, s: (i, 0, 0))),
        ],
        flops=8 * count * heads * rows * rows * WINDOW,
        aliases=None if kept is None else {5: 0},
    )
    return grads, jnp.sum(sums[:, 0], axis=0)


def place(pieces, slots, total):
    def kernel(slots_ref, *refs):
        for at, ref in enumerate(refs[:-1]):
            refs[-1][pl.ds(slots_ref[at], ref.shape[0])] = ref[...]

    def whole(shape):
        return fixed(shape, lambda i, s: (0, 0, 0))

    shape = (total, *pieces[0].shape[1:])
    return call(
        kernel,
        "place",
        (1,),
        jnp.stack(slots).astype(jnp.int32),
        [(piece, whole(piece.shape)) for piece in pieces],
        [(shape, pieces[0].dtype, whole(shape))],
    )[0]


def outer_sum(left, right, ranks, step):
    rows, lines = left.shape
    columns = right.shape[1] // ranks
    steps = columns // step

    def kernel(none_ref, left_ref, right_ref, out_ref):
        out_ref[...] = matmul_tn(left_ref[...], right_ref[...]).astype(out_ref.dtype)

    return call(
        kernel,
        "outer_sum",
        (ranks, steps),
        jnp.zeros((1,), jnp.int32),
        [
            (left, fixed((rows, lines), lambda t, j, s: (0, 0))),
            (right, pl.BlockSpec((rows, step), lambda t, j, s: (0, t * steps + j))),
        ],
        [((ranks * lines, columns), jnp.bfloat16, pl.BlockSpec((lines, step), lambda t, j, s: (t, j)))],
        flops=2 * rows * lines * columns * ranks,
    )[0]


def tie(*values):
    return lax.optimization_barrier(values)


def swap(array, axis, bits):
    size = lax.axis_size(axis)
    return lax.ppermute(array, axis, [(rank, rank ^ bits) for rank in range(size)])


def turn(array, axis, steps):
    size = lax.axis_size(axis)
    return lax.ppermute(array, axis, [(rank, (rank + steps) % size) for rank in range(size)])


def replica_bits():
    bit = lax.axis_size("replica") // 2
    bits = []
    while bit:
        bits.append(bit)
        bit //= 2
    return bits


def among_replicas(piece):
    found = {0: piece}
    for bit in replica_bits():
        found.update({bits ^ bit: swap(held, "replica", bit) for bits, held in list(found.items())})
    return found


def from_lines(shard):
    copies = lax.axis_size("replica")
    blocks = shard.reshape(copies, -1, shard.shape[1])
    mine = lax.dynamic_slice_in_dim(blocks, lax.axis_index("replica"), 1, 0)
    return [mine] + [turn(mine, "fsdp", step) for step in range(1, lax.axis_size("fsdp"))]


def gather_parts(shard, parts):
    copies, lines, ranks = (lax.axis_size(axis) for axis in ("replica", "fsdp", "tensor"))
    copy, line = lax.axis_index("replica"), lax.axis_index("fsdp")
    blocks = shard.reshape(copies, -1, shard.shape[1])
    wholes = []
    for rank in range(ranks):
        pieces, slots = [], []
        for step in range(lines):
            start = (line - step) % lines * copies
            if rank == 0 and step == 0:
                pieces.append(blocks)
                slots.append(start)
                continue
            piece = parts[step] if rank == 0 else swap(parts[step], "tensor", rank)
            for bits, held in among_replicas(piece).items():
                pieces.append(held)
                slots.append(start + (copy ^ bits))
        wholes.append(place(pieces, slots, lines * copies).reshape(-1, shard.shape[1]))
    return wholes


def gather_whole(shard):
    share = shard.shape[0] // lax.axis_size("replica")
    part = lax.dynamic_slice_in_dim(shard, lax.axis_index("replica") * share, share, 0)
    return lax.all_gather(part, EVERY, axis=0, tiled=True)


def add_low(first_term, *terms):
    total = first_term.astype(jnp.float32)
    for term in terms:
        total = total + term.astype(jnp.float32)
    return total.astype(jnp.bfloat16)


def by_lines(term):
    bits = len(replica_bits())
    return term.reshape(lax.axis_size("fsdp"), *(2 for _ in range(bits)), -1, term.shape[1])


def halve(held, bit):
    side = lax.axis_index("replica") // bit % 2
    axis = held.ndim - 3
    keep = lax.dynamic_index_in_dim(held, side, axis, keepdims=False)
    send = lax.dynamic_index_in_dim(held, 1 - side, axis, keepdims=False)
    return add_low(keep, swap(send, "replica", bit))


def sum_lines(held):
    lines, line = lax.axis_size("fsdp"), lax.axis_index("fsdp")
    terms = [lax.dynamic_index_in_dim(held, line, 0, keepdims=True)]
    for step in range(1, lines):
        send = lax.dynamic_index_in_dim(held, (line + step) % lines, 0, keepdims=True)
        terms.append(turn(send, "fsdp", step))
    return add_low(*terms)


def join_replicas(piece):
    copy = lax.axis_index("replica")
    found = among_replicas(piece)
    whole = place(list(found.values()), [copy ^ bits for bits in found], len(found))
    return whole.reshape(-1, piece.shape[2])


def sum_over(vector, axis):
    bit = 1
    while bit < lax.axis_size(axis):
        vector = vector + swap(vector, axis, bit)
        bit *= 2
    return vector


def norm_parts(values):
    center = jnp.mean(values, axis=1, keepdims=True)
    spread = jnp.mean(values * values, axis=1, keepdims=True) - center * center
    scale_inv = lax.rsqrt(spread + EPSILON)
    return (values - center) * scale_inv, scale_inv


def norm_backward(grad, normed, scale_inv, gain_vec):
    scaled = grad * gain_vec
    mean_one = jnp.mean(scaled, axis=1, keepdims=True)
    mean_two = jnp.mean(scaled * normed, axis=1, keepdims=True)
    return scale_inv * (scaled - mean_one - normed * mean_two)


def image_body(
    images,
    live,
    cotangent,
    ln1_gain,
    ln1_bias,
    q_weight,
    q_bias,
    k_weight,
    v_weight,
    v_bias,
    o_weight,
    o_bias,
    ln2_gain,
    ln2_bias,
    fc1_weight,
    fc1_bias,
    fc2_weight,
    fc2_bias,
):
    low, full = jnp.bfloat16, jnp.float32
    tensor_count = lax.axis_size("tensor")
    tensor_rank = lax.axis_index("tensor")
    slots, length, wide = images.shape
    count = slots // tensor_count
    rows = ceil_to(length, 32)
    half = rows // 2
    width = q_weight.shape[1]
    units = fc1_weight.shape[1]
    qvk_width = ceil_to(3 * width, WINDOW)
    o_width = ceil_to(width + SHIFT, WINDOW)
    unit_width = ceil_to(units, WINDOW)
    if unit_width % o_width:
        unit_width = ceil_to(unit_width, o_width)
    ranks = range(tensor_count)
    all_rows = count * rows
    blocks = all_rows // half
    scalars = jnp.concatenate(
        [
            jnp.stack([tensor_rank * count] + [tensor_rank ^ rank for rank in ranks]).astype(jnp.int32),
            lax.dynamic_slice_in_dim(live, tensor_rank * count, count, 0),
        ]
    )
    live_at = 1 + tensor_count

    def columns(parts, ahead, total):
        body_part = jnp.concatenate(parts, axis=1)
        return jnp.pad(body_part, ((0, 0), (ahead, total - ahead - body_part.shape[1])))

    def row(vector):
        return vector.reshape(1, -1)

    def slots_spec(first=0):
        return pl.BlockSpec((1, half, wide), lambda i, s: (s[0] + first + i // 2, i % 2, 0))

    def rows_spec(size, first=0):
        return pl.BlockSpec((half, size), lambda i, s: (2 * first + i, 0))

    def vector_spec():
        return pl.BlockSpec((1, wide), lambda i, s: (0, 0))

    def sums_spec():
        return pl.BlockSpec((8, wide), lambda i, s: (0, 0))

    def real_rows(values):
        at = lax.broadcasted_iota(jnp.int32, (half, 1), 0) + pl.program_id(0) % 2 * half
        return jnp.where(at < length, values.astype(full), 0.0)

    def live_slot(scalars_ref, first=0):
        return scalars_ref[live_at + first + pl.program_id(0) // 2].astype(full)

    def add_sums(sums_ref, *terms):
        @pl.when(pl.program_id(0) == 0)
        def _():
            sums_ref[...] = jnp.zeros_like(sums_ref)

        for at, term in enumerate(terms):
            sums_ref[at : at + 1] += jnp.sum(term, axis=0, keepdims=True)

    def product(part_refs, weight_refs):
        total = matmul_nt(part_refs[0][...], weight_refs[0][...])
        for part_ref, weight_ref in zip(part_refs[1:], weight_refs[1:]):
            total = total + matmul_nt(part_ref[...], weight_ref[...])
        return total

    qvk_shard = columns([w.astype(low) for w in (q_weight, v_weight, k_weight)], 0, qvk_width)
    parts = from_lines(qvk_shard)

    def first_kernel(scalars_ref, images_ref, cot_ref, gain_ref, shift_ref, first_ref, grad_ref, sums_ref):
        normed, _ = norm_parts(real_rows(images_ref[0]))
        first_ref[...] = (normed * gain_ref[...] + shift_ref[...]).astype(low)
        grad = real_rows(cot_ref[0]) * live_slot(scalars_ref)
        grad_ref[...] = grad.astype(low)
        add_sums(sums_ref, grad)

    first, out_grad, first_sums = call(
        first_kernel,
        "first_norm",
        (blocks,),
        scalars,
        [(images, slots_spec()), (cotangent, slots_spec()), (row(ln1_gain), vector_spec()), (row(ln1_bias), vector_spec())],
        [
            ((all_rows, wide), low, rows_spec(wide)),
            ((all_rows, wide), low, rows_spec(wide)),
            ((8, wide), full, sums_spec()),
        ],
    )

    parts, first, out_grad = tie(parts, first, out_grad)
    up_o_shard = jnp.concatenate(
        [
            columns([fc1_weight.astype(low)], 0, unit_width),
            columns([o_weight.astype(low).T], SHIFT, o_width),
        ],
        axis=1,
    )
    down_shard = columns([fc2_weight.astype(low).T], 0, unit_width)
    up_o_shard, down_shard, parts = tie(up_o_shard, down_shard, parts)
    up_o_whole = gather_whole(up_o_shard)
    down_whole = gather_whole(down_shard)
    qvk_weights = gather_parts(qvk_shard, parts)

    def of_rank(vector, rank, size):
        return lax.dynamic_slice_in_dim(vector, (tensor_rank ^ rank) * size, size, 0)

    scale_row = jnp.where(jnp.arange(qvk_width) < width, HEAD ** (-0.5), 1.0)
    qvk, mixed, probs = [], [], []
    for rank in ranks:
        shift_row = jnp.pad(
            jnp.concatenate([of_rank(q_bias, rank, width), of_rank(v_bias, rank, width)]),
            (0, qvk_width - 2 * width),
        )
        qvk.append(((matmul(first, qvk_weights[rank]) + shift_row) * scale_row).astype(low))
        mixed_part, probs_part = attention(qvk[rank], length, rows, width, 4)
        mixed.append(mixed_part)
        probs.append(probs_part)

    def o_spec(rank):
        return fixed((wide, o_width), lambda i, s: (s[1 + rank], unit_width // o_width))

    def middle_kernel(scalars_ref, *refs):
        images_ref, bias_ref, gain_ref, shift_ref, middle_ref, second_ref = refs[2 * tensor_count :]
        total = product(refs[:tensor_count], refs[tensor_count : 2 * tensor_count])
        middle = real_rows(images_ref[0]) + (total + bias_ref[...])
        middle_ref[...] = middle
        normed, _ = norm_parts(middle)
        second_ref[...] = (normed * gain_ref[...] + shift_ref[...]).astype(low)

    middle, second = call(
        middle_kernel,
        "middle_norm",
        (blocks,),
        scalars,
        [(part, rows_spec(o_width)) for part in mixed]
        + [(up_o_whole, o_spec(rank)) for rank in ranks]
        + [
            (images, slots_spec()),
            (row(o_bias), vector_spec()),
            (row(ln2_gain), vector_spec()),
            (row(ln2_bias), vector_spec()),
        ],
        [((all_rows, wide), full, rows_spec(wide)), ((all_rows, wide), low, rows_spec(wide))],
        flops=2 * all_rows * wide * o_width * tensor_count,
    )

    chunk = o_width if unit_width % o_width == 0 else unit_width

    def unit_rows():
        return pl.BlockSpec((half, unit_width), lambda t, i, s: (i, t))

    def unit_weights():
        return pl.BlockSpec((wide, unit_width), lambda t, i, s: (t, 0))

    def hidden_kernel(scalars_ref, second_ref, weight_ref, shift_ref, hidden_ref, slope_ref):
        for start in range(0, unit_width, chunk):
            at = slice(start, start + chunk)
            upper = matmul(second_ref[...], weight_ref[:, at]) + shift_ref[:, at]
            square = upper * upper
            share = 0.5 + 0.5 * jnp.tanh(upper * (GELU + GELU * 0.044715 * square))
            hidden = upper * share
            slope = share + (hidden - hidden * share) * (2 * GELU + 6 * GELU * 0.044715 * square)
            hidden_ref[:, at] = hidden.astype(low)
            slope_ref[:, at] = slope.astype(low)

    unit_shift = jnp.pad(
        fc1_bias.reshape(tensor_count, units), ((0, 0), (0, unit_width - units))
    ).reshape(1, -1)
    hidden, slopes = call(
        hidden_kernel,
        "hidden",
        (tensor_count, blocks),
        scalars,
        [
            (second, pl.BlockSpec((half, wide), lambda t, i, s: (i, 0))),
            (up_o_whole, unit_weights()),
            (unit_shift, pl.BlockSpec((1, unit_width), lambda t, i, s: (0, t))),
        ],
        [((all_rows, tensor_count * unit_width), low, unit_rows())] * 2,
        flops=2 * all_rows * wide * unit_width * tensor_count,
    )
    down_terms = outer_sum(out_grad, hidden, tensor_count, chunk)
    down_terms, hidden = tie(down_terms, hidden)
    down_share = lax.psum_scatter(down_terms, EVERY, scatter_dimension=0, tiled=True)

    def weight_spec(rank):
        return fixed((wide, unit_width), lambda i, s: (rank, 0))

    def unit_spec(rank):
        return pl.BlockSpec((half, unit_width), lambda i, s: (i, rank))

    def output_kernel(scalars_ref, *refs):
        middle_ref, bias_ref, output_ref, whole_ref = refs[2 * tensor_count :]
        total = product(refs[:tensor_count], refs[tensor_count : 2 * tensor_count])
        result = middle_ref[...] + (total + bias_ref[...])
        output_ref[0] = (result * live_slot(scalars_ref)).astype(low)
        whole_ref[0] = output_ref[0]

    output, out_whole = call(
        output_kernel,
        "output",
        (blocks,),
        scalars,
        [(hidden, unit_spec(rank)) for rank in ranks]
        + [(down_whole, weight_spec(rank)) for rank in ranks]
        + [(middle, rows_spec(wide)), (row(fc2_bias), vector_spec())],
        [
            ((count, length, wide), low, pl.BlockSpec((1, half, wide), lambda i, s: (i // 2, i % 2, 0))),
            ((slots, length, wide), low, slots_spec()),
        ],
        flops=2 * all_rows * wide * unit_width * tensor_count,
    )

    def trade(part):
        return [swap(part, "tensor", rank) for rank in ranks[1:]]

    def lay(whole, parts, first):
        for rank, part in zip(ranks[1:], parts):
            whole = lax.dynamic_update_slice_in_dim(whole, part, (tensor_rank ^ rank) * count + first, 0)
        return whole

    output, out_grad = tie(output, out_grad)
    out_parts = [trade(output[slot : slot + 1]) for slot in range(count)]

    def hidden_back_kernel(scalars_ref, grad_ref, weight_ref, slope_ref, upper_ref, sums_ref):
        @pl.when(pl.program_id(1) == 0)
        def _():
            sums_ref[...] = jnp.zeros_like(sums_ref)

        for start in range(0, unit_width, chunk):
            at = slice(start, start + chunk)
            upper = matmul(grad_ref[...], weight_ref[:, at]) * slope_ref[:, at].astype(full)
            rounded = upper.astype(low)
            upper_ref[:, at] = rounded
            sums_ref[0:1, at] += jnp.sum(rounded.astype(full), axis=0, keepdims=True)

    upper_grads, upper_sums = call(
        hidden_back_kernel,
        "hidden_back",
        (tensor_count, blocks),
        scalars,
        [
            (out_grad, pl.BlockSpec((half, wide), lambda t, i, s: (i, 0))),
            (down_whole, unit_weights()),
            (slopes, unit_rows()),
        ],
        [
            ((all_rows, tensor_count * unit_width), low, unit_rows()),
            ((8, tensor_count * unit_width), full, pl.BlockSpec((8, unit_width), lambda t, i, s: (0, t))),
        ],
        flops=2 * all_rows * wide * unit_width * tensor_count,
    )
    up_terms = outer_sum(second, upper_grads, tensor_count, chunk)
    up_terms, upper_grads = tie(up_terms, upper_grads)
    up_share = lax.psum_scatter(up_terms, EVERY, scatter_dimension=0, tiled=True)

    def middle_back_kernel(scalars_ref, *refs):
        middle_ref, grad_ref, gain_ref, middle_grad_ref, low_ref, sums_ref = refs[2 * tensor_count :]
        total = product(refs[:tensor_count], refs[tensor_count : 2 * tensor_count])
        normed, scale_inv = norm_parts(middle_ref[...])
        middle_grad = grad_ref[...].astype(full) + norm_backward(total, normed, scale_inv, gain_ref[...])
        middle_grad_ref[...] = middle_grad
        rounded = middle_grad.astype(low)
        low_ref[...] = rounded
        add_sums(sums_ref, total * normed, total, rounded.astype(full))

    middle_grad, middle_low, second_sums = call(
        middle_back_kernel,
        "middle_back",
        (blocks,),
        scalars,
        [(upper_grads, unit_spec(rank)) for rank in ranks]
        + [(up_o_whole, weight_spec(rank)) for rank in ranks]
        + [(middle, rows_spec(wide)), (out_grad, rows_spec(wide)), (row(ln2_gain), vector_spec())],
        [
            ((all_rows, wide), full, rows_spec(wide)),
            ((all_rows, wide), low, rows_spec(wide)),
            ((8, wide), full, sums_spec()),
        ],
        flops=2 * all_rows * wide * unit_width * tensor_count,
    )

    def o_block(rank):
        block = lax.dynamic_slice_in_dim(up_o_whole, (tensor_rank ^ rank) * wide, wide, 0)
        return block[:, unit_width:]

    o_held = [by_lines(outer_sum(middle_low, mixed[rank], 1, o_width)) for rank in ranks]
    o_held, middle_low = tie(o_held, middle_low)
    mixed_grads = [matmul(middle_low, o_block(rank)).astype(low) for rank in ranks]
    bits = replica_bits()[::-1]
    halved = [halve(held, bits[0]) for held in o_held] if bits else o_held
    halved, mixed_grads, out_parts = tie(halved, mixed_grads, out_parts)
    for slot in range(count):
        out_whole = lay(out_whole, out_parts[slot], slot)

    def back(rank, which, kept):
        return attention_back(
            qvk[rank], mixed[rank], mixed_grads[rank], probs[rank], which, kept, rows, width, 2
        )

    def first_back_kernel(first_slot, scalars_ref, *refs):
        images_ref, grad_ref, gain_ref = refs[2 * tensor_count : 2 * tensor_count + 3]
        out_ref, whole_ref, sums_ref = refs[-3:]
        total = product(refs[:tensor_count], refs[tensor_count : 2 * tensor_count])
        normed, scale_inv = norm_parts(real_rows(images_ref[0]))
        grad = grad_ref[...] + norm_backward(total, normed, scale_inv, gain_ref[...])
        out_ref[0] = grad.astype(low)
        whole_ref[0] = out_ref[0]
        add_sums(sums_ref, total * normed, total)

    qvk_grads, qvk_sums = [None] * tensor_count, [0.0] * tensor_count
    for rank in ranks[1:]:
        qvk_grads[rank], qvk_sums[rank] = back(rank, range(count), None)
    for bit in bits[1:]:
        halved = [halve(held, bit) for held in halved]
    halved, qvk_grads[1:] = tie(halved, qvk_grads[1:])
    far = [by_lines(outer_sum(first, grads, 1, qvk_width // 2)) for grads in qvk_grads[1:]]
    o_held = halved[0]
    for rank in ranks[1:]:
        o_held = add_low(o_held, swap(halved[rank], "tensor", rank))
    o_held, far, mixed_grads[0], out_whole = tie(o_held, far, mixed_grads[0], out_whole)
    input_whole = None
    third_sums = 0.0
    in_parts = []
    for slot in range(count):
        qvk_grads[0], sums = back(0, range(slot, slot + 1), qvk_grads[0])
        qvk_sums[0] = qvk_sums[0] + sums
        if slot == 0:
            far = [halve(held, bits[0]) for held in far] if bits else far
            o_held = sum_lines(o_held)
            far, o_held, qvk_grads[0], down_share = tie(far, o_held, qvk_grads[0], down_share)
            down_grads = lax.all_gather(down_share, "replica", axis=0, tiled=True)
        if slot == count - 1:
            near = by_lines(outer_sum(first, qvk_grads[0], 1, qvk_width // 2))
            near, in_parts, qvk_grads[0], far, o_grads, down_grads, up_grads = tie(
                near, in_parts, qvk_grads[0], far, o_grads, down_grads, up_grads
            )
        ahead = [] if input_whole is None else [(input_whole, pl.BlockSpec(memory_space=pl.ANY))]
        input_grad, input_whole, sums = call(
            functools.partial(first_back_kernel, slot),
            "first_back",
            (2,),
            scalars,
            [(grads, rows_spec(qvk_width, slot)) for grads in qvk_grads]
            + [(weight, fixed((wide, qvk_width), lambda i, s: (0, 0))) for weight in qvk_weights]
            + [(images, slots_spec(slot)), (middle_grad, rows_spec(wide, slot)), (row(ln1_gain), vector_spec())]
            + ahead,
            [
                ((1, length, wide), low, pl.BlockSpec((1, half, wide), lambda i, s: (0, i, 0))),
                ((slots, length, wide), low, slots_spec(slot)),
                ((8, wide), full, sums_spec()),
            ],
            flops=2 * rows * wide * qvk_width * tensor_count,
            aliases={2 * tensor_count + 4: 1} if ahead else None,
        )
        third_sums = third_sums + sums
        input_grad, mixed_grads[0] = tie(input_grad, mixed_grads[0])
        in_parts.append(trade(input_grad))
        if slot == 0:
            for bit in bits[1:]:
                far = [halve(held, bit) for held in far]
            far, mixed_grads[0], up_share = tie(far, mixed_grads[0], up_share)
            up_grads = lax.all_gather(up_share, "replica", axis=0, tiled=True)
            o_grads = join_replicas(o_held)
            far = [swap(held, "tensor", rank) for rank, held in zip(ranks[1:], far)]
    for bit in bits:
        near = halve(near, bit)
    in_grads = join_replicas(sum_lines(add_low(near, *far)))

    def all_ranks(parts, size):
        whole = jnp.zeros((tensor_count * size,), full)
        for rank in ranks:
            whole = lax.dynamic_update_slice_in_dim(whole, parts[rank], (tensor_rank ^ rank) * size, 0)
        return whole

    vectors = [
        third_sums[0],
        third_sums[1],
        all_ranks([sums[:width] for sums in qvk_sums], width),
        all_ranks([sums[width : 2 * width] for sums in qvk_sums], width),
        second_sums[2],
        second_sums[0],
        second_sums[1],
        upper_sums[0].reshape(tensor_count, unit_width)[:, :units].reshape(-1),
        first_sums[0],
    ]
    sizes = [vector.shape[0] for vector in vectors]
    joined = jnp.concatenate(vectors)
    padded = ceil_to(joined.shape[0], 8 * LANES)
    summed = jnp.pad(joined, (0, padded - joined.shape[0])).reshape(-1, LANES)
    summed = sum_over(sum_over(summed, "replica"), "fsdp")
    summed, in_parts = tie(summed, in_parts)
    summed = sum_over(summed, "tensor").reshape(-1)
    for slot in range(count):
        input_whole = lay(input_whole, in_parts[slot], slot)
    ends, start = [], 0
    for size in sizes:
        share = size // tensor_count
        ends.append(lax.dynamic_slice_in_dim(summed, start + tensor_rank * share, share, 0))
        start += size
    gain_one, shift_one, q_sum, v_sum, o_sum, gain_two, shift_two, up_sum, down_sum = ends
    return (
        out_whole,
        input_whole,
        gain_one,
        shift_one,
        in_grads[:, :width].astype(full),
        q_sum,
        in_grads[:, 2 * width : 3 * width].astype(full),
        in_grads[:, width : 2 * width].astype(full),
        v_sum,
        o_grads[:, SHIFT : SHIFT + width].astype(full).T,
        o_sum,
        gain_two,
        shift_two,
        up_grads[:, :units].astype(full),
        up_sum,
        down_grads[:, :units].astype(full).T,
        down_sum,
    )


def halves(size):
    return size & (size - 1) == 0


def by_images(mesh):
    return SLOTS * MB % mesh.shape["tensor"] == 0 and all(halves(size) for size in mesh.shape.values())


def solution(mesh):
    in_specs = (
        P(("replica", "fsdp"), None, None),
        P(("replica", "fsdp")),
        P(("replica", "fsdp"), None, None),
        P(),
        P(),
        P("fsdp", "tensor"),
        P(),
        P("fsdp", "tensor"),
        P("fsdp", "tensor"),
        P(),
        P("tensor", "fsdp"),
        P(),
        P(),
        P(),
        P("fsdp", "tensor"),
        P(),
        P("tensor", "fsdp"),
        P(),
    )
    out_specs = (
        P(("replica", "fsdp"), None, None),
        P(("replica", "fsdp"), None, None),
        P("tensor"),
        P("tensor"),
        P("fsdp", "tensor"),
        P("tensor"),
        P("fsdp", "tensor"),
        P("fsdp", "tensor"),
        P("tensor"),
        P("tensor", "fsdp"),
        P("tensor"),
        P("tensor"),
        P("tensor"),
        P("fsdp", "tensor"),
        P("tensor"),
        P("tensor", "fsdp"),
        P("tensor"),
    )
    body = image_body if by_images(mesh) else split_heads_body
    return jax.shard_map(body, mesh=mesh, in_specs=in_specs, out_specs=out_specs, check_vma=False)
```

```python
import functools

import jax
import jax.numpy as jnp
from jax import lax
from jax.experimental import pallas as pl
from jax.experimental.pallas import tpu as pltpu
from jax.sharding import PartitionSpec as P

HEAD = 72
MB = 2
SLOTS = 3


EPSILON = 1e-06


def matmul(first_op, second_op):
    return jnp.dot(first_op, second_op, preferred_element_type=jnp.float32)


def matmul_tn(first_op, second_op):
    return lax.dot_general(
        first_op, second_op, (((0,), (0,)), ((), ())), preferred_element_type=jnp.float32
    )


def matmul_nt(first_op, second_op):
    return lax.dot_general(
        first_op, second_op, (((1,), (1,)), ((), ())), preferred_element_type=jnp.float32
    )


def gelu_tanh(values):
    return jax.nn.gelu(values, approximate=True)


def row_totals(first_sum, second_sum):
    return lax.psum((first_sum, second_sum), "tensor")


def spread_whole(rounded):
    return lax.all_gather(rounded, "tensor", axis=1, tiled=True)


def combine_parts(partial_value):
    return lax.psum_scatter(partial_value, "tensor", scatter_dimension=1, tiled=True)


def normalize(stream, gain_vec, shift_vec):
    full_width = stream.shape[1] * lax.axis_size("tensor")
    totals = row_totals(
        jnp.sum(stream, axis=1, keepdims=True), jnp.sum(stream * stream, axis=1, keepdims=True)
    )
    center = totals[0] / full_width
    spread = totals[1] / full_width - center * center
    scale_inv = lax.rsqrt(spread + EPSILON)
    normed = (stream - center) * scale_inv
    rounded = (normed * gain_vec + shift_vec).astype(jnp.bfloat16)
    return (spread_whole(rounded), normed, scale_inv)


def norm_back(grad_part, normed, scale_inv, gain_vec):
    scaled = grad_part * gain_vec
    full_width = grad_part.shape[1] * lax.axis_size("tensor")
    totals = row_totals(
        jnp.sum(scaled, axis=1, keepdims=True), jnp.sum(scaled * normed, axis=1, keepdims=True)
    )
    mean_one = totals[0] / full_width
    mean_two = totals[1] / full_width
    return scale_inv * (scaled - mean_one - normed * mean_two)


def score_block(queries, key_rows):
    return jnp.einsum("bqhd,bkhd->bhqk", queries, key_rows, preferred_element_type=jnp.float32)


def forward_pass(stream, row_mask, weights, vectors, sizes_info):
    q_full, k_full, v_full, o_full, up_full, down_full = weights
    gain_one, shift_one, q_shift, v_shift, o_shift, gain_two, shift_two, up_shift, down_shift = (
        vectors
    )
    blocks, length, row_count, padded_rows = sizes_info
    head_count = q_shift.shape[0] // HEAD
    shape_four = (blocks, length, head_count, HEAD)
    first, normed_one, inv_one = normalize(stream, gain_one, shift_one)
    queries = (
        ((matmul(first, q_full) + q_shift) * HEAD ** (-0.5))
        .astype(jnp.bfloat16)
        .reshape(shape_four)
    )
    key_rows = matmul(first, k_full).astype(jnp.bfloat16).reshape(shape_four)
    value_rows = (matmul(first, v_full) + v_shift).astype(jnp.bfloat16).reshape(shape_four)
    scores = score_block(queries, key_rows)
    top_score = jnp.max(scores, axis=-1, keepdims=True)
    log_total = top_score + jnp.log(jnp.sum(jnp.exp(scores - top_score), axis=-1, keepdims=True))
    probs_bf = jnp.exp(scores - log_total).astype(jnp.bfloat16)
    attended = jnp.einsum(
        "bhqk,bkhd->bqhd", probs_bf, value_rows, preferred_element_type=jnp.float32
    )
    attended_bf = attended.reshape(row_count, head_count * HEAD).astype(jnp.bfloat16)
    middle = stream + combine_parts(matmul(attended_bf, o_full)) + o_shift
    second, normed_two, inv_two = normalize(middle, gain_two, shift_two)
    upper_pre = matmul(second, up_full) + up_shift
    hidden = gelu_tanh(upper_pre).astype(jnp.bfloat16)
    result = middle + combine_parts(matmul(hidden, down_full)) + down_shift
    output = (result * row_mask).astype(jnp.bfloat16)
    kept_state = (
        first,
        normed_one,
        inv_one,
        queries,
        key_rows,
        value_rows,
        log_total,
        attended_bf,
        normed_two,
        inv_two,
        second,
        upper_pre,
        hidden,
    )
    return (output, kept_state)


def backward_pass(cot_stream, row_mask, weights, vectors, kept_state, sizes_info):
    q_full, k_full, v_full, o_full, up_full, down_full = weights
    gain_one, shift_one, q_shift, v_shift, o_shift, gain_two, shift_two, up_shift, down_shift = (
        vectors
    )
    (
        first,
        normed_one,
        inv_one,
        queries,
        key_rows,
        value_rows,
        log_total,
        attended_bf,
        normed_two,
        inv_two,
        second,
        upper_pre,
        hidden,
    ) = kept_state
    blocks, length, row_count, padded_rows = sizes_info
    shape_four = queries.shape
    out_grad = cot_stream.astype(jnp.float32) * row_mask
    out_whole = spread_whole(out_grad.astype(jnp.bfloat16))
    down_grad = matmul_tn(hidden, out_whole)
    hidden_grad = matmul_nt(out_whole, down_full)
    upper_grad = jax.vjp(gelu_tanh, upper_pre)[1](hidden_grad)[0].astype(jnp.bfloat16)
    up_grad = matmul_tn(second, upper_grad)
    second_grad = combine_parts(matmul_nt(upper_grad, up_full))
    middle_grad = out_grad + norm_back(second_grad, normed_two, inv_two, gain_two)
    middle_bf = middle_grad.astype(jnp.bfloat16)
    middle_whole = spread_whole(middle_bf)
    o_grad = matmul_tn(attended_bf, middle_whole)
    attended_grad = matmul_nt(middle_whole, o_full).astype(jnp.bfloat16).reshape(shape_four)
    scores = score_block(queries, key_rows)
    probs = jnp.exp(scores - log_total)
    probs_bf = probs.astype(jnp.bfloat16)
    prob_grad = jnp.einsum(
        "bqhd,bkhd->bhqk", attended_grad, value_rows, preferred_element_type=jnp.float32
    )
    value_grad = jnp.einsum(
        "bhqk,bqhd->bkhd", probs_bf, attended_grad, preferred_element_type=jnp.float32
    )
    value_grad = value_grad.reshape(row_count, -1).astype(jnp.bfloat16)
    row_dot = jnp.sum(prob_grad * probs, axis=-1, keepdims=True)
    score_grad = (probs * (prob_grad - row_dot)).astype(jnp.bfloat16)
    query_grad = jnp.einsum(
        "bhqk,bkhd->bqhd", score_grad, key_rows, preferred_element_type=jnp.float32
    )
    query_grad = (query_grad.reshape(row_count, -1) * HEAD ** (-0.5)).astype(jnp.bfloat16)
    key_grad = jnp.einsum(
        "bhqk,bqhd->bkhd", score_grad, queries, preferred_element_type=jnp.float32
    )
    key_grad = key_grad.reshape(row_count, -1).astype(jnp.bfloat16)
    first_grad = combine_parts(
        matmul_nt(query_grad, q_full) + matmul_nt(key_grad, k_full) + matmul_nt(value_grad, v_full)
    )
    input_grad = middle_grad + norm_back(first_grad, normed_one, inv_one, gain_one)
    matrices = (
        matmul_tn(first, query_grad),
        matmul_tn(first, key_grad),
        matmul_tn(first, value_grad),
        o_grad,
        up_grad,
        down_grad,
    )
    vector_grads = (
        jnp.sum(first_grad * normed_one, axis=0),
        jnp.sum(first_grad, axis=0),
        jnp.sum(query_grad, axis=0, dtype=jnp.float32),
        jnp.sum(value_grad, axis=0, dtype=jnp.float32),
        jnp.sum(middle_bf, axis=0, dtype=jnp.float32),
        jnp.sum(second_grad * normed_two, axis=0),
        jnp.sum(second_grad, axis=0),
        jnp.sum(upper_grad, axis=0, dtype=jnp.float32),
        jnp.sum(out_grad, axis=0),
    )
    return (input_grad.astype(jnp.bfloat16), matrices, vector_grads)


def split_heads_body(
    images,
    live,
    cotangent,
    ln1_gain,
    ln1_bias,
    q_weight,
    q_bias,
    k_weight,
    v_weight,
    v_bias,
    o_weight,
    o_bias,
    ln2_gain,
    ln2_bias,
    fc1_weight,
    fc1_bias,
    fc2_weight,
    fc2_bias,
):
    tensor_count = lax.axis_size("tensor")
    tensor_rank = lax.axis_index("tensor")
    length = images.shape[1]
    full_width = images.shape[2]
    part_width = full_width // tensor_count
    feature_start = tensor_rank * part_width
    head_width = q_bias.shape[0] // tensor_count
    head_start = tensor_rank * head_width
    unit_width = fc1_bias.shape[0] // tensor_count
    unit_start = tensor_rank * unit_width
    row_count = SLOTS * length
    row_share = (row_count + tensor_count - 1) // tensor_count
    padded_rows = row_share * tensor_count
    sizes_info = (SLOTS, length, row_count, padded_rows)
    q_shift = lax.dynamic_slice_in_dim(q_bias, head_start, head_width, 0)
    v_shift = lax.dynamic_slice_in_dim(v_bias, head_start, head_width, 0)
    up_shift = lax.dynamic_slice_in_dim(fc1_bias, unit_start, unit_width, 0)
    gain_one, shift_one, o_shift, gain_two, shift_two, down_shift = tuple(
        (
            lax.dynamic_slice_in_dim(vector, feature_start, part_width, 0)
            for vector in (ln1_gain, ln1_bias, o_bias, ln2_gain, ln2_bias, fc2_bias)
        )
    )
    vectors = (
        gain_one,
        shift_one,
        q_shift,
        v_shift,
        o_shift,
        gain_two,
        shift_two,
        up_shift,
        down_shift,
    )
    q_low = q_weight.astype(jnp.bfloat16)
    k_low = k_weight.astype(jnp.bfloat16)
    v_low = v_weight.astype(jnp.bfloat16)
    o_low = o_weight.astype(jnp.bfloat16)
    up_low = fc1_weight.astype(jnp.bfloat16)
    down_low = fc2_weight.astype(jnp.bfloat16)
    slot_mask = live.astype(jnp.float32)
    outputs = []
    input_grads = []
    matrix_sums = None
    vector_sums = None
    for micro_batch in range(MB):
        slot_start = micro_batch * SLOTS
        batch_tokens = images[slot_start : slot_start + SLOTS].reshape(row_count, full_width)
        batch_cot = cotangent[slot_start : slot_start + SLOTS].reshape(row_count, full_width)
        mask_rows = jnp.broadcast_to(
            slot_mask[slot_start : slot_start + SLOTS, None], (SLOTS, length)
        ).reshape(-1, 1)
        stream = lax.dynamic_slice_in_dim(batch_tokens, feature_start, part_width, 1).astype(
            jnp.float32
        )
        cot_stream = lax.dynamic_slice_in_dim(batch_cot, feature_start, part_width, 1)
        forward_weights = (
            lax.all_gather(q_low, "fsdp", axis=0, tiled=True),
            lax.all_gather(k_low, "fsdp", axis=0, tiled=True),
            lax.all_gather(v_low, "fsdp", axis=0, tiled=True),
            lax.all_gather(o_low, "fsdp", axis=1, tiled=True),
            lax.all_gather(up_low, "fsdp", axis=0, tiled=True),
            lax.all_gather(down_low, "fsdp", axis=1, tiled=True),
        )
        output, kept_state = forward_pass(stream, mask_rows, forward_weights, vectors, sizes_info)
        backward_weights = (
            lax.all_gather(q_low, "fsdp", axis=0, tiled=True),
            lax.all_gather(k_low, "fsdp", axis=0, tiled=True),
            lax.all_gather(v_low, "fsdp", axis=0, tiled=True),
            lax.all_gather(o_low, "fsdp", axis=1, tiled=True),
            lax.all_gather(up_low, "fsdp", axis=0, tiled=True),
            lax.all_gather(down_low, "fsdp", axis=1, tiled=True),
        )
        grad_in, matrices, vector_grads = backward_pass(
            cot_stream, mask_rows, backward_weights, vectors, kept_state, sizes_info
        )
        whole_out, whole_grad = (
            lax.all_gather(output, "tensor", axis=1, tiled=True),
            lax.all_gather(grad_in, "tensor", axis=1, tiled=True),
        )
        outputs.append(whole_out.reshape(SLOTS, length, full_width))
        input_grads.append(whole_grad.reshape(SLOTS, length, full_width))
        vector_sums = (
            vector_grads
            if vector_sums is None
            else jax.tree.map(jnp.add, vector_sums, vector_grads)
        )
        matrix_sums = (
            matrices if matrix_sums is None else jax.tree.map(jnp.add, matrix_sums, matrices)
        )
    total_wq, total_wk, total_wv, total_wo, total_up, total_down = matrix_sums
    shard_wq, shard_wk, shard_wv, shard_wo, shard_up, shard_down = (
        lax.psum_scatter(
            total_wq.astype(jnp.bfloat16), "fsdp", scatter_dimension=0, tiled=True
        ).astype(jnp.float32),
        lax.psum_scatter(
            total_wk.astype(jnp.bfloat16), "fsdp", scatter_dimension=0, tiled=True
        ).astype(jnp.float32),
        lax.psum_scatter(
            total_wv.astype(jnp.bfloat16), "fsdp", scatter_dimension=0, tiled=True
        ).astype(jnp.float32),
        lax.psum_scatter(
            total_wo.astype(jnp.bfloat16), "fsdp", scatter_dimension=1, tiled=True
        ).astype(jnp.float32),
        lax.psum_scatter(
            total_up.astype(jnp.bfloat16), "fsdp", scatter_dimension=0, tiled=True
        ).astype(jnp.float32),
        lax.psum_scatter(
            total_down.astype(jnp.bfloat16), "fsdp", scatter_dimension=1, tiled=True
        ).astype(jnp.float32),
    )
    final_wq, final_wk, final_wv, final_wo, final_up, final_down = (
        lax.psum(shard_wq.astype(jnp.bfloat16), "replica").astype(jnp.float32),
        lax.psum(shard_wk.astype(jnp.bfloat16), "replica").astype(jnp.float32),
        lax.psum(shard_wv.astype(jnp.bfloat16), "replica").astype(jnp.float32),
        lax.psum(shard_wo.astype(jnp.bfloat16), "replica").astype(jnp.float32),
        lax.psum(shard_up.astype(jnp.bfloat16), "replica").astype(jnp.float32),
        lax.psum(shard_down.astype(jnp.bfloat16), "replica").astype(jnp.float32),
    )
    (
        sum_gain_one,
        sum_shift_one,
        sum_q_shift,
        sum_v_shift,
        sum_o_shift,
        sum_gain_two,
        sum_shift_two,
        sum_up_shift,
        sum_down_shift,
    ) = vector_sums
    summed = lax.psum(
        (
            sum_gain_one,
            sum_shift_one,
            sum_q_shift,
            sum_v_shift,
            sum_o_shift,
            sum_gain_two,
            sum_shift_two,
            sum_up_shift,
            sum_down_shift,
        ),
        ("replica", "fsdp"),
    )
    (
        grad_gain_one,
        grad_shift_one,
        grad_q_shift,
        grad_v_shift,
        grad_o_shift,
        grad_gain_two,
        grad_shift_two,
        grad_up_shift,
        grad_down_shift,
    ) = summed
    return (
        jnp.concatenate(outputs, axis=0),
        jnp.concatenate(input_grads, axis=0),
        grad_gain_one,
        grad_shift_one,
        final_wq,
        grad_q_shift,
        final_wk,
        final_wv,
        grad_v_shift,
        final_wo,
        grad_o_shift,
        grad_gain_two,
        grad_shift_two,
        final_up,
        grad_up_shift,
        final_down,
        grad_down_shift,
    )


WINDOW = 256
LANES = 128
SHIFT = 64
VMEM = 60 * 2**20
GELU = 0.7978845608
EVERY = ("tensor", "fsdp", "replica")


def ceil_to(value, step):
    return -(-value // step) * step


def call(kernel, name, grid, scalars, ins, outs, flops=0, scratch=(), aliases=None):
    total = sum(array.size * array.dtype.itemsize for array, _ in ins)
    return pl.pallas_call(
        kernel,
        grid_spec=pltpu.PrefetchScalarGridSpec(
            num_scalar_prefetch=1,
            grid=grid,
            in_specs=[spec for _, spec in ins],
            out_specs=[spec for _, _, spec in outs],
            scratch_shapes=list(scratch),
        ),
        out_shape=[jax.ShapeDtypeStruct(shape, dtype) for shape, dtype, _ in outs],
        input_output_aliases=aliases or {},
        compiler_params=pltpu.CompilerParams(vmem_limit_bytes=VMEM),
        cost_estimate=pl.CostEstimate(flops=flops, bytes_accessed=total, transcendentals=0),
        name=name,
    )(scalars, *(array for array, _ in ins))


def fixed(shape, index):
    return pl.BlockSpec(shape, index, pipeline_mode=pl.Buffered(1))


def head_window(offset, base, rows):
    start = (offset + base) // LANES * LANES
    lane = lax.broadcasted_iota(jnp.int32, (rows, WINDOW), 1) + start
    inside = (lane >= offset + base) & (lane < offset + base + HEAD)
    return pl.ds(pl.multiple_of(start, LANES), WINDOW), inside


def attention(qvk, length, rows, width, group):
    heads = width // HEAD
    count = qvk.shape[0] // rows
    steps = heads // group
    out_width = ceil_to(width + SHIFT, WINDOW)

    def kernel(none_ref, qvk_ref, mixed_ref, probs_ref):
        @pl.when(pl.program_id(1) == 0)
        def _():
            mixed_ref[...] = jnp.zeros_like(mixed_ref)

        real = lax.broadcasted_iota(jnp.int32, (rows, rows), 1) < length

        def head(item):
            return (pl.program_id(1) * group + item) * HEAD

        def scores_of(item):
            at_q, _ = head_window(head(item), 0, rows)
            at_k, in_k = head_window(head(item), 2 * width, rows)
            key_rows = jnp.where(in_k, qvk_ref[:, at_k], 0)
            return jnp.where(real, matmul_nt(qvk_ref[:, at_q], key_rows), -1e30)

        following = scores_of(0)
        for item in range(group):
            scores = following
            if item + 1 < group:
                following = scores_of(item + 1)
            at_v, in_v = head_window(head(item), width, rows)
            at_o, in_o = head_window(head(item), SHIFT, rows)
            value_rows = jnp.where(in_v, qvk_ref[:, at_v], 0)
            powers = jnp.exp(scores - jnp.max(scores, axis=1, keepdims=True))
            total = jnp.sum(powers, axis=1, keepdims=True)
            probs = (powers * (1.0 / total)).astype(jnp.bfloat16)
            probs_ref[item] = probs
            mixed = matmul(probs, value_rows).astype(jnp.bfloat16)
            mixed_ref[:, at_o] = jnp.where(in_o, mixed, mixed_ref[:, at_o])

    return call(
        kernel,
        "attention",
        (count, steps),
        jnp.zeros((1,), jnp.int32),
        [(qvk, pl.BlockSpec((rows, qvk.shape[1]), lambda i, g, s: (i, 0)))],
        [
            ((count * rows, out_width), jnp.bfloat16, pl.BlockSpec((rows, out_width), lambda i, g, s: (i, 0))),
            (
                (count * heads, rows, rows),
                jnp.bfloat16,
                pl.BlockSpec((group, rows, rows), lambda i, g, s: (i * steps + g, 0, 0)),
            ),
        ],
        flops=4 * count * heads * rows * rows * WINDOW,
    )


def attention_back(qvk, mixed, grad, probs, images, kept, rows, width, group):
    heads = width // HEAD
    steps = heads // group
    at = images.start
    count = len(images)

    def kernel(none_ref, qvk_ref, mixed_ref, grad_ref, probs_ref, *refs):
        out_ref, sums_ref = refs[-2:]

        @pl.when(pl.program_id(1) == 0)
        def _():
            out_ref[...] = jnp.zeros_like(out_ref)

        for item in range(group):
            offset = (pl.program_id(1) * group + item) * HEAD
            at_q, in_q = head_window(offset, 0, rows)
            at_v, in_v = head_window(offset, width, rows)
            at_k, in_k = head_window(offset, 2 * width, rows)
            at_o, in_o = head_window(offset, SHIFT, rows)
            grad = jnp.where(in_o, grad_ref[:, at_o], 0)
            query_rows = jnp.where(in_q, qvk_ref[:, at_q], 0)
            key_rows = jnp.where(in_k, qvk_ref[:, at_k], 0)
            probs = probs_ref[item]
            row_dot = jnp.sum(
                grad.astype(jnp.float32) * mixed_ref[:, at_o].astype(jnp.float32), axis=1, keepdims=True
            )
            prob_grad = matmul_nt(grad, qvk_ref[:, at_v])
            score_grad = (probs.astype(jnp.float32) * (prob_grad - row_dot)).astype(jnp.bfloat16)
            value_grad = matmul_tn(probs, grad).astype(jnp.bfloat16)
            query_grad = (matmul(score_grad, key_rows) * HEAD ** (-0.5)).astype(jnp.bfloat16)
            key_grad = matmul_tn(score_grad, query_rows).astype(jnp.bfloat16)
            out_ref[:, at_q] = jnp.where(in_q, query_grad, out_ref[:, at_q])
            out_ref[:, at_v] = jnp.where(in_v, value_grad, out_ref[:, at_v])
            out_ref[:, at_k] = jnp.where(in_k, key_grad, out_ref[:, at_k])

        @pl.when(pl.program_id(1) == steps - 1)
        def _():
            total = jnp.sum(out_ref[...].astype(jnp.float32), axis=0, keepdims=True)
            sums_ref[0] = jnp.broadcast_to(total, sums_ref.shape[1:])

    ins = [
        (qvk, pl.BlockSpec((rows, qvk.shape[1]), lambda i, g, s: (at + i, 0))),
        (mixed, pl.BlockSpec((rows, mixed.shape[1]), lambda i, g, s: (at + i, 0))),
        (grad, pl.BlockSpec((rows, mixed.shape[1]), lambda i, g, s: (at + i, 0))),
        (probs, pl.BlockSpec((group, rows, rows), lambda i, g, s: ((at + i) * steps + g, 0, 0))),
    ]
    if kept is not None:
        ins.append((kept, pl.BlockSpec(memory_space=pl.ANY)))
    grads, sums = call(
        kernel,
        "attention_back",
        (count, steps),
        jnp.zeros((1,), jnp.int32),
        ins,
        [
            (qvk.shape, jnp.bfloat16, pl.BlockSpec((rows, qvk.shape[1]), lambda i, g, s: (at + i, 0))),
            ((count, 8, qvk.shape[1]), jnp.float32, pl.BlockSpec((1, 8, qvk.shape[1]), lambda i, g, s: (i, 0, 0))),
        ],
        aliases=None if kept is None else {5: 0},
        flops=8 * count * heads * rows * rows * WINDOW,
    )
    return grads, jnp.sum(sums[:, 0], axis=0)


def place(pieces, slots, total):
    def kernel(slots_ref, *refs):
        at = 0
        for ref in refs[:-1]:
            for block in range(ref.shape[0]):
                refs[-1][pl.ds(slots_ref[at], 1)] = ref[block : block + 1]
                at += 1

    def whole(shape):
        return fixed(shape, lambda i, s: (0, 0, 0))

    shape = (total, *pieces[0].shape[1:])
    return call(
        kernel,
        "place",
        (1,),
        jnp.stack([slot for group in slots for slot in group]).astype(jnp.int32),
        [(piece, whole(piece.shape)) for piece in pieces],
        [(shape, pieces[0].dtype, whole(shape))],
    )[0]


def outer_sum(left, right, ranks, step, total=None, kept=None, at=None, scalars=None):
    rows, lines = left.shape
    columns = right.shape[1] // ranks
    steps = columns // step
    held = ranks * lines if kept is None else kept.shape[0]

    def kernel(scalars_ref, left_ref, right_ref, *refs):
        refs[-1][...] = matmul_tn(left_ref[...], right_ref[...]).astype(refs[-1].dtype)

    def place_of(t, j, s):
        return (t, j) if kept is None else (s[at[0]], at[1])

    return call(
        kernel,
        "outer_sum",
        (ranks, steps),
        jnp.zeros((1,), jnp.int32) if scalars is None else scalars,
        [
            (left, fixed((rows, lines), lambda t, j, s: (0, 0))),
            (right, pl.BlockSpec((rows, step), lambda t, j, s: (0, t * steps + j))),
        ]
        + ([] if kept is None else [(kept, pl.BlockSpec(memory_space=pl.ANY))]),
        [((held, total or columns), jnp.bfloat16, pl.BlockSpec((lines, step), place_of))],
        flops=2 * rows * lines * columns * ranks,
        aliases=None if kept is None else {3: 0},
    )[0]


def tie(*values):
    return lax.optimization_barrier(values)


def swap(array, axis, bits):
    size = lax.axis_size(axis)
    return lax.ppermute(array, axis, [(rank, rank ^ bits) for rank in range(size)])


def turn(array, axis, steps):
    size = lax.axis_size(axis)
    return lax.ppermute(array, axis, [(rank, (rank + steps) % size) for rank in range(size)])


def replica_bits():
    bit = lax.axis_size("replica") // 2
    bits = []
    while bit:
        bits.append(bit)
        bit //= 2
    return bits


def swap_found(found, bit):
    return {**found, **{bits ^ bit: swap(held, "replica", bit) for bits, held in found.items()}}


def among_replicas(piece):
    found = {0: piece}
    for bit in replica_bits():
        found = swap_found(found, bit)
    return found


def from_lines(shard):
    copies = lax.axis_size("replica")
    blocks = shard.reshape(copies, -1, shard.shape[1])
    mine = lax.dynamic_slice_in_dim(blocks, lax.axis_index("replica"), 1, 0)
    return [mine] + [turn(mine, "fsdp", step) for step in range(1, lax.axis_size("fsdp"))]


def slots_of(found, skip):
    copies, lines = lax.axis_size("replica"), lax.axis_size("fsdp")
    copy, line = lax.axis_index("replica"), lax.axis_index("fsdp")
    starts = [(line - step) % lines * copies for step in range(skip, lines)]
    return [[start + (copy ^ bits) for start in starts] for bits in found]


def gather_own(shard, parts):
    copies, lines, line = lax.axis_size("replica"), lax.axis_size("fsdp"), lax.axis_index("fsdp")
    blocks = shard.reshape(copies, -1, shard.shape[1])
    pieces, slots = [blocks], [[line * copies + at for at in range(copies)]]
    if lines > 1:
        found = among_replicas(jnp.concatenate(parts[1:], axis=0))
        pieces += list(found.values())
        slots += slots_of(found, 1)
    return place(pieces, slots, lines * copies).reshape(-1, shard.shape[1])


def gather_far(parts, rank):
    found = {0: swap(jnp.concatenate(parts, axis=0), "tensor", rank)}
    for bit in replica_bits()[:-1]:
        found = swap_found(found, bit)
    return found


def finish_far(found):
    for bit in replica_bits()[-1:]:
        found = swap_found(found, bit)
    total = lax.axis_size("replica") * lax.axis_size("fsdp")
    whole = place(list(found.values()), slots_of(found, 0), total)
    return whole.reshape(-1, whole.shape[2])


def gather_whole(shard):
    share = shard.shape[0] // lax.axis_size("replica")
    part = lax.dynamic_slice_in_dim(shard, lax.axis_index("replica") * share, share, 0)
    return lax.all_gather(part, EVERY, axis=0, tiled=True)


def add_low(first_term, *terms):
    total = first_term.astype(jnp.float32)
    for term in terms:
        total = total + term.astype(jnp.float32)
    return total.astype(jnp.bfloat16)


def by_lines(term):
    bits = len(replica_bits())
    return term.reshape(lax.axis_size("fsdp"), *(2 for _ in range(bits)), -1, term.shape[1])


def halve(held, bit):
    side = lax.axis_index("replica") // bit % 2
    axis = held.ndim - 3
    keep = lax.dynamic_index_in_dim(held, side, axis, keepdims=False)
    send = lax.dynamic_index_in_dim(held, 1 - side, axis, keepdims=False)
    return add_low(keep, swap(send, "replica", bit))


def sum_lines(held):
    lines, line = lax.axis_size("fsdp"), lax.axis_index("fsdp")
    terms = [lax.dynamic_index_in_dim(held, line, 0, keepdims=True)]
    for step in range(1, lines):
        send = lax.dynamic_index_in_dim(held, (line + step) % lines, 0, keepdims=True)
        terms.append(turn(send, "fsdp", step))
    return add_low(*terms)


def place_found(found):
    copy = lax.axis_index("replica")
    whole = place(list(found.values()), [[copy ^ bits] for bits in found], len(found))
    return whole.reshape(-1, whole.shape[2])


def sum_over(vector, axes):
    size = lax.axis_size(axes)
    terms = [vector] + [
        lax.ppermute(vector, axes, [(rank, rank ^ bits) for rank in range(size)]) for bits in range(1, size)
    ]
    while len(terms) > 1:
        terms = [left + right for left, right in zip(terms[::2], terms[1::2])]
    return terms[0]


def norm_parts(values):
    center = jnp.mean(values, axis=1, keepdims=True)
    spread = jnp.mean(values * values, axis=1, keepdims=True) - center * center
    scale_inv = lax.rsqrt(spread + EPSILON)
    return (values - center) * scale_inv, scale_inv


def norm_backward(grad, normed, scale_inv, gain_vec):
    scaled = grad * gain_vec
    mean_one = jnp.mean(scaled, axis=1, keepdims=True)
    mean_two = jnp.mean(scaled * normed, axis=1, keepdims=True)
    return scale_inv * (scaled - mean_one - normed * mean_two)


def image_body(
    images,
    live,
    cotangent,
    ln1_gain,
    ln1_bias,
    q_weight,
    q_bias,
    k_weight,
    v_weight,
    v_bias,
    o_weight,
    o_bias,
    ln2_gain,
    ln2_bias,
    fc1_weight,
    fc1_bias,
    fc2_weight,
    fc2_bias,
):
    low, full = jnp.bfloat16, jnp.float32
    tensor_count = lax.axis_size("tensor")
    tensor_rank = lax.axis_index("tensor")
    slots, length, wide = images.shape
    count = slots // tensor_count
    rows = ceil_to(length, 32)
    half = rows // 2
    width = q_weight.shape[1]
    units = fc1_weight.shape[1]
    qvk_width = ceil_to(3 * width, WINDOW)
    o_width = ceil_to(width + SHIFT, WINDOW)
    unit_width = ceil_to(units, WINDOW)
    unit_width = ceil_to(unit_width, o_width)
    ranks = range(tensor_count)
    all_rows = count * rows
    heads = width // HEAD
    group = next(size for size in (8, 4, 2, 1) if heads % size == 0)
    blocks = all_rows // half
    scalars = jnp.concatenate(
        [
            jnp.stack([tensor_rank * count] + [tensor_rank ^ rank for rank in ranks]).astype(jnp.int32),
            lax.dynamic_slice_in_dim(live, tensor_rank * count, count, 0),
        ]
    )
    live_at = 1 + tensor_count

    def columns(parts, ahead, total):
        body_part = jnp.concatenate(parts, axis=1)
        return jnp.pad(body_part, ((0, 0), (ahead, total - ahead - body_part.shape[1])))

    def row(vector):
        return vector.reshape(1, -1)

    def slots_spec(first=0):
        return pl.BlockSpec((1, half, wide), lambda i, s: (s[0] + first + i // 2, i % 2, 0))

    def rows_spec(size, first=0):
        return pl.BlockSpec((half, size), lambda i, s: (2 * first + i, 0))

    def vector_spec():
        return pl.BlockSpec((1, wide), lambda i, s: (0, 0))

    def sums_spec():
        return pl.BlockSpec((8, wide), lambda i, s: (0, 0))

    def real_rows(values):
        at = lax.broadcasted_iota(jnp.int32, (half, 1), 0) + pl.program_id(0) % 2 * half
        return jnp.where(at < length, values.astype(full), 0.0)

    def live_slot(scalars_ref, first=0):
        return scalars_ref[live_at + first + pl.program_id(0) // 2].astype(full)

    def add_sums(sums_ref, *terms):
        @pl.when(pl.program_id(0) == 0)
        def _():
            sums_ref[...] = jnp.zeros_like(sums_ref)

        for at, term in enumerate(terms):
            sums_ref[at : at + 1] += jnp.sum(term, axis=0, keepdims=True)

    def product(part_refs, weight_refs):
        total = matmul_nt(part_refs[0][...], weight_refs[0][...])
        for part_ref, weight_ref in zip(part_refs[1:], weight_refs[1:]):
            total = total + matmul_nt(part_ref[...], weight_ref[...])
        return total

    qvk_shard = columns([w.astype(low) for w in (q_weight, v_weight, k_weight)], 0, qvk_width)
    parts = from_lines(qvk_shard)

    def first_kernel(scalars_ref, images_ref, cot_ref, gain_ref, shift_ref, first_ref, grad_ref, sums_ref):
        normed, _ = norm_parts(real_rows(images_ref[0]))
        first_ref[...] = (normed * gain_ref[...] + shift_ref[...]).astype(low)
        grad = real_rows(cot_ref[0]) * live_slot(scalars_ref)
        grad_ref[...] = grad.astype(low)
        add_sums(sums_ref, grad)

    first, out_grad, first_sums = call(
        first_kernel,
        "first_norm",
        (blocks,),
        scalars,
        [(images, slots_spec()), (cotangent, slots_spec()), (row(ln1_gain), vector_spec()), (row(ln1_bias), vector_spec())],
        [
            ((all_rows, wide), low, rows_spec(wide)),
            ((all_rows, wide), low, rows_spec(wide)),
            ((8, wide), full, sums_spec()),
        ],
    )

    parts, first, out_grad = tie(parts, first, out_grad)
    up_o_shard = jnp.concatenate(
        [
            columns([fc1_weight.astype(low)], 0, unit_width),
            columns([o_weight.astype(low).T], SHIFT, o_width),
        ],
        axis=1,
    )
    down_shard = columns([fc2_weight.astype(low).T], 0, unit_width)
    up_o_shard, down_shard, parts = tie(up_o_shard, down_shard, parts)
    up_o_whole = gather_whole(up_o_shard)
    down_whole = gather_whole(down_shard)
    qvk_weights = [gather_own(qvk_shard, parts)]
    far_parts = [gather_far(parts, rank) for rank in ranks[1:]]

    def of_rank(vector, rank, size):
        return lax.dynamic_slice_in_dim(vector, (tensor_rank ^ rank) * size, size, 0)

    scale_row = jnp.where(jnp.arange(qvk_width) < width, HEAD ** (-0.5), 1.0)
    qvk, mixed, probs = [], [], []
    for rank in ranks:
        shift_row = jnp.pad(
            jnp.concatenate([of_rank(q_bias, rank, width), of_rank(v_bias, rank, width)]),
            (0, qvk_width - 2 * width),
        )
        qvk.append(((matmul(first, qvk_weights[rank]) + shift_row) * scale_row).astype(low))
        mixed_part, probs_part = attention(qvk[rank], length, rows, width, group)
        if rank == 0:
            mixed_part, first, far_parts = tie(mixed_part, first, far_parts)
            qvk_weights += [finish_far(found) for found in far_parts]
        mixed.append(mixed_part)
        probs.append(probs_part)

    def o_spec(rank):
        return fixed((wide, o_width), lambda i, s: (s[1 + rank], unit_width // o_width))

    def middle_kernel(scalars_ref, *refs):
        images_ref, bias_ref, gain_ref, shift_ref, middle_ref, second_ref = refs[2 * tensor_count :]
        total = product(refs[:tensor_count], refs[tensor_count : 2 * tensor_count])
        middle = real_rows(images_ref[0]) + (total + bias_ref[...])
        middle_ref[...] = middle
        normed, _ = norm_parts(middle)
        second_ref[...] = (normed * gain_ref[...] + shift_ref[...]).astype(low)

    middle, second = call(
        middle_kernel,
        "middle_norm",
        (blocks,),
        scalars,
        [(part, rows_spec(o_width)) for part in mixed]
        + [(up_o_whole, o_spec(rank)) for rank in ranks]
        + [
            (images, slots_spec()),
            (row(o_bias), vector_spec()),
            (row(ln2_gain), vector_spec()),
            (row(ln2_bias), vector_spec()),
        ],
        [((all_rows, wide), full, rows_spec(wide)), ((all_rows, wide), low, rows_spec(wide))],
        flops=2 * all_rows * wide * o_width * tensor_count,
    )

    chunk = o_width

    def unit_rows():
        return pl.BlockSpec((half, unit_width), lambda t, i, s: (i, t))

    def unit_weights():
        return pl.BlockSpec((wide, unit_width), lambda t, i, s: (t, 0))

    def hidden_kernel(scalars_ref, second_ref, weight_ref, shift_ref, hidden_ref, slope_ref):
        for start in range(0, unit_width, chunk):
            at = slice(start, start + chunk)
            upper = matmul(second_ref[...], weight_ref[:, at]) + shift_ref[:, at]
            square = upper * upper
            share = 0.5 + 0.5 * jnp.tanh(upper * (GELU + GELU * 0.044715 * square))
            hidden = upper * share
            slope = share + (hidden - hidden * share) * (2 * GELU + 6 * GELU * 0.044715 * square)
            hidden_ref[:, at] = hidden.astype(low)
            slope_ref[:, at] = slope.astype(low)

    unit_shift = jnp.pad(
        fc1_bias.reshape(tensor_count, units), ((0, 0), (0, unit_width - units))
    ).reshape(1, -1)
    hidden, slopes = call(
        hidden_kernel,
        "hidden",
        (tensor_count, blocks),
        scalars,
        [
            (second, pl.BlockSpec((half, wide), lambda t, i, s: (i, 0))),
            (up_o_whole, unit_weights()),
            (unit_shift, pl.BlockSpec((1, unit_width), lambda t, i, s: (0, t))),
        ],
        [((all_rows, tensor_count * unit_width), low, unit_rows())] * 2,
        flops=2 * all_rows * wide * unit_width * tensor_count,
    )
    down_terms = outer_sum(out_grad, hidden, tensor_count, chunk)
    down_terms, hidden = tie(down_terms, hidden)
    down_share = lax.psum_scatter(down_terms, EVERY, scatter_dimension=0, tiled=True)

    def weight_spec(rank):
        return fixed((wide, unit_width), lambda i, s: (rank, 0))

    def unit_spec(rank):
        return pl.BlockSpec((half, unit_width), lambda i, s: (i, rank))

    def output_kernel(scalars_ref, *refs):
        middle_ref, bias_ref, output_ref, whole_ref = refs[2 * tensor_count :]
        total = product(refs[:tensor_count], refs[tensor_count : 2 * tensor_count])
        result = middle_ref[...] + (total + bias_ref[...])
        output_ref[0] = (result * live_slot(scalars_ref)).astype(low)
        whole_ref[0] = output_ref[0]

    output, out_whole = call(
        output_kernel,
        "output",
        (blocks,),
        scalars,
        [(hidden, unit_spec(rank)) for rank in ranks]
        + [(down_whole, weight_spec(rank)) for rank in ranks]
        + [(middle, rows_spec(wide)), (row(fc2_bias), vector_spec())],
        [
            ((count, length, wide), low, pl.BlockSpec((1, half, wide), lambda i, s: (i // 2, i % 2, 0))),
            ((slots, length, wide), low, slots_spec()),
        ],
        flops=2 * all_rows * wide * unit_width * tensor_count,
    )

    def trade(part):
        return [swap(part, "tensor", rank) for rank in ranks[1:]]

    def lay(whole, parts, first):
        for rank, part in zip(ranks[1:], parts):
            whole = lax.dynamic_update_slice_in_dim(whole, part, (tensor_rank ^ rank) * count + first, 0)
        return whole

    output, out_grad = tie(output, out_grad)
    out_parts = trade(output)

    def hidden_back_kernel(scalars_ref, grad_ref, weight_ref, slope_ref, upper_ref, sums_ref):
        @pl.when(pl.program_id(1) == 0)
        def _():
            sums_ref[...] = jnp.zeros_like(sums_ref)

        for start in range(0, unit_width, chunk):
            at = slice(start, start + chunk)
            upper = matmul(grad_ref[...], weight_ref[:, at]) * slope_ref[:, at].astype(full)
            rounded = upper.astype(low)
            upper_ref[:, at] = rounded
            sums_ref[0:1, at] += jnp.sum(rounded.astype(full), axis=0, keepdims=True)

    upper_grads, upper_sums = call(
        hidden_back_kernel,
        "hidden_back",
        (tensor_count, blocks),
        scalars,
        [
            (out_grad, pl.BlockSpec((half, wide), lambda t, i, s: (i, 0))),
            (down_whole, unit_weights()),
            (slopes, unit_rows()),
        ],
        [
            ((all_rows, tensor_count * unit_width), low, unit_rows()),
            ((8, tensor_count * unit_width), full, pl.BlockSpec((8, unit_width), lambda t, i, s: (0, t))),
        ],
        flops=2 * all_rows * wide * unit_width * tensor_count,
    )
    up_terms = outer_sum(second, upper_grads, tensor_count, o_width, unit_width + o_width)
    up_terms, upper_grads = tie(up_terms, upper_grads)

    def middle_back_kernel(scalars_ref, *refs):
        middle_ref, grad_ref, gain_ref, *o_refs = refs[2 * tensor_count : 3 * tensor_count + 3]
        middle_grad_ref, low_ref, sums_ref, *mixed_grad_refs = refs[3 * tensor_count + 3 :]
        total = product(refs[:tensor_count], refs[tensor_count : 2 * tensor_count])
        normed, scale_inv = norm_parts(middle_ref[...])
        middle_grad = grad_ref[...].astype(full) + norm_backward(total, normed, scale_inv, gain_ref[...])
        middle_grad_ref[...] = middle_grad
        rounded = middle_grad.astype(low)
        low_ref[...] = rounded
        for o_ref, mixed_grad_ref in zip(o_refs, mixed_grad_refs):
            mixed_grad_ref[...] = matmul(rounded, o_ref[...]).astype(low)
        add_sums(sums_ref, total * normed, total, rounded.astype(full))

    middle_grad, middle_low, second_sums, *mixed_grads = call(
        middle_back_kernel,
        "middle_back",
        (blocks,),
        scalars,
        [(upper_grads, unit_spec(rank)) for rank in ranks]
        + [(up_o_whole, weight_spec(rank)) for rank in ranks]
        + [(middle, rows_spec(wide)), (out_grad, rows_spec(wide)), (row(ln2_gain), vector_spec())]
        + [(up_o_whole, o_spec(rank)) for rank in ranks],
        [
            ((all_rows, wide), full, rows_spec(wide)),
            ((all_rows, wide), low, rows_spec(wide)),
            ((8, wide), full, sums_spec()),
        ]
        + [((all_rows, o_width), low, rows_spec(o_width)) for rank in ranks],
        flops=2 * all_rows * wide * (unit_width + o_width) * tensor_count,
    )

    for rank in ranks:
        up_terms = outer_sum(
            middle_low,
            mixed[rank],
            1,
            o_width,
            unit_width + o_width,
            up_terms,
            (1 + rank, unit_width // o_width),
            scalars,
        )
    up_terms, mixed_grads[-1], out_parts = tie(up_terms, mixed_grads[-1], out_parts)
    up_share = lax.psum_scatter(up_terms, EVERY, scatter_dimension=0, tiled=True)
    bits = replica_bits()[::-1]

    def back(rank, which, kept):
        return attention_back(
            qvk[rank], mixed[rank], mixed_grads[rank], probs[rank], which, kept, rows, width, group
        )

    def first_back_kernel(scalars_ref, *refs):
        images_ref, grad_ref, gain_ref = refs[2 * tensor_count : 2 * tensor_count + 3]
        out_ref, whole_ref, sums_ref = refs[-3:]
        total = product(refs[:tensor_count], refs[tensor_count : 2 * tensor_count])
        normed, scale_inv = norm_parts(real_rows(images_ref[0]))
        grad = grad_ref[...] + norm_backward(total, normed, scale_inv, gain_ref[...])
        out_ref[0] = grad.astype(low)
        whole_ref[0] = out_ref[0]
        add_sums(sums_ref, total * normed, total)

    qvk_grads, qvk_sums = [None] * tensor_count, [0.0] * tensor_count
    input_whole = None
    third_sums = 0.0
    in_parts = []

    def attend(rank, which):
        qvk_grads[rank], sums = back(rank, which, qvk_grads[rank])
        qvk_sums[rank] = qvk_sums[rank] + sums

    def first_back(slot, whole):
        ahead = [] if whole is None else [(whole, pl.BlockSpec(memory_space=pl.ANY))]
        return call(
            first_back_kernel,
            "first_back",
            (2,),
            scalars,
            [(grads, rows_spec(qvk_width, slot)) for grads in qvk_grads]
            + [(weight, fixed((wide, qvk_width), lambda i, s: (0, 0))) for weight in qvk_weights]
            + [(images, slots_spec(slot)), (middle_grad, rows_spec(wide, slot)), (row(ln1_gain), vector_spec())]
            + ahead,
            [
                ((1, length, wide), low, pl.BlockSpec((1, half, wide), lambda i, s: (0, i, 0))),
                ((slots, length, wide), low, slots_spec(slot)),
                ((8, wide), full, sums_spec()),
            ],
            aliases={2 * tensor_count + 4: 1} if ahead else None,
            flops=2 * rows * wide * qvk_width * tensor_count,
        )

    last = count - 1

    def halve_all(terms, which):
        for bit in which:
            terms = [halve(term, bit) for term in terms]
        return terms

    def join_on(found, which):
        for bit in which:
            found = swap_found(found, bit)
        return found

    far_bits, far_bit = replica_bits()[:-1], replica_bits()[-1:]

    down_found = join_on({0: down_share[None]}, far_bits)
    for rank in ranks[1:]:
        attend(rank, range(count))
    qvk_grads[1:], mixed_grads[0], down_found, first = tie(qvk_grads[1:], mixed_grads[0], down_found, first)
    far = [by_lines(outer_sum(first, grads, 1, qvk_width // 2)) for grads in qvk_grads[1:]]
    down_grads = place_found(join_on(down_found, far_bit))
    far, mixed_grads[0], down_grads = tie(far, mixed_grads[0], down_grads)
    far_done = 0
    for slot in range(last):
        if slot > 0:
            in_parts.append(trade(input_grad))
        attend(0, range(slot, slot + 1))
        if slot == 0:
            far = halve_all(far, bits[:1])
            far, qvk_grads[0] = tie(far, qvk_grads[0])
        elif far_done == 1:
            far = halve_all(far, bits[1:])
        far_done += 1
        input_grad, input_whole, sums = first_back(slot, input_whole)
        third_sums = third_sums + sums
        far, in_parts, input_grad, mixed_grads[0] = tie(far, in_parts, input_grad, mixed_grads[0])
    if last > 0:
        in_parts.append(trade(input_grad))
    attend(0, range(last, count))
    near = by_lines(outer_sum(first, qvk_grads[0], 1, qvk_width // 2))
    if far_done < 2:
        far = halve_all(far, bits[far_done:])
    near, far, in_parts, qvk_grads[0] = tie(near, far, in_parts, qvk_grads[0])
    near = halve_all([near], bits[:1])
    near, qvk_grads[0], far = tie(near, qvk_grads[0], far)
    input_grad, input_whole, sums = first_back(last, input_whole)
    near = halve_all(near, bits[1:])
    far = [sum_lines(held) for held in far]
    (
        near,
        far,
        input_grad,
        input_whole,
        sums,
        third_sums,
        qvk_sums,
        first_sums,
        second_sums,
        upper_sums,
        out_whole,
        out_parts,
        down_grads,
        up_share,
    ) = tie(
        near,
        far,
        input_grad,
        input_whole,
        sums,
        third_sums,
        qvk_sums,
        first_sums,
        second_sums,
        upper_sums,
        out_whole,
        out_parts,
        down_grads,
        up_share,
    )
    third_sums = third_sums + sums
    in_parts.append(trade(input_grad))
    out_whole = lay(out_whole, out_parts, 0)
    for slot in range(last):
        input_whole = lay(input_whole, in_parts[slot], slot)
    near_total = add_low(
        sum_lines(near[0]), *(swap(term, "tensor", rank) for rank, term in zip(ranks[1:], far))
    )
    near_found = among_replicas(near_total)
    up_found = among_replicas(up_share[None])

    def all_ranks(parts, size):
        whole = jnp.zeros((tensor_count * size,), full)
        for rank in ranks:
            whole = lax.dynamic_update_slice_in_dim(whole, parts[rank], (tensor_rank ^ rank) * size, 0)
        return whole

    vectors = [
        third_sums[0],
        third_sums[1],
        all_ranks([sums[:width] for sums in qvk_sums], width),
        all_ranks([sums[width : 2 * width] for sums in qvk_sums], width),
        second_sums[2],
        second_sums[0],
        second_sums[1],
        upper_sums[0].reshape(tensor_count, unit_width)[:, :units].reshape(-1),
        first_sums[0],
    ]
    sizes = [vector.shape[0] for vector in vectors]
    joined = jnp.concatenate(vectors)
    padded = ceil_to(joined.shape[0], 8 * LANES)
    summed = jnp.pad(joined, (0, padded - joined.shape[0])).reshape(-1, LANES)
    summed = sum_over(sum_over(summed, "replica"), "fsdp")
    near_found, up_found, summed, in_parts[-1] = tie(near_found, up_found, summed, in_parts[-1])
    summed = sum_over(summed, "tensor").reshape(-1)
    in_grads = place_found(near_found)
    up_o_grads = place_found(up_found)
    input_whole = lay(input_whole, in_parts[-1], last)
    ends, start = [], 0
    for size in sizes:
        share = size // tensor_count
        ends.append(lax.dynamic_slice_in_dim(summed, start + tensor_rank * share, share, 0))
        start += size
    gain_one, shift_one, q_sum, v_sum, o_sum, gain_two, shift_two, up_sum, down_sum = ends
    return (
        out_whole,
        input_whole,
        gain_one,
        shift_one,
        in_grads[:, :width].astype(full),
        q_sum,
        in_grads[:, 2 * width : 3 * width].astype(full),
        in_grads[:, width : 2 * width].astype(full),
        v_sum,
        up_o_grads[:, unit_width + SHIFT : unit_width + SHIFT + width].astype(full).T,
        o_sum,
        gain_two,
        shift_two,
        up_o_grads[:, :units].astype(full),
        up_sum,
        down_grads[:, :units].astype(full).T,
        down_sum,
    )


def halves(size):
    return size & (size - 1) == 0


def by_images(mesh):
    return SLOTS * MB % mesh.shape["tensor"] == 0 and all(halves(size) for size in mesh.shape.values())


def solution(mesh):
    in_specs = (
        P(("replica", "fsdp"), None, None),
        P(("replica", "fsdp")),
        P(("replica", "fsdp"), None, None),
        P(),
        P(),
        P("fsdp", "tensor"),
        P(),
        P("fsdp", "tensor"),
        P("fsdp", "tensor"),
        P(),
        P("tensor", "fsdp"),
        P(),
        P(),
        P(),
        P("fsdp", "tensor"),
        P(),
        P("tensor", "fsdp"),
        P(),
    )
    out_specs = (
        P(("replica", "fsdp"), None, None),
        P(("replica", "fsdp"), None, None),
        P("tensor"),
        P("tensor"),
        P("fsdp", "tensor"),
        P("tensor"),
        P("fsdp", "tensor"),
        P("fsdp", "tensor"),
        P("tensor"),
        P("tensor", "fsdp"),
        P("tensor"),
        P("tensor"),
        P("tensor"),
        P("fsdp", "tensor"),
        P("tensor"),
        P("tensor", "fsdp"),
        P("tensor"),
    )
    body = image_body if by_images(mesh) else split_heads_body
    return jax.shard_map(body, mesh=mesh, in_specs=in_specs, out_specs=out_specs, check_vma=False)
```

```python
import functools

import jax
import jax.numpy as jnp
from jax import lax
from jax.experimental import pallas as pl
from jax.experimental.pallas import tpu as pltpu
from jax.sharding import PartitionSpec as P

HEAD = 72
MB = 2
SLOTS = 3


EPSILON = 1e-06


def matmul(first_op, second_op):
    return jnp.dot(first_op, second_op, preferred_element_type=jnp.float32)


def matmul_tn(first_op, second_op):
    return lax.dot_general(
        first_op, second_op, (((0,), (0,)), ((), ())), preferred_element_type=jnp.float32
    )


def matmul_nt(first_op, second_op):
    return lax.dot_general(
        first_op, second_op, (((1,), (1,)), ((), ())), preferred_element_type=jnp.float32
    )


def gelu_tanh(values):
    return jax.nn.gelu(values, approximate=True)


def row_totals(first_sum, second_sum):
    return lax.psum((first_sum, second_sum), "tensor")


def spread_whole(rounded):
    return lax.all_gather(rounded, "tensor", axis=1, tiled=True)


def combine_parts(partial_value):
    return lax.psum_scatter(partial_value, "tensor", scatter_dimension=1, tiled=True)


def normalize(stream, gain_vec, shift_vec):
    full_width = stream.shape[1] * lax.axis_size("tensor")
    totals = row_totals(
        jnp.sum(stream, axis=1, keepdims=True), jnp.sum(stream * stream, axis=1, keepdims=True)
    )
    center = totals[0] / full_width
    spread = totals[1] / full_width - center * center
    scale_inv = lax.rsqrt(spread + EPSILON)
    normed = (stream - center) * scale_inv
    rounded = (normed * gain_vec + shift_vec).astype(jnp.bfloat16)
    return (spread_whole(rounded), normed, scale_inv)


def norm_back(grad_part, normed, scale_inv, gain_vec):
    scaled = grad_part * gain_vec
    full_width = grad_part.shape[1] * lax.axis_size("tensor")
    totals = row_totals(
        jnp.sum(scaled, axis=1, keepdims=True), jnp.sum(scaled * normed, axis=1, keepdims=True)
    )
    mean_one = totals[0] / full_width
    mean_two = totals[1] / full_width
    return scale_inv * (scaled - mean_one - normed * mean_two)


def score_block(queries, key_rows):
    return jnp.einsum("bqhd,bkhd->bhqk", queries, key_rows, preferred_element_type=jnp.float32)


def forward_pass(stream, row_mask, weights, vectors, sizes_info):
    q_full, k_full, v_full, o_full, up_full, down_full = weights
    gain_one, shift_one, q_shift, v_shift, o_shift, gain_two, shift_two, up_shift, down_shift = (
        vectors
    )
    blocks, length, row_count, padded_rows = sizes_info
    head_count = q_shift.shape[0] // HEAD
    shape_four = (blocks, length, head_count, HEAD)
    first, normed_one, inv_one = normalize(stream, gain_one, shift_one)
    queries = (
        ((matmul(first, q_full) + q_shift) * HEAD ** (-0.5))
        .astype(jnp.bfloat16)
        .reshape(shape_four)
    )
    key_rows = matmul(first, k_full).astype(jnp.bfloat16).reshape(shape_four)
    value_rows = (matmul(first, v_full) + v_shift).astype(jnp.bfloat16).reshape(shape_four)
    scores = score_block(queries, key_rows)
    top_score = jnp.max(scores, axis=-1, keepdims=True)
    log_total = top_score + jnp.log(jnp.sum(jnp.exp(scores - top_score), axis=-1, keepdims=True))
    probs_bf = jnp.exp(scores - log_total).astype(jnp.bfloat16)
    attended = jnp.einsum(
        "bhqk,bkhd->bqhd", probs_bf, value_rows, preferred_element_type=jnp.float32
    )
    attended_bf = attended.reshape(row_count, head_count * HEAD).astype(jnp.bfloat16)
    middle = stream + combine_parts(matmul(attended_bf, o_full)) + o_shift
    second, normed_two, inv_two = normalize(middle, gain_two, shift_two)
    upper_pre = matmul(second, up_full) + up_shift
    hidden = gelu_tanh(upper_pre).astype(jnp.bfloat16)
    result = middle + combine_parts(matmul(hidden, down_full)) + down_shift
    output = (result * row_mask).astype(jnp.bfloat16)
    kept_state = (
        first,
        normed_one,
        inv_one,
        queries,
        key_rows,
        value_rows,
        log_total,
        attended_bf,
        normed_two,
        inv_two,
        second,
        upper_pre,
        hidden,
    )
    return (output, kept_state)


def backward_pass(cot_stream, row_mask, weights, vectors, kept_state, sizes_info):
    q_full, k_full, v_full, o_full, up_full, down_full = weights
    gain_one, shift_one, q_shift, v_shift, o_shift, gain_two, shift_two, up_shift, down_shift = (
        vectors
    )
    (
        first,
        normed_one,
        inv_one,
        queries,
        key_rows,
        value_rows,
        log_total,
        attended_bf,
        normed_two,
        inv_two,
        second,
        upper_pre,
        hidden,
    ) = kept_state
    blocks, length, row_count, padded_rows = sizes_info
    shape_four = queries.shape
    out_grad = cot_stream.astype(jnp.float32) * row_mask
    out_whole = spread_whole(out_grad.astype(jnp.bfloat16))
    down_grad = matmul_tn(hidden, out_whole)
    hidden_grad = matmul_nt(out_whole, down_full)
    upper_grad = jax.vjp(gelu_tanh, upper_pre)[1](hidden_grad)[0].astype(jnp.bfloat16)
    up_grad = matmul_tn(second, upper_grad)
    second_grad = combine_parts(matmul_nt(upper_grad, up_full))
    middle_grad = out_grad + norm_back(second_grad, normed_two, inv_two, gain_two)
    middle_bf = middle_grad.astype(jnp.bfloat16)
    middle_whole = spread_whole(middle_bf)
    o_grad = matmul_tn(attended_bf, middle_whole)
    attended_grad = matmul_nt(middle_whole, o_full).astype(jnp.bfloat16).reshape(shape_four)
    scores = score_block(queries, key_rows)
    probs = jnp.exp(scores - log_total)
    probs_bf = probs.astype(jnp.bfloat16)
    prob_grad = jnp.einsum(
        "bqhd,bkhd->bhqk", attended_grad, value_rows, preferred_element_type=jnp.float32
    )
    value_grad = jnp.einsum(
        "bhqk,bqhd->bkhd", probs_bf, attended_grad, preferred_element_type=jnp.float32
    )
    value_grad = value_grad.reshape(row_count, -1).astype(jnp.bfloat16)
    row_dot = jnp.sum(prob_grad * probs, axis=-1, keepdims=True)
    score_grad = (probs * (prob_grad - row_dot)).astype(jnp.bfloat16)
    query_grad = jnp.einsum(
        "bhqk,bkhd->bqhd", score_grad, key_rows, preferred_element_type=jnp.float32
    )
    query_grad = (query_grad.reshape(row_count, -1) * HEAD ** (-0.5)).astype(jnp.bfloat16)
    key_grad = jnp.einsum(
        "bhqk,bqhd->bkhd", score_grad, queries, preferred_element_type=jnp.float32
    )
    key_grad = key_grad.reshape(row_count, -1).astype(jnp.bfloat16)
    first_grad = combine_parts(
        matmul_nt(query_grad, q_full) + matmul_nt(key_grad, k_full) + matmul_nt(value_grad, v_full)
    )
    input_grad = middle_grad + norm_back(first_grad, normed_one, inv_one, gain_one)
    matrices = (
        matmul_tn(first, query_grad),
        matmul_tn(first, key_grad),
        matmul_tn(first, value_grad),
        o_grad,
        up_grad,
        down_grad,
    )
    vector_grads = (
        jnp.sum(first_grad * normed_one, axis=0),
        jnp.sum(first_grad, axis=0),
        jnp.sum(query_grad, axis=0, dtype=jnp.float32),
        jnp.sum(value_grad, axis=0, dtype=jnp.float32),
        jnp.sum(middle_bf, axis=0, dtype=jnp.float32),
        jnp.sum(second_grad * normed_two, axis=0),
        jnp.sum(second_grad, axis=0),
        jnp.sum(upper_grad, axis=0, dtype=jnp.float32),
        jnp.sum(out_grad, axis=0),
    )
    return (input_grad.astype(jnp.bfloat16), matrices, vector_grads)


def split_heads_body(
    images,
    live,
    cotangent,
    ln1_gain,
    ln1_bias,
    q_weight,
    q_bias,
    k_weight,
    v_weight,
    v_bias,
    o_weight,
    o_bias,
    ln2_gain,
    ln2_bias,
    fc1_weight,
    fc1_bias,
    fc2_weight,
    fc2_bias,
):
    tensor_count = lax.axis_size("tensor")
    tensor_rank = lax.axis_index("tensor")
    length = images.shape[1]
    full_width = images.shape[2]
    part_width = full_width // tensor_count
    feature_start = tensor_rank * part_width
    head_width = q_bias.shape[0] // tensor_count
    head_start = tensor_rank * head_width
    unit_width = fc1_bias.shape[0] // tensor_count
    unit_start = tensor_rank * unit_width
    row_count = SLOTS * length
    row_share = (row_count + tensor_count - 1) // tensor_count
    padded_rows = row_share * tensor_count
    sizes_info = (SLOTS, length, row_count, padded_rows)
    q_shift = lax.dynamic_slice_in_dim(q_bias, head_start, head_width, 0)
    v_shift = lax.dynamic_slice_in_dim(v_bias, head_start, head_width, 0)
    up_shift = lax.dynamic_slice_in_dim(fc1_bias, unit_start, unit_width, 0)
    gain_one, shift_one, o_shift, gain_two, shift_two, down_shift = tuple(
        (
            lax.dynamic_slice_in_dim(vector, feature_start, part_width, 0)
            for vector in (ln1_gain, ln1_bias, o_bias, ln2_gain, ln2_bias, fc2_bias)
        )
    )
    vectors = (
        gain_one,
        shift_one,
        q_shift,
        v_shift,
        o_shift,
        gain_two,
        shift_two,
        up_shift,
        down_shift,
    )
    q_low = q_weight.astype(jnp.bfloat16)
    k_low = k_weight.astype(jnp.bfloat16)
    v_low = v_weight.astype(jnp.bfloat16)
    o_low = o_weight.astype(jnp.bfloat16)
    up_low = fc1_weight.astype(jnp.bfloat16)
    down_low = fc2_weight.astype(jnp.bfloat16)
    slot_mask = live.astype(jnp.float32)
    outputs = []
    input_grads = []
    matrix_sums = None
    vector_sums = None
    for micro_batch in range(MB):
        slot_start = micro_batch * SLOTS
        batch_tokens = images[slot_start : slot_start + SLOTS].reshape(row_count, full_width)
        batch_cot = cotangent[slot_start : slot_start + SLOTS].reshape(row_count, full_width)
        mask_rows = jnp.broadcast_to(
            slot_mask[slot_start : slot_start + SLOTS, None], (SLOTS, length)
        ).reshape(-1, 1)
        stream = lax.dynamic_slice_in_dim(batch_tokens, feature_start, part_width, 1).astype(
            jnp.float32
        )
        cot_stream = lax.dynamic_slice_in_dim(batch_cot, feature_start, part_width, 1)
        forward_weights = (
            lax.all_gather(q_low, "fsdp", axis=0, tiled=True),
            lax.all_gather(k_low, "fsdp", axis=0, tiled=True),
            lax.all_gather(v_low, "fsdp", axis=0, tiled=True),
            lax.all_gather(o_low, "fsdp", axis=1, tiled=True),
            lax.all_gather(up_low, "fsdp", axis=0, tiled=True),
            lax.all_gather(down_low, "fsdp", axis=1, tiled=True),
        )
        output, kept_state = forward_pass(stream, mask_rows, forward_weights, vectors, sizes_info)
        backward_weights = (
            lax.all_gather(q_low, "fsdp", axis=0, tiled=True),
            lax.all_gather(k_low, "fsdp", axis=0, tiled=True),
            lax.all_gather(v_low, "fsdp", axis=0, tiled=True),
            lax.all_gather(o_low, "fsdp", axis=1, tiled=True),
            lax.all_gather(up_low, "fsdp", axis=0, tiled=True),
            lax.all_gather(down_low, "fsdp", axis=1, tiled=True),
        )
        grad_in, matrices, vector_grads = backward_pass(
            cot_stream, mask_rows, backward_weights, vectors, kept_state, sizes_info
        )
        whole_out, whole_grad = (
            lax.all_gather(output, "tensor", axis=1, tiled=True),
            lax.all_gather(grad_in, "tensor", axis=1, tiled=True),
        )
        outputs.append(whole_out.reshape(SLOTS, length, full_width))
        input_grads.append(whole_grad.reshape(SLOTS, length, full_width))
        vector_sums = (
            vector_grads
            if vector_sums is None
            else jax.tree.map(jnp.add, vector_sums, vector_grads)
        )
        matrix_sums = (
            matrices if matrix_sums is None else jax.tree.map(jnp.add, matrix_sums, matrices)
        )
    total_wq, total_wk, total_wv, total_wo, total_up, total_down = matrix_sums
    shard_wq, shard_wk, shard_wv, shard_wo, shard_up, shard_down = (
        lax.psum_scatter(
            total_wq.astype(jnp.bfloat16), "fsdp", scatter_dimension=0, tiled=True
        ).astype(jnp.float32),
        lax.psum_scatter(
            total_wk.astype(jnp.bfloat16), "fsdp", scatter_dimension=0, tiled=True
        ).astype(jnp.float32),
        lax.psum_scatter(
            total_wv.astype(jnp.bfloat16), "fsdp", scatter_dimension=0, tiled=True
        ).astype(jnp.float32),
        lax.psum_scatter(
            total_wo.astype(jnp.bfloat16), "fsdp", scatter_dimension=1, tiled=True
        ).astype(jnp.float32),
        lax.psum_scatter(
            total_up.astype(jnp.bfloat16), "fsdp", scatter_dimension=0, tiled=True
        ).astype(jnp.float32),
        lax.psum_scatter(
            total_down.astype(jnp.bfloat16), "fsdp", scatter_dimension=1, tiled=True
        ).astype(jnp.float32),
    )
    final_wq, final_wk, final_wv, final_wo, final_up, final_down = (
        lax.psum(shard_wq.astype(jnp.bfloat16), "replica").astype(jnp.float32),
        lax.psum(shard_wk.astype(jnp.bfloat16), "replica").astype(jnp.float32),
        lax.psum(shard_wv.astype(jnp.bfloat16), "replica").astype(jnp.float32),
        lax.psum(shard_wo.astype(jnp.bfloat16), "replica").astype(jnp.float32),
        lax.psum(shard_up.astype(jnp.bfloat16), "replica").astype(jnp.float32),
        lax.psum(shard_down.astype(jnp.bfloat16), "replica").astype(jnp.float32),
    )
    (
        sum_gain_one,
        sum_shift_one,
        sum_q_shift,
        sum_v_shift,
        sum_o_shift,
        sum_gain_two,
        sum_shift_two,
        sum_up_shift,
        sum_down_shift,
    ) = vector_sums
    summed = lax.psum(
        (
            sum_gain_one,
            sum_shift_one,
            sum_q_shift,
            sum_v_shift,
            sum_o_shift,
            sum_gain_two,
            sum_shift_two,
            sum_up_shift,
            sum_down_shift,
        ),
        ("replica", "fsdp"),
    )
    (
        grad_gain_one,
        grad_shift_one,
        grad_q_shift,
        grad_v_shift,
        grad_o_shift,
        grad_gain_two,
        grad_shift_two,
        grad_up_shift,
        grad_down_shift,
    ) = summed
    return (
        jnp.concatenate(outputs, axis=0),
        jnp.concatenate(input_grads, axis=0),
        grad_gain_one,
        grad_shift_one,
        final_wq,
        grad_q_shift,
        final_wk,
        final_wv,
        grad_v_shift,
        final_wo,
        grad_o_shift,
        grad_gain_two,
        grad_shift_two,
        final_up,
        grad_up_shift,
        final_down,
        grad_down_shift,
    )


WINDOW = 256
LANES = 128
SHIFT = 64
VMEM = 60 * 2**20
GELU = 0.7978845608
EVERY = ("tensor", "fsdp", "replica")


def ceil_to(value, step):
    return -(-value // step) * step


def call(kernel, name, grid, scalars, ins, outs, flops=0, scratch=(), aliases=None):
    total = sum(array.size * array.dtype.itemsize for array, _ in ins)
    return pl.pallas_call(
        kernel,
        grid_spec=pltpu.PrefetchScalarGridSpec(
            num_scalar_prefetch=1,
            grid=grid,
            in_specs=[spec for _, spec in ins],
            out_specs=[spec for _, _, spec in outs],
            scratch_shapes=list(scratch),
        ),
        out_shape=[jax.ShapeDtypeStruct(shape, dtype) for shape, dtype, _ in outs],
        input_output_aliases=aliases or {},
        compiler_params=pltpu.CompilerParams(vmem_limit_bytes=VMEM),
        cost_estimate=pl.CostEstimate(flops=flops, bytes_accessed=total, transcendentals=0),
        name=name,
    )(scalars, *(array for array, _ in ins))


def fixed(shape, index):
    return pl.BlockSpec(shape, index, pipeline_mode=pl.Buffered(1))


def head_window(offset, base, rows):
    start = (offset + base) // LANES * LANES
    lane = lax.broadcasted_iota(jnp.int32, (rows, WINDOW), 1) + start
    inside = (lane >= offset + base) & (lane < offset + base + HEAD)
    return pl.ds(pl.multiple_of(start, LANES), WINDOW), inside


def attention(qvk, length, rows, width, group):
    heads = width // HEAD
    count = qvk.shape[0] // rows
    steps = heads // group
    out_width = ceil_to(width + SHIFT, WINDOW)

    def kernel(none_ref, qvk_ref, mixed_ref, probs_ref):
        @pl.when(pl.program_id(1) == 0)
        def _():
            mixed_ref[...] = jnp.zeros_like(mixed_ref)

        real = lax.broadcasted_iota(jnp.int32, (rows, rows), 1) < length

        def head(item):
            return (pl.program_id(1) * group + item) * HEAD

        def scores_of(item):
            at_q, _ = head_window(head(item), 0, rows)
            at_k, in_k = head_window(head(item), 2 * width, rows)
            key_rows = jnp.where(in_k, qvk_ref[:, at_k], 0)
            return jnp.where(real, matmul_nt(qvk_ref[:, at_q], key_rows), -1e30)

        following = scores_of(0)
        for item in range(group):
            scores = following
            if item + 1 < group:
                following = scores_of(item + 1)
            at_v, in_v = head_window(head(item), width, rows)
            at_o, in_o = head_window(head(item), SHIFT, rows)
            value_rows = jnp.where(in_v, qvk_ref[:, at_v], 0)
            powers = jnp.exp(scores - jnp.max(scores, axis=1, keepdims=True))
            total = jnp.sum(powers, axis=1, keepdims=True)
            probs = (powers * (1.0 / total)).astype(jnp.bfloat16)
            probs_ref[item] = probs
            mixed = matmul(probs, value_rows).astype(jnp.bfloat16)
            mixed_ref[:, at_o] = jnp.where(in_o, mixed, mixed_ref[:, at_o])

    return call(
        kernel,
        "attention",
        (count, steps),
        jnp.zeros((1,), jnp.int32),
        [(qvk, pl.BlockSpec((rows, qvk.shape[1]), lambda i, g, s: (i, 0)))],
        [
            ((count * rows, out_width), jnp.bfloat16, pl.BlockSpec((rows, out_width), lambda i, g, s: (i, 0))),
            (
                (count * heads, rows, rows),
                jnp.bfloat16,
                pl.BlockSpec((group, rows, rows), lambda i, g, s: (i * steps + g, 0, 0)),
            ),
        ],
        flops=4 * count * heads * rows * rows * WINDOW,
    )


def attention_back(qvk, mixed, grad, probs, images, kept, rows, width, group):
    heads = width // HEAD
    steps = heads // group
    at = images.start
    count = len(images)

    def kernel(none_ref, qvk_ref, mixed_ref, grad_ref, probs_ref, *refs):
        out_ref, sums_ref = refs[-2:]

        @pl.when(pl.program_id(1) == 0)
        def _():
            out_ref[...] = jnp.zeros_like(out_ref)

        for item in range(group):
            offset = (pl.program_id(1) * group + item) * HEAD
            at_q, in_q = head_window(offset, 0, rows)
            at_v, in_v = head_window(offset, width, rows)
            at_k, in_k = head_window(offset, 2 * width, rows)
            at_o, in_o = head_window(offset, SHIFT, rows)
            grad = jnp.where(in_o, grad_ref[:, at_o], 0)
            query_rows = jnp.where(in_q, qvk_ref[:, at_q], 0)
            key_rows = jnp.where(in_k, qvk_ref[:, at_k], 0)
            probs = probs_ref[item]
            row_dot = jnp.sum(
                grad.astype(jnp.float32) * mixed_ref[:, at_o].astype(jnp.float32), axis=1, keepdims=True
            )
            prob_grad = matmul_nt(grad, qvk_ref[:, at_v])
            score_grad = (probs.astype(jnp.float32) * (prob_grad - row_dot)).astype(jnp.bfloat16)
            value_grad = matmul_tn(probs, grad).astype(jnp.bfloat16)
            query_grad = (matmul(score_grad, key_rows) * HEAD ** (-0.5)).astype(jnp.bfloat16)
            key_grad = matmul_tn(score_grad, query_rows).astype(jnp.bfloat16)
            out_ref[:, at_q] = jnp.where(in_q, query_grad, out_ref[:, at_q])
            out_ref[:, at_v] = jnp.where(in_v, value_grad, out_ref[:, at_v])
            out_ref[:, at_k] = jnp.where(in_k, key_grad, out_ref[:, at_k])

        @pl.when(pl.program_id(1) == steps - 1)
        def _():
            total = jnp.sum(out_ref[...].astype(jnp.float32), axis=0, keepdims=True)
            sums_ref[0] = jnp.broadcast_to(total, sums_ref.shape[1:])

    ins = [
        (qvk, pl.BlockSpec((rows, qvk.shape[1]), lambda i, g, s: (at + i, 0))),
        (mixed, pl.BlockSpec((rows, mixed.shape[1]), lambda i, g, s: (at + i, 0))),
        (grad, pl.BlockSpec((rows, mixed.shape[1]), lambda i, g, s: (at + i, 0))),
        (probs, pl.BlockSpec((group, rows, rows), lambda i, g, s: ((at + i) * steps + g, 0, 0))),
    ]
    if kept is not None:
        ins.append((kept, pl.BlockSpec(memory_space=pl.ANY)))
    grads, sums = call(
        kernel,
        "attention_back",
        (count, steps),
        jnp.zeros((1,), jnp.int32),
        ins,
        [
            (qvk.shape, jnp.bfloat16, pl.BlockSpec((rows, qvk.shape[1]), lambda i, g, s: (at + i, 0))),
            ((count, 8, qvk.shape[1]), jnp.float32, pl.BlockSpec((1, 8, qvk.shape[1]), lambda i, g, s: (i, 0, 0))),
        ],
        aliases=None if kept is None else {5: 0},
        flops=8 * count * heads * rows * rows * WINDOW,
    )
    return grads, jnp.sum(sums[:, 0], axis=0)


def place(pieces, slots, total):
    def kernel(slots_ref, *refs):
        at = 0
        for ref in refs[:-1]:
            for block in range(ref.shape[0]):
                refs[-1][pl.ds(slots_ref[at], 1)] = ref[block : block + 1]
                at += 1

    def whole(shape):
        return fixed(shape, lambda i, s: (0, 0, 0))

    shape = (total, *pieces[0].shape[1:])
    return call(
        kernel,
        "place",
        (1,),
        jnp.stack([slot for group in slots for slot in group]).astype(jnp.int32),
        [(piece, whole(piece.shape)) for piece in pieces],
        [(shape, pieces[0].dtype, whole(shape))],
    )[0]


def outer_sum(left, right, ranks, step, total=None, kept=None, at=None, scalars=None):
    rows, lines = left.shape
    columns = right.shape[1] // ranks
    steps = columns // step
    held = ranks * lines if kept is None else kept.shape[0]

    def kernel(scalars_ref, left_ref, right_ref, *refs):
        refs[-1][...] = matmul_tn(left_ref[...], right_ref[...]).astype(refs[-1].dtype)

    def place_of(t, j, s):
        return (t, j) if kept is None else (s[at[0]], at[1])

    return call(
        kernel,
        "outer_sum",
        (ranks, steps),
        jnp.zeros((1,), jnp.int32) if scalars is None else scalars,
        [
            (left, fixed((rows, lines), lambda t, j, s: (0, 0))),
            (right, pl.BlockSpec((rows, step), lambda t, j, s: (0, t * steps + j))),
        ]
        + ([] if kept is None else [(kept, pl.BlockSpec(memory_space=pl.ANY))]),
        [((held, total or columns), jnp.bfloat16, pl.BlockSpec((lines, step), place_of))],
        flops=2 * rows * lines * columns * ranks,
        aliases=None if kept is None else {3: 0},
    )[0]


def tie(*values):
    return lax.optimization_barrier(values)


def swap(array, axis, bits):
    size = lax.axis_size(axis)
    return lax.ppermute(array, axis, [(rank, rank ^ bits) for rank in range(size)])


def turn(array, axis, steps):
    size = lax.axis_size(axis)
    return lax.ppermute(array, axis, [(rank, (rank + steps) % size) for rank in range(size)])


def replica_bits():
    bit = lax.axis_size("replica") // 2
    bits = []
    while bit:
        bits.append(bit)
        bit //= 2
    return bits


def swap_found(found, bit):
    return {**found, **{bits ^ bit: swap(held, "replica", bit) for bits, held in found.items()}}


def among_replicas(piece):
    found = {0: piece}
    for bit in replica_bits():
        found = swap_found(found, bit)
    return found


def from_lines(shard):
    copies = lax.axis_size("replica")
    blocks = shard.reshape(copies, -1, shard.shape[1])
    mine = lax.dynamic_slice_in_dim(blocks, lax.axis_index("replica"), 1, 0)
    return [mine] + [turn(mine, "fsdp", step) for step in range(1, lax.axis_size("fsdp"))]


def slots_of(found, skip):
    copies, lines = lax.axis_size("replica"), lax.axis_size("fsdp")
    copy, line = lax.axis_index("replica"), lax.axis_index("fsdp")
    starts = [(line - step) % lines * copies for step in range(skip, lines)]
    return [[start + (copy ^ bits) for start in starts] for bits in found]


def gather_own(shard, parts):
    copies, lines, line = lax.axis_size("replica"), lax.axis_size("fsdp"), lax.axis_index("fsdp")
    blocks = shard.reshape(copies, -1, shard.shape[1])
    pieces, slots = [blocks], [[line * copies + at for at in range(copies)]]
    if lines > 1:
        found = among_replicas(jnp.concatenate(parts[1:], axis=0))
        pieces += list(found.values())
        slots += slots_of(found, 1)
    return place(pieces, slots, lines * copies).reshape(-1, shard.shape[1])


def gather_far(parts, rank):
    found = {0: swap(jnp.concatenate(parts, axis=0), "tensor", rank)}
    for bit in replica_bits()[:-1]:
        found = swap_found(found, bit)
    return found


def finish_far(found):
    for bit in replica_bits()[-1:]:
        found = swap_found(found, bit)
    total = lax.axis_size("replica") * lax.axis_size("fsdp")
    whole = place(list(found.values()), slots_of(found, 0), total)
    return whole.reshape(-1, whole.shape[2])


def gather_whole(shard):
    share = shard.shape[0] // lax.axis_size("replica")
    part = lax.dynamic_slice_in_dim(shard, lax.axis_index("replica") * share, share, 0)
    return lax.all_gather(part, EVERY, axis=0, tiled=True)


def add_low(first_term, *terms):
    total = first_term.astype(jnp.float32)
    for term in terms:
        total = total + term.astype(jnp.float32)
    return total.astype(jnp.bfloat16)


def by_lines(term):
    bits = len(replica_bits())
    return term.reshape(lax.axis_size("fsdp"), *(2 for _ in range(bits)), -1, term.shape[1])


def halve(held, bit):
    side = lax.axis_index("replica") // bit % 2
    axis = held.ndim - 3
    keep = lax.dynamic_index_in_dim(held, side, axis, keepdims=False)
    send = lax.dynamic_index_in_dim(held, 1 - side, axis, keepdims=False)
    return add_low(keep, swap(send, "replica", bit))


def sum_lines(held):
    lines, line = lax.axis_size("fsdp"), lax.axis_index("fsdp")
    terms = [lax.dynamic_index_in_dim(held, line, 0, keepdims=True)]
    for step in range(1, lines):
        send = lax.dynamic_index_in_dim(held, (line + step) % lines, 0, keepdims=True)
        terms.append(turn(send, "fsdp", step))
    return add_low(*terms)


def place_found(found):
    copy = lax.axis_index("replica")
    whole = place(list(found.values()), [[copy ^ bits] for bits in found], len(found))
    return whole.reshape(-1, whole.shape[2])


def sum_over(vector, axes):
    size = lax.axis_size(axes)
    terms = [vector] + [
        lax.ppermute(vector, axes, [(rank, rank ^ bits) for rank in range(size)]) for bits in range(1, size)
    ]
    while len(terms) > 1:
        terms = [left + right for left, right in zip(terms[::2], terms[1::2])]
    return terms[0]


def norm_parts(values):
    center = jnp.mean(values, axis=1, keepdims=True)
    spread = jnp.mean(values * values, axis=1, keepdims=True) - center * center
    scale_inv = lax.rsqrt(spread + EPSILON)
    return (values - center) * scale_inv, scale_inv


def norm_backward(grad, normed, scale_inv, gain_vec):
    scaled = grad * gain_vec
    mean_one = jnp.mean(scaled, axis=1, keepdims=True)
    mean_two = jnp.mean(scaled * normed, axis=1, keepdims=True)
    return scale_inv * (scaled - mean_one - normed * mean_two)


def image_body(
    images,
    live,
    cotangent,
    ln1_gain,
    ln1_bias,
    q_weight,
    q_bias,
    k_weight,
    v_weight,
    v_bias,
    o_weight,
    o_bias,
    ln2_gain,
    ln2_bias,
    fc1_weight,
    fc1_bias,
    fc2_weight,
    fc2_bias,
):
    low, full = jnp.bfloat16, jnp.float32
    tensor_count = lax.axis_size("tensor")
    tensor_rank = lax.axis_index("tensor")
    slots, length, wide = images.shape
    count = slots // tensor_count
    rows = ceil_to(length, 32)
    half = rows // 2
    width = q_weight.shape[1]
    units = fc1_weight.shape[1]
    qvk_width = ceil_to(3 * width, WINDOW)
    o_width = ceil_to(width + SHIFT, WINDOW)
    unit_width = ceil_to(units, WINDOW)
    unit_width = ceil_to(unit_width, o_width)
    ranks = range(tensor_count)
    all_rows = count * rows
    heads = width // HEAD
    group = next(size for size in (8, 4, 2, 1) if heads % size == 0)
    blocks = all_rows // half
    scalars = jnp.concatenate(
        [
            jnp.stack([tensor_rank * count] + [tensor_rank ^ rank for rank in ranks]).astype(jnp.int32),
            lax.dynamic_slice_in_dim(live, tensor_rank * count, count, 0),
        ]
    )
    live_at = 1 + tensor_count

    def columns(parts, ahead, total):
        body_part = jnp.concatenate(parts, axis=1)
        return jnp.pad(body_part, ((0, 0), (ahead, total - ahead - body_part.shape[1])))

    def row(vector):
        return vector.reshape(1, -1)

    def slots_spec(first=0):
        return pl.BlockSpec((1, half, wide), lambda i, s: (s[0] + first + i // 2, i % 2, 0))

    def rows_spec(size, first=0):
        return pl.BlockSpec((half, size), lambda i, s: (2 * first + i, 0))

    def vector_spec():
        return pl.BlockSpec((1, wide), lambda i, s: (0, 0))

    def sums_spec():
        return pl.BlockSpec((8, wide), lambda i, s: (0, 0))

    def real_rows(values):
        at = lax.broadcasted_iota(jnp.int32, (half, 1), 0) + pl.program_id(0) % 2 * half
        return jnp.where(at < length, values.astype(full), 0.0)

    def live_slot(scalars_ref, first=0):
        return scalars_ref[live_at + first + pl.program_id(0) // 2].astype(full)

    def add_sums(sums_ref, *terms):
        @pl.when(pl.program_id(0) == 0)
        def _():
            sums_ref[...] = jnp.zeros_like(sums_ref)

        for at, term in enumerate(terms):
            sums_ref[at : at + 1] += jnp.sum(term, axis=0, keepdims=True)

    def product(part_refs, weight_refs):
        total = matmul_nt(part_refs[0][...], weight_refs[0][...])
        for part_ref, weight_ref in zip(part_refs[1:], weight_refs[1:]):
            total = total + matmul_nt(part_ref[...], weight_ref[...])
        return total

    qvk_shard = columns([w.astype(low) for w in (q_weight, v_weight, k_weight)], 0, qvk_width)
    parts = from_lines(qvk_shard)

    def first_kernel(scalars_ref, images_ref, cot_ref, gain_ref, shift_ref, first_ref, grad_ref, sums_ref):
        normed, _ = norm_parts(real_rows(images_ref[0]))
        first_ref[...] = (normed * gain_ref[...] + shift_ref[...]).astype(low)
        grad = real_rows(cot_ref[0]) * live_slot(scalars_ref)
        grad_ref[...] = grad.astype(low)
        add_sums(sums_ref, grad)

    first, out_grad, first_sums = call(
        first_kernel,
        "first_norm",
        (blocks,),
        scalars,
        [(images, slots_spec()), (cotangent, slots_spec()), (row(ln1_gain), vector_spec()), (row(ln1_bias), vector_spec())],
        [
            ((all_rows, wide), low, rows_spec(wide)),
            ((all_rows, wide), low, rows_spec(wide)),
            ((8, wide), full, sums_spec()),
        ],
    )

    parts, first, out_grad = tie(parts, first, out_grad)
    up_o_shard = jnp.concatenate(
        [
            columns([fc1_weight.astype(low)], 0, unit_width),
            columns([o_weight.astype(low).T], SHIFT, o_width),
        ],
        axis=1,
    )
    down_shard = columns([fc2_weight.astype(low).T], 0, unit_width)
    up_o_shard, down_shard, parts = tie(up_o_shard, down_shard, parts)
    up_o_whole = gather_whole(up_o_shard)
    down_whole = gather_whole(down_shard)
    qvk_weights = [gather_own(qvk_shard, parts)]
    far_parts = [gather_far(parts, rank) for rank in ranks[1:]]

    def of_rank(vector, rank, size):
        return lax.dynamic_slice_in_dim(vector, (tensor_rank ^ rank) * size, size, 0)

    scale_row = jnp.where(jnp.arange(qvk_width) < width, HEAD ** (-0.5), 1.0)
    qvk, mixed, probs = [], [], []
    for rank in ranks:
        shift_row = jnp.pad(
            jnp.concatenate([of_rank(q_bias, rank, width), of_rank(v_bias, rank, width)]),
            (0, qvk_width - 2 * width),
        )
        qvk.append(((matmul(first, qvk_weights[rank]) + shift_row) * scale_row).astype(low))
        mixed_part, probs_part = attention(qvk[rank], length, rows, width, group)
        if rank == 0:
            mixed_part, first, far_parts = tie(mixed_part, first, far_parts)
            qvk_weights += [finish_far(found) for found in far_parts]
        mixed.append(mixed_part)
        probs.append(probs_part)

    def o_spec(rank):
        return fixed((wide, o_width), lambda i, s: (s[1 + rank], unit_width // o_width))

    def middle_kernel(scalars_ref, *refs):
        images_ref, bias_ref, gain_ref, shift_ref, middle_ref, second_ref = refs[2 * tensor_count :]
        total = product(refs[:tensor_count], refs[tensor_count : 2 * tensor_count])
        middle = real_rows(images_ref[0]) + (total + bias_ref[...])
        middle_ref[...] = middle
        normed, _ = norm_parts(middle)
        second_ref[...] = (normed * gain_ref[...] + shift_ref[...]).astype(low)

    middle, second = call(
        middle_kernel,
        "middle_norm",
        (blocks,),
        scalars,
        [(part, rows_spec(o_width)) for part in mixed]
        + [(up_o_whole, o_spec(rank)) for rank in ranks]
        + [
            (images, slots_spec()),
            (row(o_bias), vector_spec()),
            (row(ln2_gain), vector_spec()),
            (row(ln2_bias), vector_spec()),
        ],
        [((all_rows, wide), full, rows_spec(wide)), ((all_rows, wide), low, rows_spec(wide))],
        flops=2 * all_rows * wide * o_width * tensor_count,
    )

    chunk = o_width

    def unit_rows():
        return pl.BlockSpec((half, unit_width), lambda t, i, s: (i, t))

    def unit_weights():
        return pl.BlockSpec((wide, unit_width), lambda t, i, s: (t, 0))

    def hidden_kernel(scalars_ref, second_ref, weight_ref, shift_ref, hidden_ref, slope_ref):
        for start in range(0, unit_width, chunk):
            at = slice(start, start + chunk)
            upper = matmul(second_ref[...], weight_ref[:, at]) + shift_ref[:, at]
            square = upper * upper
            share = 0.5 + 0.5 * jnp.tanh(upper * (GELU + GELU * 0.044715 * square))
            hidden = upper * share
            slope = share + (hidden - hidden * share) * (2 * GELU + 6 * GELU * 0.044715 * square)
            hidden_ref[:, at] = hidden.astype(low)
            slope_ref[:, at] = slope.astype(low)

    unit_shift = jnp.pad(
        fc1_bias.reshape(tensor_count, units), ((0, 0), (0, unit_width - units))
    ).reshape(1, -1)
    hidden, slopes = call(
        hidden_kernel,
        "hidden",
        (tensor_count, blocks),
        scalars,
        [
            (second, pl.BlockSpec((half, wide), lambda t, i, s: (i, 0))),
            (up_o_whole, unit_weights()),
            (unit_shift, pl.BlockSpec((1, unit_width), lambda t, i, s: (0, t))),
        ],
        [((all_rows, tensor_count * unit_width), low, unit_rows())] * 2,
        flops=2 * all_rows * wide * unit_width * tensor_count,
    )
    down_terms = outer_sum(out_grad, hidden, tensor_count, chunk)
    down_terms, hidden = tie(down_terms, hidden)
    down_share = lax.psum_scatter(down_terms, EVERY, scatter_dimension=0, tiled=True)

    def weight_spec(rank):
        return fixed((wide, unit_width), lambda i, s: (rank, 0))

    def unit_spec(rank):
        return pl.BlockSpec((half, unit_width), lambda i, s: (i, rank))

    def output_kernel(scalars_ref, *refs):
        middle_ref, bias_ref, output_ref, whole_ref = refs[2 * tensor_count :]
        total = product(refs[:tensor_count], refs[tensor_count : 2 * tensor_count])
        result = middle_ref[...] + (total + bias_ref[...])
        output_ref[0] = (result * live_slot(scalars_ref)).astype(low)
        whole_ref[0] = output_ref[0]

    output, out_whole = call(
        output_kernel,
        "output",
        (blocks,),
        scalars,
        [(hidden, unit_spec(rank)) for rank in ranks]
        + [(down_whole, weight_spec(rank)) for rank in ranks]
        + [(middle, rows_spec(wide)), (row(fc2_bias), vector_spec())],
        [
            ((count, length, wide), low, pl.BlockSpec((1, half, wide), lambda i, s: (i // 2, i % 2, 0))),
            ((slots, length, wide), low, slots_spec()),
        ],
        flops=2 * all_rows * wide * unit_width * tensor_count,
    )

    def trade(part):
        return [swap(part, "tensor", rank) for rank in ranks[1:]]

    def trade_halves(part):
        return [trade(piece) for piece in part]

    def lay_halves(whole, parts, first):
        for rank, *pieces in zip(ranks[1:], *parts):
            for at, piece in enumerate(pieces):
                start = ((tensor_rank ^ rank) * count + first, at * half, 0)
                whole = lax.dynamic_update_slice(whole, piece, start)
        return whole

    def lay(whole, parts, first):
        for rank, part in zip(ranks[1:], parts):
            whole = lax.dynamic_update_slice_in_dim(whole, part, (tensor_rank ^ rank) * count + first, 0)
        return whole

    output, out_grad = tie(output, out_grad)
    out_parts = trade(output)

    def hidden_back_kernel(scalars_ref, grad_ref, weight_ref, slope_ref, upper_ref, sums_ref):
        @pl.when(pl.program_id(1) == 0)
        def _():
            sums_ref[...] = jnp.zeros_like(sums_ref)

        for start in range(0, unit_width, chunk):
            at = slice(start, start + chunk)
            upper = matmul(grad_ref[...], weight_ref[:, at]) * slope_ref[:, at].astype(full)
            rounded = upper.astype(low)
            upper_ref[:, at] = rounded
            sums_ref[0:1, at] += jnp.sum(rounded.astype(full), axis=0, keepdims=True)

    upper_grads, upper_sums = call(
        hidden_back_kernel,
        "hidden_back",
        (tensor_count, blocks),
        scalars,
        [
            (out_grad, pl.BlockSpec((half, wide), lambda t, i, s: (i, 0))),
            (down_whole, unit_weights()),
            (slopes, unit_rows()),
        ],
        [
            ((all_rows, tensor_count * unit_width), low, unit_rows()),
            ((8, tensor_count * unit_width), full, pl.BlockSpec((8, unit_width), lambda t, i, s: (0, t))),
        ],
        flops=2 * all_rows * wide * unit_width * tensor_count,
    )
    up_terms = outer_sum(second, upper_grads, tensor_count, o_width, unit_width + o_width)
    up_terms, upper_grads = tie(up_terms, upper_grads)

    def middle_back_kernel(scalars_ref, *refs):
        middle_ref, grad_ref, gain_ref, *o_refs = refs[2 * tensor_count : 3 * tensor_count + 3]
        middle_grad_ref, low_ref, sums_ref, *mixed_grad_refs = refs[3 * tensor_count + 3 :]
        total = product(refs[:tensor_count], refs[tensor_count : 2 * tensor_count])
        normed, scale_inv = norm_parts(middle_ref[...])
        middle_grad = grad_ref[...].astype(full) + norm_backward(total, normed, scale_inv, gain_ref[...])
        middle_grad_ref[...] = middle_grad
        rounded = middle_grad.astype(low)
        low_ref[...] = rounded
        for o_ref, mixed_grad_ref in zip(o_refs, mixed_grad_refs):
            mixed_grad_ref[...] = matmul(rounded, o_ref[...]).astype(low)
        add_sums(sums_ref, total * normed, total, rounded.astype(full))

    middle_grad, middle_low, second_sums, *mixed_grads = call(
        middle_back_kernel,
        "middle_back",
        (blocks,),
        scalars,
        [(upper_grads, unit_spec(rank)) for rank in ranks]
        + [(up_o_whole, weight_spec(rank)) for rank in ranks]
        + [(middle, rows_spec(wide)), (out_grad, rows_spec(wide)), (row(ln2_gain), vector_spec())]
        + [(up_o_whole, o_spec(rank)) for rank in ranks],
        [
            ((all_rows, wide), full, rows_spec(wide)),
            ((all_rows, wide), low, rows_spec(wide)),
            ((8, wide), full, sums_spec()),
        ]
        + [((all_rows, o_width), low, rows_spec(o_width)) for rank in ranks],
        flops=2 * all_rows * wide * (unit_width + o_width) * tensor_count,
    )

    for rank in ranks:
        up_terms = outer_sum(
            middle_low,
            mixed[rank],
            1,
            o_width,
            unit_width + o_width,
            up_terms,
            (1 + rank, unit_width // o_width),
            scalars,
        )
    up_terms, mixed_grads[-1], out_parts = tie(up_terms, mixed_grads[-1], out_parts)
    up_share = lax.psum_scatter(up_terms, EVERY, scatter_dimension=0, tiled=True)
    bits = replica_bits()[::-1]

    def back(rank, which, kept):
        return attention_back(
            qvk[rank], mixed[rank], mixed_grads[rank], probs[rank], which, kept, rows, width, group
        )

    def first_back_kernel(scalars_ref, *refs):
        images_ref, grad_ref, gain_ref = refs[2 * tensor_count : 2 * tensor_count + 3]
        upper_ref, lower_ref, whole_ref, sums_ref = refs[-4:]
        total = product(refs[:tensor_count], refs[tensor_count : 2 * tensor_count])
        normed, scale_inv = norm_parts(real_rows(images_ref[0]))
        grad = grad_ref[...] + norm_backward(total, normed, scale_inv, gain_ref[...])
        whole_ref[0] = grad.astype(low)

        @pl.when(pl.program_id(0) == 0)
        def _():
            upper_ref[...] = whole_ref[...]

        @pl.when(pl.program_id(0) == 1)
        def _():
            lower_ref[...] = whole_ref[:, : length - half]

        add_sums(sums_ref, total * normed, total)

    qvk_grads, qvk_sums = [None] * tensor_count, [0.0] * tensor_count
    input_whole = None
    third_sums = 0.0
    in_parts = []

    def attend(rank, which):
        qvk_grads[rank], sums = back(rank, which, qvk_grads[rank])
        qvk_sums[rank] = qvk_sums[rank] + sums

    def first_back(slot, whole):
        ahead = [] if whole is None else [(whole, pl.BlockSpec(memory_space=pl.ANY))]
        upper, lower, whole, sums = call(
            first_back_kernel,
            "first_back",
            (2,),
            scalars,
            [(grads, rows_spec(qvk_width, slot)) for grads in qvk_grads]
            + [(weight, fixed((wide, qvk_width), lambda i, s: (0, 0))) for weight in qvk_weights]
            + [(images, slots_spec(slot)), (middle_grad, rows_spec(wide, slot)), (row(ln1_gain), vector_spec())]
            + ahead,
            [
                ((1, half, wide), low, pl.BlockSpec((1, half, wide), lambda i, s: (0, 0, 0))),
                ((1, length - half, wide), low, pl.BlockSpec((1, length - half, wide), lambda i, s: (0, 0, 0))),
                ((slots, length, wide), low, slots_spec(slot)),
                ((8, wide), full, sums_spec()),
            ],
            aliases={2 * tensor_count + 4: 2} if ahead else None,
            flops=2 * rows * wide * qvk_width * tensor_count,
        )
        return (upper, lower), whole, sums

    last = count - 1

    def halve_all(terms, which):
        for bit in which:
            terms = [halve(term, bit) for term in terms]
        return terms

    def join_on(found, which):
        for bit in which:
            found = swap_found(found, bit)
        return found

    far_bits, far_bit = replica_bits()[:-1], replica_bits()[-1:]

    down_found = join_on({0: down_share[None]}, far_bits)
    for rank in ranks[1:]:
        attend(rank, range(count))
    qvk_grads[1:], mixed_grads[0], down_found, first = tie(qvk_grads[1:], mixed_grads[0], down_found, first)
    far = [by_lines(outer_sum(first, grads, 1, qvk_width // 2)) for grads in qvk_grads[1:]]
    down_grads = place_found(join_on(down_found, far_bit))
    far, mixed_grads[0], down_grads = tie(far, mixed_grads[0], down_grads)
    far_done = 0
    for slot in range(last):
        if slot > 0:
            in_parts.append(trade_halves(input_grad))
        attend(0, range(slot, slot + 1))
        if slot == 0:
            far = halve_all(far, bits[:1])
            far, qvk_grads[0] = tie(far, qvk_grads[0])
        elif far_done == 1:
            far = halve_all(far, bits[1:])
        far_done += 1
        input_grad, input_whole, sums = first_back(slot, input_whole)
        third_sums = third_sums + sums
        far, input_grad, mixed_grads[0] = tie(far, input_grad, mixed_grads[0])
        if slot > 0:
            in_parts[-1][0], input_grad, mixed_grads[0] = tie(in_parts[-1][0], input_grad, mixed_grads[0])
    if last > 0:
        in_parts.append(trade_halves(input_grad))
    attend(0, range(last, count))
    near = by_lines(outer_sum(first, qvk_grads[0], 1, qvk_width // 2))
    if far_done < 2:
        far = halve_all(far, bits[far_done:])
    near, far, in_parts[:-1], qvk_grads[0] = tie(near, far, in_parts[:-1], qvk_grads[0])
    if last > 0:
        in_parts[-1][0], near, qvk_grads[0] = tie(in_parts[-1][0], near, qvk_grads[0])
    near = halve_all([near], bits[:1])
    near, qvk_grads[0], far, up_share = tie(near, qvk_grads[0], far, up_share)
    input_grad, input_whole, sums = first_back(last, input_whole)
    near = halve_all(near, bits[1:])
    far = [sum_lines(held) for held in far]
    (
        near,
        far,
        input_grad,
        input_whole,
        sums,
        third_sums,
        qvk_sums,
        first_sums,
        second_sums,
        upper_sums,
        out_whole,
        out_parts,
        down_grads,
        up_share,
        in_parts,
    ) = tie(
        near,
        far,
        input_grad,
        input_whole,
        sums,
        third_sums,
        qvk_sums,
        first_sums,
        second_sums,
        upper_sums,
        out_whole,
        out_parts,
        down_grads,
        up_share,
        in_parts,
    )
    third_sums = third_sums + sums
    in_parts.append(trade_halves(input_grad))
    lower = in_parts[-1][1]
    up_found = join_on({0: up_share[None]}, far_bits)
    near_total = add_low(
        sum_lines(near[0]), *(swap(term, "tensor", rank) for rank, term in zip(ranks[1:], far))
    )
    (
        near_total,
        in_parts,
        up_found,
        out_parts,
        out_whole,
        input_whole,
        third_sums,
        qvk_sums,
        first_sums,
        second_sums,
        upper_sums,
        down_grads,
    ) = tie(
        near_total,
        [*in_parts[:-1], in_parts[-1][:1]],
        up_found,
        out_parts,
        out_whole,
        input_whole,
        third_sums,
        qvk_sums,
        first_sums,
        second_sums,
        upper_sums,
        down_grads,
    )
    in_parts[-1].append(lower)
    out_whole = lay(out_whole, out_parts, 0)
    for slot in range(last):
        input_whole = lay_halves(input_whole, in_parts[slot], slot)
    near_found = among_replicas(near_total)
    up_o_grads = place_found(join_on(up_found, far_bit))

    def all_ranks(parts, size):
        whole = jnp.zeros((tensor_count * size,), full)
        for rank in ranks:
            whole = lax.dynamic_update_slice_in_dim(whole, parts[rank], (tensor_rank ^ rank) * size, 0)
        return whole

    vectors = [
        third_sums[0],
        third_sums[1],
        all_ranks([sums[:width] for sums in qvk_sums], width),
        all_ranks([sums[width : 2 * width] for sums in qvk_sums], width),
        second_sums[2],
        second_sums[0],
        second_sums[1],
        upper_sums[0].reshape(tensor_count, unit_width)[:, :units].reshape(-1),
        first_sums[0],
    ]
    sizes = [vector.shape[0] for vector in vectors]
    joined = jnp.concatenate(vectors)
    padded = ceil_to(joined.shape[0], 8 * LANES)
    summed = jnp.pad(joined, (0, padded - joined.shape[0])).reshape(-1, LANES)
    summed = sum_over(summed, "replica")
    near_found, summed = tie(near_found, summed)
    summed = sum_over(summed, "fsdp")
    summed, in_parts[-1][1] = tie(summed, in_parts[-1][1])
    summed = sum_over(summed, "tensor").reshape(-1)
    in_grads = place_found(near_found)
    input_whole = lay_halves(input_whole, in_parts[-1], last)
    ends, start = [], 0
    for size in sizes:
        share = size // tensor_count
        ends.append(lax.dynamic_slice_in_dim(summed, start + tensor_rank * share, share, 0))
        start += size
    gain_one, shift_one, q_sum, v_sum, o_sum, gain_two, shift_two, up_sum, down_sum = ends
    return (
        out_whole,
        input_whole,
        gain_one,
        shift_one,
        in_grads[:, :width].astype(full),
        q_sum,
        in_grads[:, 2 * width : 3 * width].astype(full),
        in_grads[:, width : 2 * width].astype(full),
        v_sum,
        up_o_grads[:, unit_width + SHIFT : unit_width + SHIFT + width].astype(full).T,
        o_sum,
        gain_two,
        shift_two,
        up_o_grads[:, :units].astype(full),
        up_sum,
        down_grads[:, :units].astype(full).T,
        down_sum,
    )


def halves(size):
    return size & (size - 1) == 0


def by_images(mesh):
    return SLOTS * MB % mesh.shape["tensor"] == 0 and all(halves(size) for size in mesh.shape.values())


def solution(mesh):
    in_specs = (
        P(("replica", "fsdp"), None, None),
        P(("replica", "fsdp")),
        P(("replica", "fsdp"), None, None),
        P(),
        P(),
        P("fsdp", "tensor"),
        P(),
        P("fsdp", "tensor"),
        P("fsdp", "tensor"),
        P(),
        P("tensor", "fsdp"),
        P(),
        P(),
        P(),
        P("fsdp", "tensor"),
        P(),
        P("tensor", "fsdp"),
        P(),
    )
    out_specs = (
        P(("replica", "fsdp"), None, None),
        P(("replica", "fsdp"), None, None),
        P("tensor"),
        P("tensor"),
        P("fsdp", "tensor"),
        P("tensor"),
        P("fsdp", "tensor"),
        P("fsdp", "tensor"),
        P("tensor"),
        P("tensor", "fsdp"),
        P("tensor"),
        P("tensor"),
        P("tensor"),
        P("fsdp", "tensor"),
        P("tensor"),
        P("tensor", "fsdp"),
        P("tensor"),
    )
    body = image_body if by_images(mesh) else split_heads_body
    return jax.shard_map(body, mesh=mesh, in_specs=in_specs, out_specs=out_specs, check_vma=False)
```

```python
import functools

import jax
import jax.numpy as jnp
from jax import lax
from jax.experimental import pallas as pl
from jax.experimental.pallas import tpu as pltpu
from jax.sharding import PartitionSpec as P

HEAD = 72
MB = 2
SLOTS = 3


EPSILON = 1e-06


def matmul(first_op, second_op):
    return jnp.dot(first_op, second_op, preferred_element_type=jnp.float32)


def matmul_tn(first_op, second_op):
    return lax.dot_general(
        first_op, second_op, (((0,), (0,)), ((), ())), preferred_element_type=jnp.float32
    )


def matmul_nt(first_op, second_op):
    return lax.dot_general(
        first_op, second_op, (((1,), (1,)), ((), ())), preferred_element_type=jnp.float32
    )


def gelu_tanh(values):
    return jax.nn.gelu(values, approximate=True)


def row_totals(first_sum, second_sum):
    return lax.psum((first_sum, second_sum), "tensor")


def spread_whole(rounded):
    return lax.all_gather(rounded, "tensor", axis=1, tiled=True)


def combine_parts(partial_value):
    return lax.psum_scatter(partial_value, "tensor", scatter_dimension=1, tiled=True)


def normalize(stream, gain_vec, shift_vec):
    full_width = stream.shape[1] * lax.axis_size("tensor")
    totals = row_totals(
        jnp.sum(stream, axis=1, keepdims=True), jnp.sum(stream * stream, axis=1, keepdims=True)
    )
    center = totals[0] / full_width
    spread = totals[1] / full_width - center * center
    scale_inv = lax.rsqrt(spread + EPSILON)
    normed = (stream - center) * scale_inv
    rounded = (normed * gain_vec + shift_vec).astype(jnp.bfloat16)
    return (spread_whole(rounded), normed, scale_inv)


def norm_back(grad_part, normed, scale_inv, gain_vec):
    scaled = grad_part * gain_vec
    full_width = grad_part.shape[1] * lax.axis_size("tensor")
    totals = row_totals(
        jnp.sum(scaled, axis=1, keepdims=True), jnp.sum(scaled * normed, axis=1, keepdims=True)
    )
    mean_one = totals[0] / full_width
    mean_two = totals[1] / full_width
    return scale_inv * (scaled - mean_one - normed * mean_two)


def score_block(queries, key_rows):
    return jnp.einsum("bqhd,bkhd->bhqk", queries, key_rows, preferred_element_type=jnp.float32)


def forward_pass(stream, row_mask, weights, vectors, sizes_info):
    q_full, k_full, v_full, o_full, up_full, down_full = weights
    gain_one, shift_one, q_shift, v_shift, o_shift, gain_two, shift_two, up_shift, down_shift = (
        vectors
    )
    blocks, length, row_count, padded_rows = sizes_info
    head_count = q_shift.shape[0] // HEAD
    shape_four = (blocks, length, head_count, HEAD)
    first, normed_one, inv_one = normalize(stream, gain_one, shift_one)
    queries = (
        ((matmul(first, q_full) + q_shift) * HEAD ** (-0.5))
        .astype(jnp.bfloat16)
        .reshape(shape_four)
    )
    key_rows = matmul(first, k_full).astype(jnp.bfloat16).reshape(shape_four)
    value_rows = (matmul(first, v_full) + v_shift).astype(jnp.bfloat16).reshape(shape_four)
    scores = score_block(queries, key_rows)
    top_score = jnp.max(scores, axis=-1, keepdims=True)
    log_total = top_score + jnp.log(jnp.sum(jnp.exp(scores - top_score), axis=-1, keepdims=True))
    probs_bf = jnp.exp(scores - log_total).astype(jnp.bfloat16)
    attended = jnp.einsum(
        "bhqk,bkhd->bqhd", probs_bf, value_rows, preferred_element_type=jnp.float32
    )
    attended_bf = attended.reshape(row_count, head_count * HEAD).astype(jnp.bfloat16)
    middle = stream + combine_parts(matmul(attended_bf, o_full)) + o_shift
    second, normed_two, inv_two = normalize(middle, gain_two, shift_two)
    upper_pre = matmul(second, up_full) + up_shift
    hidden = gelu_tanh(upper_pre).astype(jnp.bfloat16)
    result = middle + combine_parts(matmul(hidden, down_full)) + down_shift
    output = (result * row_mask).astype(jnp.bfloat16)
    kept_state = (
        first,
        normed_one,
        inv_one,
        queries,
        key_rows,
        value_rows,
        log_total,
        attended_bf,
        normed_two,
        inv_two,
        second,
        upper_pre,
        hidden,
    )
    return (output, kept_state)


def backward_pass(cot_stream, row_mask, weights, vectors, kept_state, sizes_info):
    q_full, k_full, v_full, o_full, up_full, down_full = weights
    gain_one, shift_one, q_shift, v_shift, o_shift, gain_two, shift_two, up_shift, down_shift = (
        vectors
    )
    (
        first,
        normed_one,
        inv_one,
        queries,
        key_rows,
        value_rows,
        log_total,
        attended_bf,
        normed_two,
        inv_two,
        second,
        upper_pre,
        hidden,
    ) = kept_state
    blocks, length, row_count, padded_rows = sizes_info
    shape_four = queries.shape
    out_grad = cot_stream.astype(jnp.float32) * row_mask
    out_whole = spread_whole(out_grad.astype(jnp.bfloat16))
    down_grad = matmul_tn(hidden, out_whole)
    hidden_grad = matmul_nt(out_whole, down_full)
    upper_grad = jax.vjp(gelu_tanh, upper_pre)[1](hidden_grad)[0].astype(jnp.bfloat16)
    up_grad = matmul_tn(second, upper_grad)
    second_grad = combine_parts(matmul_nt(upper_grad, up_full))
    middle_grad = out_grad + norm_back(second_grad, normed_two, inv_two, gain_two)
    middle_bf = middle_grad.astype(jnp.bfloat16)
    middle_whole = spread_whole(middle_bf)
    o_grad = matmul_tn(attended_bf, middle_whole)
    attended_grad = matmul_nt(middle_whole, o_full).astype(jnp.bfloat16).reshape(shape_four)
    scores = score_block(queries, key_rows)
    probs = jnp.exp(scores - log_total)
    probs_bf = probs.astype(jnp.bfloat16)
    prob_grad = jnp.einsum(
        "bqhd,bkhd->bhqk", attended_grad, value_rows, preferred_element_type=jnp.float32
    )
    value_grad = jnp.einsum(
        "bhqk,bqhd->bkhd", probs_bf, attended_grad, preferred_element_type=jnp.float32
    )
    value_grad = value_grad.reshape(row_count, -1).astype(jnp.bfloat16)
    row_dot = jnp.sum(prob_grad * probs, axis=-1, keepdims=True)
    score_grad = (probs * (prob_grad - row_dot)).astype(jnp.bfloat16)
    query_grad = jnp.einsum(
        "bhqk,bkhd->bqhd", score_grad, key_rows, preferred_element_type=jnp.float32
    )
    query_grad = (query_grad.reshape(row_count, -1) * HEAD ** (-0.5)).astype(jnp.bfloat16)
    key_grad = jnp.einsum(
        "bhqk,bqhd->bkhd", score_grad, queries, preferred_element_type=jnp.float32
    )
    key_grad = key_grad.reshape(row_count, -1).astype(jnp.bfloat16)
    first_grad = combine_parts(
        matmul_nt(query_grad, q_full) + matmul_nt(key_grad, k_full) + matmul_nt(value_grad, v_full)
    )
    input_grad = middle_grad + norm_back(first_grad, normed_one, inv_one, gain_one)
    matrices = (
        matmul_tn(first, query_grad),
        matmul_tn(first, key_grad),
        matmul_tn(first, value_grad),
        o_grad,
        up_grad,
        down_grad,
    )
    vector_grads = (
        jnp.sum(first_grad * normed_one, axis=0),
        jnp.sum(first_grad, axis=0),
        jnp.sum(query_grad, axis=0, dtype=jnp.float32),
        jnp.sum(value_grad, axis=0, dtype=jnp.float32),
        jnp.sum(middle_bf, axis=0, dtype=jnp.float32),
        jnp.sum(second_grad * normed_two, axis=0),
        jnp.sum(second_grad, axis=0),
        jnp.sum(upper_grad, axis=0, dtype=jnp.float32),
        jnp.sum(out_grad, axis=0),
    )
    return (input_grad.astype(jnp.bfloat16), matrices, vector_grads)


def split_heads_body(
    images,
    live,
    cotangent,
    ln1_gain,
    ln1_bias,
    q_weight,
    q_bias,
    k_weight,
    v_weight,
    v_bias,
    o_weight,
    o_bias,
    ln2_gain,
    ln2_bias,
    fc1_weight,
    fc1_bias,
    fc2_weight,
    fc2_bias,
):
    tensor_count = lax.axis_size("tensor")
    tensor_rank = lax.axis_index("tensor")
    length = images.shape[1]
    full_width = images.shape[2]
    part_width = full_width // tensor_count
    feature_start = tensor_rank * part_width
    head_width = q_bias.shape[0] // tensor_count
    head_start = tensor_rank * head_width
    unit_width = fc1_bias.shape[0] // tensor_count
    unit_start = tensor_rank * unit_width
    row_count = SLOTS * length
    row_share = (row_count + tensor_count - 1) // tensor_count
    padded_rows = row_share * tensor_count
    sizes_info = (SLOTS, length, row_count, padded_rows)
    q_shift = lax.dynamic_slice_in_dim(q_bias, head_start, head_width, 0)
    v_shift = lax.dynamic_slice_in_dim(v_bias, head_start, head_width, 0)
    up_shift = lax.dynamic_slice_in_dim(fc1_bias, unit_start, unit_width, 0)
    gain_one, shift_one, o_shift, gain_two, shift_two, down_shift = tuple(
        (
            lax.dynamic_slice_in_dim(vector, feature_start, part_width, 0)
            for vector in (ln1_gain, ln1_bias, o_bias, ln2_gain, ln2_bias, fc2_bias)
        )
    )
    vectors = (
        gain_one,
        shift_one,
        q_shift,
        v_shift,
        o_shift,
        gain_two,
        shift_two,
        up_shift,
        down_shift,
    )
    q_low = q_weight.astype(jnp.bfloat16)
    k_low = k_weight.astype(jnp.bfloat16)
    v_low = v_weight.astype(jnp.bfloat16)
    o_low = o_weight.astype(jnp.bfloat16)
    up_low = fc1_weight.astype(jnp.bfloat16)
    down_low = fc2_weight.astype(jnp.bfloat16)
    slot_mask = live.astype(jnp.float32)
    outputs = []
    input_grads = []
    matrix_sums = None
    vector_sums = None
    for micro_batch in range(MB):
        slot_start = micro_batch * SLOTS
        batch_tokens = images[slot_start : slot_start + SLOTS].reshape(row_count, full_width)
        batch_cot = cotangent[slot_start : slot_start + SLOTS].reshape(row_count, full_width)
        mask_rows = jnp.broadcast_to(
            slot_mask[slot_start : slot_start + SLOTS, None], (SLOTS, length)
        ).reshape(-1, 1)
        stream = lax.dynamic_slice_in_dim(batch_tokens, feature_start, part_width, 1).astype(
            jnp.float32
        )
        cot_stream = lax.dynamic_slice_in_dim(batch_cot, feature_start, part_width, 1)
        forward_weights = (
            lax.all_gather(q_low, "fsdp", axis=0, tiled=True),
            lax.all_gather(k_low, "fsdp", axis=0, tiled=True),
            lax.all_gather(v_low, "fsdp", axis=0, tiled=True),
            lax.all_gather(o_low, "fsdp", axis=1, tiled=True),
            lax.all_gather(up_low, "fsdp", axis=0, tiled=True),
            lax.all_gather(down_low, "fsdp", axis=1, tiled=True),
        )
        output, kept_state = forward_pass(stream, mask_rows, forward_weights, vectors, sizes_info)
        backward_weights = (
            lax.all_gather(q_low, "fsdp", axis=0, tiled=True),
            lax.all_gather(k_low, "fsdp", axis=0, tiled=True),
            lax.all_gather(v_low, "fsdp", axis=0, tiled=True),
            lax.all_gather(o_low, "fsdp", axis=1, tiled=True),
            lax.all_gather(up_low, "fsdp", axis=0, tiled=True),
            lax.all_gather(down_low, "fsdp", axis=1, tiled=True),
        )
        grad_in, matrices, vector_grads = backward_pass(
            cot_stream, mask_rows, backward_weights, vectors, kept_state, sizes_info
        )
        whole_out, whole_grad = (
            lax.all_gather(output, "tensor", axis=1, tiled=True),
            lax.all_gather(grad_in, "tensor", axis=1, tiled=True),
        )
        outputs.append(whole_out.reshape(SLOTS, length, full_width))
        input_grads.append(whole_grad.reshape(SLOTS, length, full_width))
        vector_sums = (
            vector_grads
            if vector_sums is None
            else jax.tree.map(jnp.add, vector_sums, vector_grads)
        )
        matrix_sums = (
            matrices if matrix_sums is None else jax.tree.map(jnp.add, matrix_sums, matrices)
        )
    total_wq, total_wk, total_wv, total_wo, total_up, total_down = matrix_sums
    shard_wq, shard_wk, shard_wv, shard_wo, shard_up, shard_down = (
        lax.psum_scatter(
            total_wq.astype(jnp.bfloat16), "fsdp", scatter_dimension=0, tiled=True
        ).astype(jnp.float32),
        lax.psum_scatter(
            total_wk.astype(jnp.bfloat16), "fsdp", scatter_dimension=0, tiled=True
        ).astype(jnp.float32),
        lax.psum_scatter(
            total_wv.astype(jnp.bfloat16), "fsdp", scatter_dimension=0, tiled=True
        ).astype(jnp.float32),
        lax.psum_scatter(
            total_wo.astype(jnp.bfloat16), "fsdp", scatter_dimension=1, tiled=True
        ).astype(jnp.float32),
        lax.psum_scatter(
            total_up.astype(jnp.bfloat16), "fsdp", scatter_dimension=0, tiled=True
        ).astype(jnp.float32),
        lax.psum_scatter(
            total_down.astype(jnp.bfloat16), "fsdp", scatter_dimension=1, tiled=True
        ).astype(jnp.float32),
    )
    final_wq, final_wk, final_wv, final_wo, final_up, final_down = (
        lax.psum(shard_wq.astype(jnp.bfloat16), "replica").astype(jnp.float32),
        lax.psum(shard_wk.astype(jnp.bfloat16), "replica").astype(jnp.float32),
        lax.psum(shard_wv.astype(jnp.bfloat16), "replica").astype(jnp.float32),
        lax.psum(shard_wo.astype(jnp.bfloat16), "replica").astype(jnp.float32),
        lax.psum(shard_up.astype(jnp.bfloat16), "replica").astype(jnp.float32),
        lax.psum(shard_down.astype(jnp.bfloat16), "replica").astype(jnp.float32),
    )
    (
        sum_gain_one,
        sum_shift_one,
        sum_q_shift,
        sum_v_shift,
        sum_o_shift,
        sum_gain_two,
        sum_shift_two,
        sum_up_shift,
        sum_down_shift,
    ) = vector_sums
    summed = lax.psum(
        (
            sum_gain_one,
            sum_shift_one,
            sum_q_shift,
            sum_v_shift,
            sum_o_shift,
            sum_gain_two,
            sum_shift_two,
            sum_up_shift,
            sum_down_shift,
        ),
        ("replica", "fsdp"),
    )
    (
        grad_gain_one,
        grad_shift_one,
        grad_q_shift,
        grad_v_shift,
        grad_o_shift,
        grad_gain_two,
        grad_shift_two,
        grad_up_shift,
        grad_down_shift,
    ) = summed
    return (
        jnp.concatenate(outputs, axis=0),
        jnp.concatenate(input_grads, axis=0),
        grad_gain_one,
        grad_shift_one,
        final_wq,
        grad_q_shift,
        final_wk,
        final_wv,
        grad_v_shift,
        final_wo,
        grad_o_shift,
        grad_gain_two,
        grad_shift_two,
        final_up,
        grad_up_shift,
        final_down,
        grad_down_shift,
    )


WINDOW = 256
LANES = 128
SHIFT = 64
VMEM = 60 * 2**20
GELU = 0.7978845608
EVERY = ("tensor", "fsdp", "replica")


def ceil_to(value, step):
    return -(-value // step) * step


def call(kernel, name, grid, scalars, ins, outs, flops=0, scratch=(), aliases=None):
    total = sum(array.size * array.dtype.itemsize for array, _ in ins)
    return pl.pallas_call(
        kernel,
        grid_spec=pltpu.PrefetchScalarGridSpec(
            num_scalar_prefetch=1,
            grid=grid,
            in_specs=[spec for _, spec in ins],
            out_specs=[spec for _, _, spec in outs],
            scratch_shapes=list(scratch),
        ),
        out_shape=[jax.ShapeDtypeStruct(shape, dtype) for shape, dtype, _ in outs],
        input_output_aliases=aliases or {},
        compiler_params=pltpu.CompilerParams(vmem_limit_bytes=VMEM),
        cost_estimate=pl.CostEstimate(flops=flops, bytes_accessed=total, transcendentals=0),
        name=name,
    )(scalars, *(array for array, _ in ins))


def fixed(shape, index):
    return pl.BlockSpec(shape, index, pipeline_mode=pl.Buffered(1))


def head_window(offset, base, rows):
    start = (offset + base) // LANES * LANES
    lane = lax.broadcasted_iota(jnp.int32, (rows, WINDOW), 1) + start
    inside = (lane >= offset + base) & (lane < offset + base + HEAD)
    return pl.ds(pl.multiple_of(start, LANES), WINDOW), inside


def attention(qvk, length, rows, width, group):
    heads = width // HEAD
    count = qvk.shape[0] // rows
    steps = heads // group
    out_width = ceil_to(width + SHIFT, WINDOW)

    def kernel(none_ref, qvk_ref, mixed_ref, probs_ref):
        @pl.when(pl.program_id(1) == 0)
        def _():
            mixed_ref[...] = jnp.zeros_like(mixed_ref)

        real = lax.broadcasted_iota(jnp.int32, (rows, rows), 1) < length

        def head(item):
            return (pl.program_id(1) * group + item) * HEAD

        def scores_of(item):
            at_q, _ = head_window(head(item), 0, rows)
            at_k, in_k = head_window(head(item), 2 * width, rows)
            key_rows = jnp.where(in_k, qvk_ref[:, at_k], 0)
            return jnp.where(real, matmul_nt(qvk_ref[:, at_q], key_rows), -1e30)

        following = scores_of(0)
        for item in range(group):
            scores = following
            if item + 1 < group:
                following = scores_of(item + 1)
            at_v, in_v = head_window(head(item), width, rows)
            at_o, in_o = head_window(head(item), SHIFT, rows)
            value_rows = jnp.where(in_v, qvk_ref[:, at_v], 0)
            powers = jnp.exp(scores - jnp.max(scores, axis=1, keepdims=True))
            total = jnp.sum(powers, axis=1, keepdims=True)
            probs = (powers * (1.0 / total)).astype(jnp.bfloat16)
            probs_ref[item] = probs
            mixed = matmul(probs, value_rows).astype(jnp.bfloat16)
            mixed_ref[:, at_o] = jnp.where(in_o, mixed, mixed_ref[:, at_o])

    return call(
        kernel,
        "attention",
        (count, steps),
        jnp.zeros((1,), jnp.int32),
        [(qvk, pl.BlockSpec((rows, qvk.shape[1]), lambda i, g, s: (i, 0)))],
        [
            ((count * rows, out_width), jnp.bfloat16, pl.BlockSpec((rows, out_width), lambda i, g, s: (i, 0))),
            (
                (count * heads, rows, rows),
                jnp.bfloat16,
                pl.BlockSpec((group, rows, rows), lambda i, g, s: (i * steps + g, 0, 0)),
            ),
        ],
        flops=4 * count * heads * rows * rows * WINDOW,
    )


def attention_back(qvk, mixed, grad, probs, images, kept, rows, width, group):
    heads = width // HEAD
    steps = heads // group
    at = images.start
    count = len(images)

    def kernel(none_ref, qvk_ref, mixed_ref, grad_ref, probs_ref, *refs):
        out_ref, sums_ref = refs[-2:]

        @pl.when(pl.program_id(1) == 0)
        def _():
            out_ref[...] = jnp.zeros_like(out_ref)

        for item in range(group):
            offset = (pl.program_id(1) * group + item) * HEAD
            at_q, in_q = head_window(offset, 0, rows)
            at_v, in_v = head_window(offset, width, rows)
            at_k, in_k = head_window(offset, 2 * width, rows)
            at_o, in_o = head_window(offset, SHIFT, rows)
            grad = jnp.where(in_o, grad_ref[:, at_o], 0)
            query_rows = jnp.where(in_q, qvk_ref[:, at_q], 0)
            key_rows = jnp.where(in_k, qvk_ref[:, at_k], 0)
            probs = probs_ref[item]
            row_dot = jnp.sum(
                grad.astype(jnp.float32) * mixed_ref[:, at_o].astype(jnp.float32), axis=1, keepdims=True
            )
            prob_grad = matmul_nt(grad, qvk_ref[:, at_v])
            score_grad = (probs.astype(jnp.float32) * (prob_grad - row_dot)).astype(jnp.bfloat16)
            value_grad = matmul_tn(probs, grad).astype(jnp.bfloat16)
            query_grad = (matmul(score_grad, key_rows) * HEAD ** (-0.5)).astype(jnp.bfloat16)
            key_grad = matmul_tn(score_grad, query_rows).astype(jnp.bfloat16)
            out_ref[:, at_q] = jnp.where(in_q, query_grad, out_ref[:, at_q])
            out_ref[:, at_v] = jnp.where(in_v, value_grad, out_ref[:, at_v])
            out_ref[:, at_k] = jnp.where(in_k, key_grad, out_ref[:, at_k])

        @pl.when(pl.program_id(1) == steps - 1)
        def _():
            total = jnp.sum(out_ref[...].astype(jnp.float32), axis=0, keepdims=True)
            sums_ref[0] = jnp.broadcast_to(total, sums_ref.shape[1:])

    ins = [
        (qvk, pl.BlockSpec((rows, qvk.shape[1]), lambda i, g, s: (at + i, 0))),
        (mixed, pl.BlockSpec((rows, mixed.shape[1]), lambda i, g, s: (at + i, 0))),
        (grad, pl.BlockSpec((rows, mixed.shape[1]), lambda i, g, s: (at + i, 0))),
        (probs, pl.BlockSpec((group, rows, rows), lambda i, g, s: ((at + i) * steps + g, 0, 0))),
    ]
    if kept is not None:
        ins.append((kept, pl.BlockSpec(memory_space=pl.ANY)))
    grads, sums = call(
        kernel,
        "attention_back",
        (count, steps),
        jnp.zeros((1,), jnp.int32),
        ins,
        [
            (qvk.shape, jnp.bfloat16, pl.BlockSpec((rows, qvk.shape[1]), lambda i, g, s: (at + i, 0))),
            ((count, 8, qvk.shape[1]), jnp.float32, pl.BlockSpec((1, 8, qvk.shape[1]), lambda i, g, s: (i, 0, 0))),
        ],
        aliases=None if kept is None else {5: 0},
        flops=8 * count * heads * rows * rows * WINDOW,
    )
    return grads, jnp.sum(sums[:, 0], axis=0)


def place(pieces, slots, total):
    def kernel(slots_ref, *refs):
        at = 0
        for ref in refs[:-1]:
            for block in range(ref.shape[0]):
                refs[-1][pl.ds(slots_ref[at], 1)] = ref[block : block + 1]
                at += 1

    def whole(shape):
        return fixed(shape, lambda i, s: (0, 0, 0))

    shape = (total, *pieces[0].shape[1:])
    return call(
        kernel,
        "place",
        (1,),
        jnp.stack([slot for group in slots for slot in group]).astype(jnp.int32),
        [(piece, whole(piece.shape)) for piece in pieces],
        [(shape, pieces[0].dtype, whole(shape))],
    )[0]


def outer_sum(left, right, ranks, step, total=None, kept=None, at=None, scalars=None):
    rows, lines = left.shape
    columns = right.shape[1] // ranks
    steps = columns // step
    held = ranks * lines if kept is None else kept.shape[0]

    def kernel(scalars_ref, left_ref, right_ref, *refs):
        refs[-1][...] = matmul_tn(left_ref[...], right_ref[...]).astype(refs[-1].dtype)

    def place_of(t, j, s):
        return (t, j) if kept is None else (s[at[0]], at[1])

    return call(
        kernel,
        "outer_sum",
        (ranks, steps),
        jnp.zeros((1,), jnp.int32) if scalars is None else scalars,
        [
            (left, fixed((rows, lines), lambda t, j, s: (0, 0))),
            (right, pl.BlockSpec((rows, step), lambda t, j, s: (0, t * steps + j))),
        ]
        + ([] if kept is None else [(kept, pl.BlockSpec(memory_space=pl.ANY))]),
        [((held, total or columns), jnp.bfloat16, pl.BlockSpec((lines, step), place_of))],
        flops=2 * rows * lines * columns * ranks,
        aliases=None if kept is None else {3: 0},
    )[0]


def tie(*values):
    return lax.optimization_barrier(values)


def swap(array, axis, bits):
    size = lax.axis_size(axis)
    return lax.ppermute(array, axis, [(rank, rank ^ bits) for rank in range(size)])


def turn(array, axis, steps):
    size = lax.axis_size(axis)
    return lax.ppermute(array, axis, [(rank, (rank + steps) % size) for rank in range(size)])


def replica_bits():
    bit = lax.axis_size("replica") // 2
    bits = []
    while bit:
        bits.append(bit)
        bit //= 2
    return bits


def swap_found(found, bit):
    return {**found, **{bits ^ bit: swap(held, "replica", bit) for bits, held in found.items()}}


def among_replicas(piece):
    found = {0: piece}
    for bit in replica_bits():
        found = swap_found(found, bit)
    return found


def from_lines(shard):
    copies = lax.axis_size("replica")
    blocks = shard.reshape(copies, -1, shard.shape[1])
    mine = lax.dynamic_slice_in_dim(blocks, lax.axis_index("replica"), 1, 0)
    return [mine] + [turn(mine, "fsdp", step) for step in range(1, lax.axis_size("fsdp"))]


def slots_of(found, skip):
    copies, lines = lax.axis_size("replica"), lax.axis_size("fsdp")
    copy, line = lax.axis_index("replica"), lax.axis_index("fsdp")
    starts = [(line - step) % lines * copies for step in range(skip, lines)]
    return [[start + (copy ^ bits) for start in starts] for bits in found]


def gather_own(shard, parts):
    copies, lines, line = lax.axis_size("replica"), lax.axis_size("fsdp"), lax.axis_index("fsdp")
    blocks = shard.reshape(copies, -1, shard.shape[1])
    pieces, slots = [blocks], [[line * copies + at for at in range(copies)]]
    if lines > 1:
        found = among_replicas(jnp.concatenate(parts[1:], axis=0))
        pieces += list(found.values())
        slots += slots_of(found, 1)
    return place(pieces, slots, lines * copies).reshape(-1, shard.shape[1])


def gather_far(parts, rank):
    found = {0: swap(jnp.concatenate(parts, axis=0), "tensor", rank)}
    for bit in replica_bits()[:-1]:
        found = swap_found(found, bit)
    return found


def finish_far(found):
    for bit in replica_bits()[-1:]:
        found = swap_found(found, bit)
    total = lax.axis_size("replica") * lax.axis_size("fsdp")
    whole = place(list(found.values()), slots_of(found, 0), total)
    return whole.reshape(-1, whole.shape[2])


def gather_whole(shard):
    share = shard.shape[0] // lax.axis_size("replica")
    part = lax.dynamic_slice_in_dim(shard, lax.axis_index("replica") * share, share, 0)
    return lax.all_gather(part, EVERY, axis=0, tiled=True)


def add_low(first_term, *terms):
    total = first_term.astype(jnp.float32)
    for term in terms:
        total = total + term.astype(jnp.float32)
    return total.astype(jnp.bfloat16)


def by_lines(term):
    bits = len(replica_bits())
    return term.reshape(lax.axis_size("fsdp"), *(2 for _ in range(bits)), -1, term.shape[1])


def halve(held, bit):
    side = lax.axis_index("replica") // bit % 2
    axis = held.ndim - 3
    keep = lax.dynamic_index_in_dim(held, side, axis, keepdims=False)
    send = lax.dynamic_index_in_dim(held, 1 - side, axis, keepdims=False)
    return add_low(keep, swap(send, "replica", bit))


def sum_lines(held):
    lines, line = lax.axis_size("fsdp"), lax.axis_index("fsdp")
    terms = [lax.dynamic_index_in_dim(held, line, 0, keepdims=True)]
    for step in range(1, lines):
        send = lax.dynamic_index_in_dim(held, (line + step) % lines, 0, keepdims=True)
        terms.append(turn(send, "fsdp", step))
    return add_low(*terms)


def place_cuts(found, cuts):
    copy = lax.axis_index("replica")
    pieces = list(found.values())
    rows = pieces[0].shape[1]

    def kernel(slots_ref, *refs):
        for at in range(len(pieces)):
            values = refs[at][...].astype(jnp.float32)
            for (start, size), out_ref in zip(cuts, refs[len(pieces) :]):
                out_ref[pl.ds(slots_ref[at], 1)] = values[:, :, start : start + size]

    def whole(shape):
        return fixed(shape, lambda i, s: (0, 0, 0))

    shapes = [(len(pieces), rows, size) for _, size in cuts]
    wholes = call(
        kernel,
        "place_cuts",
        (1,),
        jnp.stack([copy ^ bits for bits in found]).astype(jnp.int32),
        [(piece, whole(piece.shape)) for piece in pieces],
        [(shape, jnp.float32, whole(shape)) for shape in shapes],
    )
    return [array.reshape(-1, array.shape[2]) for array in wholes]


def place_found(found):
    copy = lax.axis_index("replica")
    whole = place(list(found.values()), [[copy ^ bits] for bits in found], len(found))
    return whole.reshape(-1, whole.shape[2])


def sum_over(vector, axes):
    size = lax.axis_size(axes)
    terms = [vector] + [
        lax.ppermute(vector, axes, [(rank, rank ^ bits) for rank in range(size)]) for bits in range(1, size)
    ]
    while len(terms) > 1:
        terms = [left + right for left, right in zip(terms[::2], terms[1::2])]
    return terms[0]


def norm_parts(values):
    center = jnp.mean(values, axis=1, keepdims=True)
    spread = jnp.mean(values * values, axis=1, keepdims=True) - center * center
    scale_inv = lax.rsqrt(spread + EPSILON)
    return (values - center) * scale_inv, scale_inv


def norm_backward(grad, normed, scale_inv, gain_vec):
    scaled = grad * gain_vec
    mean_one = jnp.mean(scaled, axis=1, keepdims=True)
    mean_two = jnp.mean(scaled * normed, axis=1, keepdims=True)
    return scale_inv * (scaled - mean_one - normed * mean_two)


def image_body(
    images,
    live,
    cotangent,
    ln1_gain,
    ln1_bias,
    q_weight,
    q_bias,
    k_weight,
    v_weight,
    v_bias,
    o_weight,
    o_bias,
    ln2_gain,
    ln2_bias,
    fc1_weight,
    fc1_bias,
    fc2_weight,
    fc2_bias,
):
    low, full = jnp.bfloat16, jnp.float32
    tensor_count = lax.axis_size("tensor")
    tensor_rank = lax.axis_index("tensor")
    slots, length, wide = images.shape
    count = slots // tensor_count
    rows = ceil_to(length, 32)
    half = rows // 2
    width = q_weight.shape[1]
    units = fc1_weight.shape[1]
    qvk_width = ceil_to(3 * width, WINDOW)
    o_width = ceil_to(width + SHIFT, WINDOW)
    unit_width = ceil_to(units, WINDOW)
    unit_width = ceil_to(unit_width, o_width)
    ranks = range(tensor_count)
    all_rows = count * rows
    heads = width // HEAD
    group = next(size for size in (8, 4, 2, 1) if heads % size == 0)
    blocks = all_rows // half
    scalars = jnp.concatenate(
        [
            jnp.stack([tensor_rank * count] + [tensor_rank ^ rank for rank in ranks]).astype(jnp.int32),
            lax.dynamic_slice_in_dim(live, tensor_rank * count, count, 0),
        ]
    )
    live_at = 1 + tensor_count

    def columns(parts, ahead, total):
        body_part = jnp.concatenate(parts, axis=1)
        return jnp.pad(body_part, ((0, 0), (ahead, total - ahead - body_part.shape[1])))

    def row(vector):
        return vector.reshape(1, -1)

    def slots_spec(first=0):
        return pl.BlockSpec((1, half, wide), lambda i, s: (s[0] + first + i // 2, i % 2, 0))

    def rows_spec(size, first=0):
        return pl.BlockSpec((half, size), lambda i, s: (2 * first + i, 0))

    def vector_spec():
        return pl.BlockSpec((1, wide), lambda i, s: (0, 0))

    def sums_spec():
        return pl.BlockSpec((8, wide), lambda i, s: (0, 0))

    def real_rows(values):
        at = lax.broadcasted_iota(jnp.int32, (half, 1), 0) + pl.program_id(0) % 2 * half
        return jnp.where(at < length, values.astype(full), 0.0)

    def live_slot(scalars_ref, first=0):
        return scalars_ref[live_at + first + pl.program_id(0) // 2].astype(full)

    def add_sums(sums_ref, *terms):
        @pl.when(pl.program_id(0) == 0)
        def _():
            sums_ref[...] = jnp.zeros_like(sums_ref)

        for at, term in enumerate(terms):
            sums_ref[at : at + 1] += jnp.sum(term, axis=0, keepdims=True)

    def product(part_refs, weight_refs):
        total = matmul_nt(part_refs[0][...], weight_refs[0][...])
        for part_ref, weight_ref in zip(part_refs[1:], weight_refs[1:]):
            total = total + matmul_nt(part_ref[...], weight_ref[...])
        return total

    qvk_shard = columns([w.astype(low) for w in (q_weight, v_weight, k_weight)], 0, qvk_width)
    parts = from_lines(qvk_shard)

    def first_kernel(scalars_ref, images_ref, cot_ref, gain_ref, shift_ref, first_ref, grad_ref, sums_ref):
        normed, _ = norm_parts(real_rows(images_ref[0]))
        first_ref[...] = (normed * gain_ref[...] + shift_ref[...]).astype(low)
        grad = real_rows(cot_ref[0]) * live_slot(scalars_ref)
        grad_ref[...] = grad.astype(low)
        add_sums(sums_ref, grad)

    first, out_grad, first_sums = call(
        first_kernel,
        "first_norm",
        (blocks,),
        scalars,
        [(images, slots_spec()), (cotangent, slots_spec()), (row(ln1_gain), vector_spec()), (row(ln1_bias), vector_spec())],
        [
            ((all_rows, wide), low, rows_spec(wide)),
            ((all_rows, wide), low, rows_spec(wide)),
            ((8, wide), full, sums_spec()),
        ],
    )

    parts, first, out_grad = tie(parts, first, out_grad)
    up_o_shard = jnp.concatenate(
        [
            columns([fc1_weight.astype(low)], 0, unit_width),
            columns([o_weight.astype(low).T], SHIFT, o_width),
        ],
        axis=1,
    )
    down_shard = columns([fc2_weight.astype(low).T], 0, unit_width)
    up_o_shard, down_shard, parts = tie(up_o_shard, down_shard, parts)
    up_o_whole = gather_whole(up_o_shard)
    down_whole = gather_whole(down_shard)
    qvk_weights = [gather_own(qvk_shard, parts)]
    far_parts = [gather_far(parts, rank) for rank in ranks[1:]]

    def of_rank(vector, rank, size):
        return lax.dynamic_slice_in_dim(vector, (tensor_rank ^ rank) * size, size, 0)

    scale_row = jnp.where(jnp.arange(qvk_width) < width, HEAD ** (-0.5), 1.0)
    qvk, mixed, probs = [], [], []
    for rank in ranks:
        shift_row = jnp.pad(
            jnp.concatenate([of_rank(q_bias, rank, width), of_rank(v_bias, rank, width)]),
            (0, qvk_width - 2 * width),
        )
        qvk.append(((matmul(first, qvk_weights[rank]) + shift_row) * scale_row).astype(low))
        mixed_part, probs_part = attention(qvk[rank], length, rows, width, group)
        if rank == 0:
            mixed_part, first, far_parts = tie(mixed_part, first, far_parts)
            qvk_weights += [finish_far(found) for found in far_parts]
        mixed.append(mixed_part)
        probs.append(probs_part)

    def o_spec(rank):
        return fixed((wide, o_width), lambda i, s: (s[1 + rank], unit_width // o_width))

    def middle_kernel(scalars_ref, *refs):
        images_ref, bias_ref, gain_ref, shift_ref, middle_ref, second_ref = refs[2 * tensor_count :]
        total = product(refs[:tensor_count], refs[tensor_count : 2 * tensor_count])
        middle = real_rows(images_ref[0]) + (total + bias_ref[...])
        middle_ref[...] = middle
        normed, _ = norm_parts(middle)
        second_ref[...] = (normed * gain_ref[...] + shift_ref[...]).astype(low)

    middle, second = call(
        middle_kernel,
        "middle_norm",
        (blocks,),
        scalars,
        [(part, rows_spec(o_width)) for part in mixed]
        + [(up_o_whole, o_spec(rank)) for rank in ranks]
        + [
            (images, slots_spec()),
            (row(o_bias), vector_spec()),
            (row(ln2_gain), vector_spec()),
            (row(ln2_bias), vector_spec()),
        ],
        [((all_rows, wide), full, rows_spec(wide)), ((all_rows, wide), low, rows_spec(wide))],
        flops=2 * all_rows * wide * o_width * tensor_count,
    )

    chunk = o_width

    def unit_rows():
        return pl.BlockSpec((half, unit_width), lambda t, i, s: (i, t))

    def unit_weights():
        return pl.BlockSpec((wide, unit_width), lambda t, i, s: (t, 0))

    def hidden_kernel(scalars_ref, second_ref, weight_ref, shift_ref, hidden_ref, slope_ref):
        for start in range(0, unit_width, chunk):
            at = slice(start, start + chunk)
            upper = matmul(second_ref[...], weight_ref[:, at]) + shift_ref[:, at]
            square = upper * upper
            share = 0.5 + 0.5 * jnp.tanh(upper * (GELU + GELU * 0.044715 * square))
            hidden = upper * share
            slope = share + (hidden - hidden * share) * (2 * GELU + 6 * GELU * 0.044715 * square)
            hidden_ref[:, at] = hidden.astype(low)
            slope_ref[:, at] = slope.astype(low)

    unit_shift = jnp.pad(
        fc1_bias.reshape(tensor_count, units), ((0, 0), (0, unit_width - units))
    ).reshape(1, -1)
    hidden, slopes = call(
        hidden_kernel,
        "hidden",
        (tensor_count, blocks),
        scalars,
        [
            (second, pl.BlockSpec((half, wide), lambda t, i, s: (i, 0))),
            (up_o_whole, unit_weights()),
            (unit_shift, pl.BlockSpec((1, unit_width), lambda t, i, s: (0, t))),
        ],
        [((all_rows, tensor_count * unit_width), low, unit_rows())] * 2,
        flops=2 * all_rows * wide * unit_width * tensor_count,
    )
    down_terms = outer_sum(out_grad, hidden, tensor_count, chunk)
    down_terms, hidden = tie(down_terms, hidden)
    down_share = lax.psum_scatter(down_terms, EVERY, scatter_dimension=0, tiled=True)

    def weight_spec(rank):
        return fixed((wide, unit_width), lambda i, s: (rank, 0))

    def unit_spec(rank):
        return pl.BlockSpec((half, unit_width), lambda i, s: (i, rank))

    def output_kernel(scalars_ref, *refs):
        middle_ref, bias_ref, output_ref, whole_ref = refs[2 * tensor_count :]
        total = product(refs[:tensor_count], refs[tensor_count : 2 * tensor_count])
        result = middle_ref[...] + (total + bias_ref[...])
        output_ref[0] = (result * live_slot(scalars_ref)).astype(low)
        whole_ref[0] = output_ref[0]

    output, out_whole = call(
        output_kernel,
        "output",
        (blocks,),
        scalars,
        [(hidden, unit_spec(rank)) for rank in ranks]
        + [(down_whole, weight_spec(rank)) for rank in ranks]
        + [(middle, rows_spec(wide)), (row(fc2_bias), vector_spec())],
        [
            ((count, length, wide), low, pl.BlockSpec((1, half, wide), lambda i, s: (i // 2, i % 2, 0))),
            ((slots, length, wide), low, slots_spec()),
        ],
        flops=2 * all_rows * wide * unit_width * tensor_count,
    )

    def trade(part):
        return [swap(part, "tensor", rank) for rank in ranks[1:]]

    def trade_halves(part):
        return [trade(piece) for piece in part]

    def lay_halves(whole, parts, first):
        for rank, *pieces in zip(ranks[1:], *parts):
            for at, piece in enumerate(pieces):
                start = ((tensor_rank ^ rank) * count + first, at * half, 0)
                whole = lax.dynamic_update_slice(whole, piece, start)
        return whole

    def lay(whole, parts, first):
        for rank, part in zip(ranks[1:], parts):
            whole = lax.dynamic_update_slice_in_dim(whole, part, (tensor_rank ^ rank) * count + first, 0)
        return whole

    output, out_grad = tie(output, out_grad)
    out_parts = trade(output)

    def hidden_back_kernel(scalars_ref, grad_ref, weight_ref, slope_ref, upper_ref, sums_ref):
        @pl.when(pl.program_id(1) == 0)
        def _():
            sums_ref[...] = jnp.zeros_like(sums_ref)

        for start in range(0, unit_width, chunk):
            at = slice(start, start + chunk)
            upper = matmul(grad_ref[...], weight_ref[:, at]) * slope_ref[:, at].astype(full)
            rounded = upper.astype(low)
            upper_ref[:, at] = rounded
            sums_ref[0:1, at] += jnp.sum(rounded.astype(full), axis=0, keepdims=True)

    upper_grads, upper_sums = call(
        hidden_back_kernel,
        "hidden_back",
        (tensor_count, blocks),
        scalars,
        [
            (out_grad, pl.BlockSpec((half, wide), lambda t, i, s: (i, 0))),
            (down_whole, unit_weights()),
            (slopes, unit_rows()),
        ],
        [
            ((all_rows, tensor_count * unit_width), low, unit_rows()),
            ((8, tensor_count * unit_width), full, pl.BlockSpec((8, unit_width), lambda t, i, s: (0, t))),
        ],
        flops=2 * all_rows * wide * unit_width * tensor_count,
    )
    up_terms = outer_sum(second, upper_grads, tensor_count, o_width, unit_width + o_width)
    up_terms, upper_grads = tie(up_terms, upper_grads)

    def middle_back_kernel(scalars_ref, *refs):
        middle_ref, grad_ref, gain_ref, *o_refs = refs[2 * tensor_count : 3 * tensor_count + 3]
        middle_grad_ref, low_ref, sums_ref, *mixed_grad_refs = refs[3 * tensor_count + 3 :]
        total = product(refs[:tensor_count], refs[tensor_count : 2 * tensor_count])
        normed, scale_inv = norm_parts(middle_ref[...])
        middle_grad = grad_ref[...].astype(full) + norm_backward(total, normed, scale_inv, gain_ref[...])
        middle_grad_ref[...] = middle_grad
        rounded = middle_grad.astype(low)
        low_ref[...] = rounded
        for o_ref, mixed_grad_ref in zip(o_refs, mixed_grad_refs):
            mixed_grad_ref[...] = matmul(rounded, o_ref[...]).astype(low)
        add_sums(sums_ref, total * normed, total, rounded.astype(full))

    middle_grad, middle_low, second_sums, *mixed_grads = call(
        middle_back_kernel,
        "middle_back",
        (blocks,),
        scalars,
        [(upper_grads, unit_spec(rank)) for rank in ranks]
        + [(up_o_whole, weight_spec(rank)) for rank in ranks]
        + [(middle, rows_spec(wide)), (out_grad, rows_spec(wide)), (row(ln2_gain), vector_spec())]
        + [(up_o_whole, o_spec(rank)) for rank in ranks],
        [
            ((all_rows, wide), full, rows_spec(wide)),
            ((all_rows, wide), low, rows_spec(wide)),
            ((8, wide), full, sums_spec()),
        ]
        + [((all_rows, o_width), low, rows_spec(o_width)) for rank in ranks],
        flops=2 * all_rows * wide * (unit_width + o_width) * tensor_count,
    )

    for rank in ranks:
        up_terms = outer_sum(
            middle_low,
            mixed[rank],
            1,
            o_width,
            unit_width + o_width,
            up_terms,
            (1 + rank, unit_width // o_width),
            scalars,
        )
    up_terms, mixed_grads[-1], out_parts = tie(up_terms, mixed_grads[-1], out_parts)
    up_share = lax.psum_scatter(up_terms, EVERY, scatter_dimension=0, tiled=True)
    bits = replica_bits()[::-1]

    def back(rank, which, kept):
        return attention_back(
            qvk[rank], mixed[rank], mixed_grads[rank], probs[rank], which, kept, rows, width, group
        )

    def first_back_kernel(scalars_ref, *refs):
        images_ref, grad_ref, gain_ref = refs[2 * tensor_count : 2 * tensor_count + 3]
        upper_ref, lower_ref, whole_ref, sums_ref = refs[-4:]
        total = product(refs[:tensor_count], refs[tensor_count : 2 * tensor_count])
        normed, scale_inv = norm_parts(real_rows(images_ref[0]))
        grad = grad_ref[...] + norm_backward(total, normed, scale_inv, gain_ref[...])
        whole_ref[0] = grad.astype(low)

        @pl.when(pl.program_id(0) == 0)
        def _():
            upper_ref[...] = whole_ref[...]

        @pl.when(pl.program_id(0) == 1)
        def _():
            lower_ref[...] = whole_ref[:, : length - half]

        add_sums(sums_ref, total * normed, total)

    qvk_grads, qvk_sums = [None] * tensor_count, [0.0] * tensor_count
    input_whole = None
    third_sums = 0.0
    in_parts = []

    def attend(rank, which):
        qvk_grads[rank], sums = back(rank, which, qvk_grads[rank])
        qvk_sums[rank] = qvk_sums[rank] + sums

    def first_back(slot, whole):
        ahead = [] if whole is None else [(whole, pl.BlockSpec(memory_space=pl.ANY))]
        upper, lower, whole, sums = call(
            first_back_kernel,
            "first_back",
            (2,),
            scalars,
            [(grads, rows_spec(qvk_width, slot)) for grads in qvk_grads]
            + [(weight, fixed((wide, qvk_width), lambda i, s: (0, 0))) for weight in qvk_weights]
            + [(images, slots_spec(slot)), (middle_grad, rows_spec(wide, slot)), (row(ln1_gain), vector_spec())]
            + ahead,
            [
                ((1, half, wide), low, pl.BlockSpec((1, half, wide), lambda i, s: (0, 0, 0))),
                ((1, length - half, wide), low, pl.BlockSpec((1, length - half, wide), lambda i, s: (0, 0, 0))),
                ((slots, length, wide), low, slots_spec(slot)),
                ((8, wide), full, sums_spec()),
            ],
            aliases={2 * tensor_count + 4: 2} if ahead else None,
            flops=2 * rows * wide * qvk_width * tensor_count,
        )
        return (upper, lower), whole, sums

    last = count - 1

    def halve_all(terms, which):
        for bit in which:
            terms = [halve(term, bit) for term in terms]
        return terms

    def join_on(found, which):
        for bit in which:
            found = swap_found(found, bit)
        return found

    far_bits, far_bit = replica_bits()[:-1], replica_bits()[-1:]

    down_found = join_on({0: down_share[None]}, far_bits)
    for rank in ranks[1:]:
        attend(rank, range(count))
    qvk_grads[1:], mixed_grads[0], down_found, first = tie(qvk_grads[1:], mixed_grads[0], down_found, first)
    far = [by_lines(outer_sum(first, grads, 1, qvk_width // 2)) for grads in qvk_grads[1:]]
    down_grads = place_found(join_on(down_found, far_bit))
    far, mixed_grads[0], down_grads = tie(far, mixed_grads[0], down_grads)
    far_done = 0
    for slot in range(last):
        if slot > 0:
            in_parts.append(trade_halves(input_grad))
        attend(0, range(slot, slot + 1))
        if slot == 0:
            far = halve_all(far, bits[:1])
            far, qvk_grads[0] = tie(far, qvk_grads[0])
        elif far_done == 1:
            far = halve_all(far, bits[1:])
        far_done += 1
        input_grad, input_whole, sums = first_back(slot, input_whole)
        third_sums = third_sums + sums
        far, input_grad, mixed_grads[0] = tie(far, input_grad, mixed_grads[0])
        if slot > 0:
            in_parts[-1][0], input_grad, mixed_grads[0] = tie(in_parts[-1][0], input_grad, mixed_grads[0])
    if last > 0:
        in_parts.append(trade_halves(input_grad))
    attend(0, range(last, count))
    near = by_lines(outer_sum(first, qvk_grads[0], 1, qvk_width // 2))
    if far_done < 2:
        far = halve_all(far, bits[far_done:])
    near, far, in_parts[:-1], qvk_grads[0] = tie(near, far, in_parts[:-1], qvk_grads[0])
    if last > 0:
        in_parts[-1][0], near, qvk_grads[0] = tie(in_parts[-1][0], near, qvk_grads[0])
    near = halve_all([near], bits[:1])
    near, qvk_grads[0], far, up_share = tie(near, qvk_grads[0], far, up_share)
    input_grad, input_whole, sums = first_back(last, input_whole)
    near = halve_all(near, bits[1:])
    far = [sum_lines(held) for held in far]
    (
        near,
        far,
        input_grad,
        input_whole,
        sums,
        third_sums,
        qvk_sums,
        first_sums,
        second_sums,
        upper_sums,
        out_whole,
        out_parts,
        down_grads,
        up_share,
        in_parts,
    ) = tie(
        near,
        far,
        input_grad,
        input_whole,
        sums,
        third_sums,
        qvk_sums,
        first_sums,
        second_sums,
        upper_sums,
        out_whole,
        out_parts,
        down_grads,
        up_share,
        in_parts,
    )
    third_sums = third_sums + sums
    in_parts.append(trade_halves(input_grad))
    lower = in_parts[-1][1]
    out_whole = lay(out_whole, out_parts, 0)
    up_found = join_on({0: up_share[None]}, far_bits)
    near_total = add_low(
        sum_lines(near[0]), *(swap(term, "tensor", rank) for rank, term in zip(ranks[1:], far))
    )
    (
        near_total,
        in_parts,
        up_found,
        out_whole,
        input_whole,
        third_sums,
        qvk_sums,
        first_sums,
        second_sums,
        upper_sums,
        down_grads,
    ) = tie(
        near_total,
        [*in_parts[:-1], in_parts[-1][:1]],
        up_found,
        out_whole,
        input_whole,
        third_sums,
        qvk_sums,
        first_sums,
        second_sums,
        upper_sums,
        down_grads,
    )
    in_parts[-1].append(lower)
    for slot in range(last):
        input_whole = lay_halves(input_whole, in_parts[slot], slot)
    near_found = among_replicas(near_total)
    up_grads, o_grads = place_cuts(
        join_on(up_found, far_bit), [(0, units), (unit_width + SHIFT, width)]
    )

    def all_ranks(parts, size):
        whole = jnp.zeros((tensor_count * size,), full)
        for rank in ranks:
            whole = lax.dynamic_update_slice_in_dim(whole, parts[rank], (tensor_rank ^ rank) * size, 0)
        return whole

    vectors = [
        third_sums[0],
        third_sums[1],
        all_ranks([sums[:width] for sums in qvk_sums], width),
        all_ranks([sums[width : 2 * width] for sums in qvk_sums], width),
        second_sums[2],
        second_sums[0],
        second_sums[1],
        upper_sums[0].reshape(tensor_count, unit_width)[:, :units].reshape(-1),
        first_sums[0],
    ]
    sizes = [vector.shape[0] for vector in vectors]
    joined = jnp.concatenate(vectors)
    padded = ceil_to(joined.shape[0], 8 * LANES)
    summed = jnp.pad(joined, (0, padded - joined.shape[0])).reshape(-1, LANES)
    summed = sum_over(summed, "replica")
    near_found, summed = tie(near_found, summed)
    summed = sum_over(summed, "fsdp")
    summed, in_parts[-1][1] = tie(summed, in_parts[-1][1])
    summed = sum_over(summed, "tensor").reshape(-1)
    q_grads, v_grads, k_grads = place_cuts(near_found, [(at * width, width) for at in range(3)])
    input_whole = lay_halves(input_whole, in_parts[-1], last)
    ends, start = [], 0
    for size in sizes:
        share = size // tensor_count
        ends.append(lax.dynamic_slice_in_dim(summed, start + tensor_rank * share, share, 0))
        start += size
    gain_one, shift_one, q_sum, v_sum, o_sum, gain_two, shift_two, up_sum, down_sum = ends
    return (
        out_whole,
        input_whole,
        gain_one,
        shift_one,
        q_grads,
        q_sum,
        k_grads,
        v_grads,
        v_sum,
        o_grads.T,
        o_sum,
        gain_two,
        shift_two,
        up_grads,
        up_sum,
        down_grads[:, :units].astype(full).T,
        down_sum,
    )


def halves(size):
    return size & (size - 1) == 0


def by_images(mesh):
    return SLOTS * MB % mesh.shape["tensor"] == 0 and all(halves(size) for size in mesh.shape.values())


def solution(mesh):
    in_specs = (
        P(("replica", "fsdp"), None, None),
        P(("replica", "fsdp")),
        P(("replica", "fsdp"), None, None),
        P(),
        P(),
        P("fsdp", "tensor"),
        P(),
        P("fsdp", "tensor"),
        P("fsdp", "tensor"),
        P(),
        P("tensor", "fsdp"),
        P(),
        P(),
        P(),
        P("fsdp", "tensor"),
        P(),
        P("tensor", "fsdp"),
        P(),
    )
    out_specs = (
        P(("replica", "fsdp"), None, None),
        P(("replica", "fsdp"), None, None),
        P("tensor"),
        P("tensor"),
        P("fsdp", "tensor"),
        P("tensor"),
        P("fsdp", "tensor"),
        P("fsdp", "tensor"),
        P("tensor"),
        P("tensor", "fsdp"),
        P("tensor"),
        P("tensor"),
        P("tensor"),
        P("fsdp", "tensor"),
        P("tensor"),
        P("tensor", "fsdp"),
        P("tensor"),
    )
    body = image_body if by_images(mesh) else split_heads_body
    return jax.shard_map(body, mesh=mesh, in_specs=in_specs, out_specs=out_specs, check_vma=False)
```

```python
import functools

import jax
import jax.numpy as jnp
from jax import lax
from jax.experimental import pallas as pl
from jax.experimental.pallas import tpu as pltpu
from jax.sharding import PartitionSpec as P

HEAD = 72
MB = 2
SLOTS = 3


EPSILON = 1e-06


def matmul(first_op, second_op):
    return jnp.dot(first_op, second_op, preferred_element_type=jnp.float32)


def matmul_tn(first_op, second_op):
    return lax.dot_general(
        first_op, second_op, (((0,), (0,)), ((), ())), preferred_element_type=jnp.float32
    )


def matmul_nt(first_op, second_op):
    return lax.dot_general(
        first_op, second_op, (((1,), (1,)), ((), ())), preferred_element_type=jnp.float32
    )


def gelu_tanh(values):
    return jax.nn.gelu(values, approximate=True)


def row_totals(first_sum, second_sum):
    return lax.psum((first_sum, second_sum), "tensor")


def spread_whole(rounded):
    return lax.all_gather(rounded, "tensor", axis=1, tiled=True)


def combine_parts(partial_value):
    return lax.psum_scatter(partial_value, "tensor", scatter_dimension=1, tiled=True)


def normalize(stream, gain_vec, shift_vec):
    full_width = stream.shape[1] * lax.axis_size("tensor")
    totals = row_totals(
        jnp.sum(stream, axis=1, keepdims=True), jnp.sum(stream * stream, axis=1, keepdims=True)
    )
    center = totals[0] / full_width
    spread = totals[1] / full_width - center * center
    scale_inv = lax.rsqrt(spread + EPSILON)
    normed = (stream - center) * scale_inv
    rounded = (normed * gain_vec + shift_vec).astype(jnp.bfloat16)
    return (spread_whole(rounded), normed, scale_inv)


def norm_back(grad_part, normed, scale_inv, gain_vec):
    scaled = grad_part * gain_vec
    full_width = grad_part.shape[1] * lax.axis_size("tensor")
    totals = row_totals(
        jnp.sum(scaled, axis=1, keepdims=True), jnp.sum(scaled * normed, axis=1, keepdims=True)
    )
    mean_one = totals[0] / full_width
    mean_two = totals[1] / full_width
    return scale_inv * (scaled - mean_one - normed * mean_two)


def score_block(queries, key_rows):
    return jnp.einsum("bqhd,bkhd->bhqk", queries, key_rows, preferred_element_type=jnp.float32)


def forward_pass(stream, row_mask, weights, vectors, sizes_info):
    q_full, k_full, v_full, o_full, up_full, down_full = weights
    gain_one, shift_one, q_shift, v_shift, o_shift, gain_two, shift_two, up_shift, down_shift = (
        vectors
    )
    blocks, length, row_count, padded_rows = sizes_info
    head_count = q_shift.shape[0] // HEAD
    shape_four = (blocks, length, head_count, HEAD)
    first, normed_one, inv_one = normalize(stream, gain_one, shift_one)
    queries = (
        ((matmul(first, q_full) + q_shift) * HEAD ** (-0.5))
        .astype(jnp.bfloat16)
        .reshape(shape_four)
    )
    key_rows = matmul(first, k_full).astype(jnp.bfloat16).reshape(shape_four)
    value_rows = (matmul(first, v_full) + v_shift).astype(jnp.bfloat16).reshape(shape_four)
    scores = score_block(queries, key_rows)
    top_score = jnp.max(scores, axis=-1, keepdims=True)
    log_total = top_score + jnp.log(jnp.sum(jnp.exp(scores - top_score), axis=-1, keepdims=True))
    probs_bf = jnp.exp(scores - log_total).astype(jnp.bfloat16)
    attended = jnp.einsum(
        "bhqk,bkhd->bqhd", probs_bf, value_rows, preferred_element_type=jnp.float32
    )
    attended_bf = attended.reshape(row_count, head_count * HEAD).astype(jnp.bfloat16)
    middle = stream + combine_parts(matmul(attended_bf, o_full)) + o_shift
    second, normed_two, inv_two = normalize(middle, gain_two, shift_two)
    upper_pre = matmul(second, up_full) + up_shift
    hidden = gelu_tanh(upper_pre).astype(jnp.bfloat16)
    result = middle + combine_parts(matmul(hidden, down_full)) + down_shift
    output = (result * row_mask).astype(jnp.bfloat16)
    kept_state = (
        first,
        normed_one,
        inv_one,
        queries,
        key_rows,
        value_rows,
        log_total,
        attended_bf,
        normed_two,
        inv_two,
        second,
        upper_pre,
        hidden,
    )
    return (output, kept_state)


def backward_pass(cot_stream, row_mask, weights, vectors, kept_state, sizes_info):
    q_full, k_full, v_full, o_full, up_full, down_full = weights
    gain_one, shift_one, q_shift, v_shift, o_shift, gain_two, shift_two, up_shift, down_shift = (
        vectors
    )
    (
        first,
        normed_one,
        inv_one,
        queries,
        key_rows,
        value_rows,
        log_total,
        attended_bf,
        normed_two,
        inv_two,
        second,
        upper_pre,
        hidden,
    ) = kept_state
    blocks, length, row_count, padded_rows = sizes_info
    shape_four = queries.shape
    out_grad = cot_stream.astype(jnp.float32) * row_mask
    out_whole = spread_whole(out_grad.astype(jnp.bfloat16))
    down_grad = matmul_tn(hidden, out_whole)
    hidden_grad = matmul_nt(out_whole, down_full)
    upper_grad = jax.vjp(gelu_tanh, upper_pre)[1](hidden_grad)[0].astype(jnp.bfloat16)
    up_grad = matmul_tn(second, upper_grad)
    second_grad = combine_parts(matmul_nt(upper_grad, up_full))
    middle_grad = out_grad + norm_back(second_grad, normed_two, inv_two, gain_two)
    middle_bf = middle_grad.astype(jnp.bfloat16)
    middle_whole = spread_whole(middle_bf)
    o_grad = matmul_tn(attended_bf, middle_whole)
    attended_grad = matmul_nt(middle_whole, o_full).astype(jnp.bfloat16).reshape(shape_four)
    scores = score_block(queries, key_rows)
    probs = jnp.exp(scores - log_total)
    probs_bf = probs.astype(jnp.bfloat16)
    prob_grad = jnp.einsum(
        "bqhd,bkhd->bhqk", attended_grad, value_rows, preferred_element_type=jnp.float32
    )
    value_grad = jnp.einsum(
        "bhqk,bqhd->bkhd", probs_bf, attended_grad, preferred_element_type=jnp.float32
    )
    value_grad = value_grad.reshape(row_count, -1).astype(jnp.bfloat16)
    row_dot = jnp.sum(prob_grad * probs, axis=-1, keepdims=True)
    score_grad = (probs * (prob_grad - row_dot)).astype(jnp.bfloat16)
    query_grad = jnp.einsum(
        "bhqk,bkhd->bqhd", score_grad, key_rows, preferred_element_type=jnp.float32
    )
    query_grad = (query_grad.reshape(row_count, -1) * HEAD ** (-0.5)).astype(jnp.bfloat16)
    key_grad = jnp.einsum(
        "bhqk,bqhd->bkhd", score_grad, queries, preferred_element_type=jnp.float32
    )
    key_grad = key_grad.reshape(row_count, -1).astype(jnp.bfloat16)
    first_grad = combine_parts(
        matmul_nt(query_grad, q_full) + matmul_nt(key_grad, k_full) + matmul_nt(value_grad, v_full)
    )
    input_grad = middle_grad + norm_back(first_grad, normed_one, inv_one, gain_one)
    matrices = (
        matmul_tn(first, query_grad),
        matmul_tn(first, key_grad),
        matmul_tn(first, value_grad),
        o_grad,
        up_grad,
        down_grad,
    )
    vector_grads = (
        jnp.sum(first_grad * normed_one, axis=0),
        jnp.sum(first_grad, axis=0),
        jnp.sum(query_grad, axis=0, dtype=jnp.float32),
        jnp.sum(value_grad, axis=0, dtype=jnp.float32),
        jnp.sum(middle_bf, axis=0, dtype=jnp.float32),
        jnp.sum(second_grad * normed_two, axis=0),
        jnp.sum(second_grad, axis=0),
        jnp.sum(upper_grad, axis=0, dtype=jnp.float32),
        jnp.sum(out_grad, axis=0),
    )
    return (input_grad.astype(jnp.bfloat16), matrices, vector_grads)


def split_heads_body(
    images,
    live,
    cotangent,
    ln1_gain,
    ln1_bias,
    q_weight,
    q_bias,
    k_weight,
    v_weight,
    v_bias,
    o_weight,
    o_bias,
    ln2_gain,
    ln2_bias,
    fc1_weight,
    fc1_bias,
    fc2_weight,
    fc2_bias,
):
    tensor_count = lax.axis_size("tensor")
    tensor_rank = lax.axis_index("tensor")
    length = images.shape[1]
    full_width = images.shape[2]
    part_width = full_width // tensor_count
    feature_start = tensor_rank * part_width
    head_width = q_bias.shape[0] // tensor_count
    head_start = tensor_rank * head_width
    unit_width = fc1_bias.shape[0] // tensor_count
    unit_start = tensor_rank * unit_width
    row_count = SLOTS * length
    row_share = (row_count + tensor_count - 1) // tensor_count
    padded_rows = row_share * tensor_count
    sizes_info = (SLOTS, length, row_count, padded_rows)
    q_shift = lax.dynamic_slice_in_dim(q_bias, head_start, head_width, 0)
    v_shift = lax.dynamic_slice_in_dim(v_bias, head_start, head_width, 0)
    up_shift = lax.dynamic_slice_in_dim(fc1_bias, unit_start, unit_width, 0)
    gain_one, shift_one, o_shift, gain_two, shift_two, down_shift = tuple(
        (
            lax.dynamic_slice_in_dim(vector, feature_start, part_width, 0)
            for vector in (ln1_gain, ln1_bias, o_bias, ln2_gain, ln2_bias, fc2_bias)
        )
    )
    vectors = (
        gain_one,
        shift_one,
        q_shift,
        v_shift,
        o_shift,
        gain_two,
        shift_two,
        up_shift,
        down_shift,
    )
    q_low = q_weight.astype(jnp.bfloat16)
    k_low = k_weight.astype(jnp.bfloat16)
    v_low = v_weight.astype(jnp.bfloat16)
    o_low = o_weight.astype(jnp.bfloat16)
    up_low = fc1_weight.astype(jnp.bfloat16)
    down_low = fc2_weight.astype(jnp.bfloat16)
    slot_mask = live.astype(jnp.float32)
    outputs = []
    input_grads = []
    matrix_sums = None
    vector_sums = None
    for micro_batch in range(MB):
        slot_start = micro_batch * SLOTS
        batch_tokens = images[slot_start : slot_start + SLOTS].reshape(row_count, full_width)
        batch_cot = cotangent[slot_start : slot_start + SLOTS].reshape(row_count, full_width)
        mask_rows = jnp.broadcast_to(
            slot_mask[slot_start : slot_start + SLOTS, None], (SLOTS, length)
        ).reshape(-1, 1)
        stream = lax.dynamic_slice_in_dim(batch_tokens, feature_start, part_width, 1).astype(
            jnp.float32
        )
        cot_stream = lax.dynamic_slice_in_dim(batch_cot, feature_start, part_width, 1)
        forward_weights = (
            lax.all_gather(q_low, "fsdp", axis=0, tiled=True),
            lax.all_gather(k_low, "fsdp", axis=0, tiled=True),
            lax.all_gather(v_low, "fsdp", axis=0, tiled=True),
            lax.all_gather(o_low, "fsdp", axis=1, tiled=True),
            lax.all_gather(up_low, "fsdp", axis=0, tiled=True),
            lax.all_gather(down_low, "fsdp", axis=1, tiled=True),
        )
        output, kept_state = forward_pass(stream, mask_rows, forward_weights, vectors, sizes_info)
        backward_weights = (
            lax.all_gather(q_low, "fsdp", axis=0, tiled=True),
            lax.all_gather(k_low, "fsdp", axis=0, tiled=True),
            lax.all_gather(v_low, "fsdp", axis=0, tiled=True),
            lax.all_gather(o_low, "fsdp", axis=1, tiled=True),
            lax.all_gather(up_low, "fsdp", axis=0, tiled=True),
            lax.all_gather(down_low, "fsdp", axis=1, tiled=True),
        )
        grad_in, matrices, vector_grads = backward_pass(
            cot_stream, mask_rows, backward_weights, vectors, kept_state, sizes_info
        )
        whole_out, whole_grad = (
            lax.all_gather(output, "tensor", axis=1, tiled=True),
            lax.all_gather(grad_in, "tensor", axis=1, tiled=True),
        )
        outputs.append(whole_out.reshape(SLOTS, length, full_width))
        input_grads.append(whole_grad.reshape(SLOTS, length, full_width))
        vector_sums = (
            vector_grads
            if vector_sums is None
            else jax.tree.map(jnp.add, vector_sums, vector_grads)
        )
        matrix_sums = (
            matrices if matrix_sums is None else jax.tree.map(jnp.add, matrix_sums, matrices)
        )
    total_wq, total_wk, total_wv, total_wo, total_up, total_down = matrix_sums
    shard_wq, shard_wk, shard_wv, shard_wo, shard_up, shard_down = (
        lax.psum_scatter(
            total_wq.astype(jnp.bfloat16), "fsdp", scatter_dimension=0, tiled=True
        ).astype(jnp.float32),
        lax.psum_scatter(
            total_wk.astype(jnp.bfloat16), "fsdp", scatter_dimension=0, tiled=True
        ).astype(jnp.float32),
        lax.psum_scatter(
            total_wv.astype(jnp.bfloat16), "fsdp", scatter_dimension=0, tiled=True
        ).astype(jnp.float32),
        lax.psum_scatter(
            total_wo.astype(jnp.bfloat16), "fsdp", scatter_dimension=1, tiled=True
        ).astype(jnp.float32),
        lax.psum_scatter(
            total_up.astype(jnp.bfloat16), "fsdp", scatter_dimension=0, tiled=True
        ).astype(jnp.float32),
        lax.psum_scatter(
            total_down.astype(jnp.bfloat16), "fsdp", scatter_dimension=1, tiled=True
        ).astype(jnp.float32),
    )
    final_wq, final_wk, final_wv, final_wo, final_up, final_down = (
        lax.psum(shard_wq.astype(jnp.bfloat16), "replica").astype(jnp.float32),
        lax.psum(shard_wk.astype(jnp.bfloat16), "replica").astype(jnp.float32),
        lax.psum(shard_wv.astype(jnp.bfloat16), "replica").astype(jnp.float32),
        lax.psum(shard_wo.astype(jnp.bfloat16), "replica").astype(jnp.float32),
        lax.psum(shard_up.astype(jnp.bfloat16), "replica").astype(jnp.float32),
        lax.psum(shard_down.astype(jnp.bfloat16), "replica").astype(jnp.float32),
    )
    (
        sum_gain_one,
        sum_shift_one,
        sum_q_shift,
        sum_v_shift,
        sum_o_shift,
        sum_gain_two,
        sum_shift_two,
        sum_up_shift,
        sum_down_shift,
    ) = vector_sums
    summed = lax.psum(
        (
            sum_gain_one,
            sum_shift_one,
            sum_q_shift,
            sum_v_shift,
            sum_o_shift,
            sum_gain_two,
            sum_shift_two,
            sum_up_shift,
            sum_down_shift,
        ),
        ("replica", "fsdp"),
    )
    (
        grad_gain_one,
        grad_shift_one,
        grad_q_shift,
        grad_v_shift,
        grad_o_shift,
        grad_gain_two,
        grad_shift_two,
        grad_up_shift,
        grad_down_shift,
    ) = summed
    return (
        jnp.concatenate(outputs, axis=0),
        jnp.concatenate(input_grads, axis=0),
        grad_gain_one,
        grad_shift_one,
        final_wq,
        grad_q_shift,
        final_wk,
        final_wv,
        grad_v_shift,
        final_wo,
        grad_o_shift,
        grad_gain_two,
        grad_shift_two,
        final_up,
        grad_up_shift,
        final_down,
        grad_down_shift,
    )


WINDOW = 256
LANES = 128
SHIFT = 64
VMEM = 60 * 2**20
GELU = 0.7978845608
EVERY = ("tensor", "fsdp", "replica")


def ceil_to(value, step):
    return -(-value // step) * step


def call(kernel, name, grid, scalars, ins, outs, flops=0, scratch=(), aliases=None):
    total = sum(array.size * array.dtype.itemsize for array, _ in ins)
    return pl.pallas_call(
        kernel,
        grid_spec=pltpu.PrefetchScalarGridSpec(
            num_scalar_prefetch=1,
            grid=grid,
            in_specs=[spec for _, spec in ins],
            out_specs=[spec for _, _, spec in outs],
            scratch_shapes=list(scratch),
        ),
        out_shape=[jax.ShapeDtypeStruct(shape, dtype) for shape, dtype, _ in outs],
        input_output_aliases=aliases or {},
        compiler_params=pltpu.CompilerParams(vmem_limit_bytes=VMEM),
        cost_estimate=pl.CostEstimate(flops=flops, bytes_accessed=total, transcendentals=0),
        name=name,
    )(scalars, *(array for array, _ in ins))


def fixed(shape, index):
    return pl.BlockSpec(shape, index, pipeline_mode=pl.Buffered(1))


def head_window(offset, base, rows):
    start = (offset + base) // LANES * LANES
    lane = lax.broadcasted_iota(jnp.int32, (rows, WINDOW), 1) + start
    inside = (lane >= offset + base) & (lane < offset + base + HEAD)
    return pl.ds(pl.multiple_of(start, LANES), WINDOW), inside


def attention(qvk, length, rows, width, group):
    heads = width // HEAD
    count = qvk.shape[0] // rows
    steps = heads // group
    out_width = ceil_to(width + SHIFT, WINDOW)

    def kernel(none_ref, qvk_ref, mixed_ref, probs_ref):
        @pl.when(pl.program_id(1) == 0)
        def _():
            mixed_ref[...] = jnp.zeros_like(mixed_ref)

        real = lax.broadcasted_iota(jnp.int32, (rows, rows), 1) < length

        def head(item):
            return (pl.program_id(1) * group + item) * HEAD

        def scores_of(item):
            at_q, _ = head_window(head(item), 0, rows)
            at_k, in_k = head_window(head(item), 2 * width, rows)
            key_rows = jnp.where(in_k, qvk_ref[:, at_k], 0)
            return jnp.where(real, matmul_nt(qvk_ref[:, at_q], key_rows), -1e30)

        following = scores_of(0)
        for item in range(group):
            scores = following
            if item + 1 < group:
                following = scores_of(item + 1)
            at_v, in_v = head_window(head(item), width, rows)
            at_o, in_o = head_window(head(item), SHIFT, rows)
            value_rows = jnp.where(in_v, qvk_ref[:, at_v], 0)
            powers = jnp.exp(scores - jnp.max(scores, axis=1, keepdims=True))
            total = jnp.sum(powers, axis=1, keepdims=True)
            probs = (powers * (1.0 / total)).astype(jnp.bfloat16)
            probs_ref[item] = probs
            mixed = matmul(probs, value_rows).astype(jnp.bfloat16)
            mixed_ref[:, at_o] = jnp.where(in_o, mixed, mixed_ref[:, at_o])

    return call(
        kernel,
        "attention",
        (count, steps),
        jnp.zeros((1,), jnp.int32),
        [(qvk, pl.BlockSpec((rows, qvk.shape[1]), lambda i, g, s: (i, 0)))],
        [
            ((count * rows, out_width), jnp.bfloat16, pl.BlockSpec((rows, out_width), lambda i, g, s: (i, 0))),
            (
                (count * heads, rows, rows),
                jnp.bfloat16,
                pl.BlockSpec((group, rows, rows), lambda i, g, s: (i * steps + g, 0, 0)),
            ),
        ],
        flops=4 * count * heads * rows * rows * WINDOW,
    )


def attention_back(qvk, mixed, grad, probs, images, kept, rows, width, group):
    heads = width // HEAD
    steps = heads // group
    at = images.start
    count = len(images)

    def kernel(none_ref, qvk_ref, mixed_ref, grad_ref, probs_ref, *refs):
        out_ref, sums_ref = refs[-2:]

        @pl.when(pl.program_id(1) == 0)
        def _():
            out_ref[...] = jnp.zeros_like(out_ref)

        for item in range(group):
            offset = (pl.program_id(1) * group + item) * HEAD
            at_q, in_q = head_window(offset, 0, rows)
            at_v, in_v = head_window(offset, width, rows)
            at_k, in_k = head_window(offset, 2 * width, rows)
            at_o, in_o = head_window(offset, SHIFT, rows)
            grad = jnp.where(in_o, grad_ref[:, at_o], 0)
            query_rows = jnp.where(in_q, qvk_ref[:, at_q], 0)
            key_rows = jnp.where(in_k, qvk_ref[:, at_k], 0)
            probs = probs_ref[item]
            row_dot = jnp.sum(
                grad.astype(jnp.float32) * mixed_ref[:, at_o].astype(jnp.float32), axis=1, keepdims=True
            )
            prob_grad = matmul_nt(grad, qvk_ref[:, at_v])
            score_grad = (probs.astype(jnp.float32) * (prob_grad - row_dot)).astype(jnp.bfloat16)
            value_grad = matmul_tn(probs, grad).astype(jnp.bfloat16)
            query_grad = (matmul(score_grad, key_rows) * HEAD ** (-0.5)).astype(jnp.bfloat16)
            key_grad = matmul_tn(score_grad, query_rows).astype(jnp.bfloat16)
            out_ref[:, at_q] = jnp.where(in_q, query_grad, out_ref[:, at_q])
            out_ref[:, at_v] = jnp.where(in_v, value_grad, out_ref[:, at_v])
            out_ref[:, at_k] = jnp.where(in_k, key_grad, out_ref[:, at_k])

        @pl.when(pl.program_id(1) == steps - 1)
        def _():
            total = jnp.sum(out_ref[...].astype(jnp.float32), axis=0, keepdims=True)
            sums_ref[0] = jnp.broadcast_to(total, sums_ref.shape[1:])

    ins = [
        (qvk, pl.BlockSpec((rows, qvk.shape[1]), lambda i, g, s: (at + i, 0))),
        (mixed, pl.BlockSpec((rows, mixed.shape[1]), lambda i, g, s: (at + i, 0))),
        (grad, pl.BlockSpec((rows, mixed.shape[1]), lambda i, g, s: (at + i, 0))),
        (probs, pl.BlockSpec((group, rows, rows), lambda i, g, s: ((at + i) * steps + g, 0, 0))),
    ]
    if kept is not None:
        ins.append((kept, pl.BlockSpec(memory_space=pl.ANY)))
    grads, sums = call(
        kernel,
        "attention_back",
        (count, steps),
        jnp.zeros((1,), jnp.int32),
        ins,
        [
            (qvk.shape, jnp.bfloat16, pl.BlockSpec((rows, qvk.shape[1]), lambda i, g, s: (at + i, 0))),
            ((count, 8, qvk.shape[1]), jnp.float32, pl.BlockSpec((1, 8, qvk.shape[1]), lambda i, g, s: (i, 0, 0))),
        ],
        aliases=None if kept is None else {5: 0},
        flops=8 * count * heads * rows * rows * WINDOW,
    )
    return grads, jnp.sum(sums[:, 0], axis=0)


def place(pieces, slots, total):
    def kernel(slots_ref, *refs):
        at = 0
        for ref in refs[:-1]:
            for block in range(ref.shape[0]):
                refs[-1][pl.ds(slots_ref[at], 1)] = ref[block : block + 1]
                at += 1

    def whole(shape):
        return fixed(shape, lambda i, s: (0, 0, 0))

    shape = (total, *pieces[0].shape[1:])
    return call(
        kernel,
        "place",
        (1,),
        jnp.stack([slot for group in slots for slot in group]).astype(jnp.int32),
        [(piece, whole(piece.shape)) for piece in pieces],
        [(shape, pieces[0].dtype, whole(shape))],
    )[0]


def outer_sum(left, right, ranks, step, total=None, kept=None, at=None, scalars=None):
    rows, lines = left.shape
    columns = right.shape[1] // ranks
    steps = columns // step
    held = ranks * lines if kept is None else kept.shape[0]

    def kernel(scalars_ref, left_ref, right_ref, *refs):
        refs[-1][...] = matmul_tn(left_ref[...], right_ref[...]).astype(refs[-1].dtype)

    def place_of(t, j, s):
        return (t, j) if kept is None else (s[at[0]], at[1])

    return call(
        kernel,
        "outer_sum",
        (ranks, steps),
        jnp.zeros((1,), jnp.int32) if scalars is None else scalars,
        [
            (left, fixed((rows, lines), lambda t, j, s: (0, 0))),
            (right, pl.BlockSpec((rows, step), lambda t, j, s: (0, t * steps + j))),
        ]
        + ([] if kept is None else [(kept, pl.BlockSpec(memory_space=pl.ANY))]),
        [((held, total or columns), jnp.bfloat16, pl.BlockSpec((lines, step), place_of))],
        flops=2 * rows * lines * columns * ranks,
        aliases=None if kept is None else {3: 0},
    )[0]


def tie(*values):
    return lax.optimization_barrier(values)


def swap(array, axis, bits):
    size = lax.axis_size(axis)
    return lax.ppermute(array, axis, [(rank, rank ^ bits) for rank in range(size)])


def turn(array, axis, steps):
    size = lax.axis_size(axis)
    return lax.ppermute(array, axis, [(rank, (rank + steps) % size) for rank in range(size)])


def replica_bits():
    bit = lax.axis_size("replica") // 2
    bits = []
    while bit:
        bits.append(bit)
        bit //= 2
    return bits


def swap_found(found, bit):
    return {**found, **{bits ^ bit: swap(held, "replica", bit) for bits, held in found.items()}}


def among_replicas(piece):
    found = {0: piece}
    for bit in replica_bits():
        found = swap_found(found, bit)
    return found


def from_lines(shard):
    copies = lax.axis_size("replica")
    blocks = shard.reshape(copies, -1, shard.shape[1])
    mine = lax.dynamic_slice_in_dim(blocks, lax.axis_index("replica"), 1, 0)
    return [mine] + [turn(mine, "fsdp", step) for step in range(1, lax.axis_size("fsdp"))]


def slots_of(found, skip):
    copies, lines = lax.axis_size("replica"), lax.axis_size("fsdp")
    copy, line = lax.axis_index("replica"), lax.axis_index("fsdp")
    starts = [(line - step) % lines * copies for step in range(skip, lines)]
    return [[start + (copy ^ bits) for start in starts] for bits in found]


def gather_own(shard, parts):
    copies, lines, line = lax.axis_size("replica"), lax.axis_size("fsdp"), lax.axis_index("fsdp")
    blocks = shard.reshape(copies, -1, shard.shape[1])
    pieces, slots = [blocks], [[line * copies + at for at in range(copies)]]
    if lines > 1:
        found = among_replicas(jnp.concatenate(parts[1:], axis=0))
        pieces += list(found.values())
        slots += slots_of(found, 1)
    return place(pieces, slots, lines * copies).reshape(-1, shard.shape[1])


def gather_far(parts, rank):
    found = {0: swap(jnp.concatenate(parts, axis=0), "tensor", rank)}
    for bit in replica_bits()[:-1]:
        found = swap_found(found, bit)
    return found


def finish_far(found):
    for bit in replica_bits()[-1:]:
        found = swap_found(found, bit)
    total = lax.axis_size("replica") * lax.axis_size("fsdp")
    whole = place(list(found.values()), slots_of(found, 0), total)
    return whole.reshape(-1, whole.shape[2])


def gather_whole(shard):
    share = shard.shape[0] // lax.axis_size("replica")
    part = lax.dynamic_slice_in_dim(shard, lax.axis_index("replica") * share, share, 0)
    return lax.all_gather(part, EVERY, axis=0, tiled=True)


def add_low(first_term, *terms):
    total = first_term.astype(jnp.float32)
    for term in terms:
        total = total + term.astype(jnp.float32)
    return total.astype(jnp.bfloat16)


def by_lines(term):
    bits = len(replica_bits())
    return term.reshape(lax.axis_size("fsdp"), *(2 for _ in range(bits)), -1, term.shape[1])


def halve(held, bit):
    side = lax.axis_index("replica") // bit % 2
    axis = held.ndim - 3
    keep = lax.dynamic_index_in_dim(held, side, axis, keepdims=False)
    send = lax.dynamic_index_in_dim(held, 1 - side, axis, keepdims=False)
    return add_low(keep, swap(send, "replica", bit))


def sum_lines(held):
    lines, line = lax.axis_size("fsdp"), lax.axis_index("fsdp")
    terms = [lax.dynamic_index_in_dim(held, line, 0, keepdims=True)]
    for step in range(1, lines):
        send = lax.dynamic_index_in_dim(held, (line + step) % lines, 0, keepdims=True)
        terms.append(turn(send, "fsdp", step))
    return add_low(*terms)


def place_cuts(found, cuts):
    copy = lax.axis_index("replica")
    pieces = list(found.values())
    rows = pieces[0].shape[1]

    def kernel(slots_ref, *refs):
        for at in range(len(pieces)):
            values = refs[at][...].astype(jnp.float32)
            for (start, size), out_ref in zip(cuts, refs[len(pieces) :]):
                out_ref[pl.ds(slots_ref[at], 1)] = values[:, :, start : start + size]

    def whole(shape):
        return fixed(shape, lambda i, s: (0, 0, 0))

    shapes = [(len(pieces), rows, size) for _, size in cuts]
    wholes = call(
        kernel,
        "place_cuts",
        (1,),
        jnp.stack([copy ^ bits for bits in found]).astype(jnp.int32),
        [(piece, whole(piece.shape)) for piece in pieces],
        [(shape, jnp.float32, whole(shape)) for shape in shapes],
    )
    return [array.reshape(-1, array.shape[2]) for array in wholes]


def place_found(found):
    copy = lax.axis_index("replica")
    whole = place(list(found.values()), [[copy ^ bits] for bits in found], len(found))
    return whole.reshape(-1, whole.shape[2])


def sum_over(vector, axes):
    size = lax.axis_size(axes)
    terms = [vector] + [
        lax.ppermute(vector, axes, [(rank, rank ^ bits) for rank in range(size)]) for bits in range(1, size)
    ]
    while len(terms) > 1:
        terms = [left + right for left, right in zip(terms[::2], terms[1::2])]
    return terms[0]


def norm_parts(values):
    center = jnp.mean(values, axis=1, keepdims=True)
    spread = jnp.mean(values * values, axis=1, keepdims=True) - center * center
    scale_inv = lax.rsqrt(spread + EPSILON)
    return (values - center) * scale_inv, scale_inv


def norm_backward(grad, normed, scale_inv, gain_vec):
    scaled = grad * gain_vec
    mean_one = jnp.mean(scaled, axis=1, keepdims=True)
    mean_two = jnp.mean(scaled * normed, axis=1, keepdims=True)
    return scale_inv * (scaled - mean_one - normed * mean_two)


def image_body(
    images,
    live,
    cotangent,
    ln1_gain,
    ln1_bias,
    q_weight,
    q_bias,
    k_weight,
    v_weight,
    v_bias,
    o_weight,
    o_bias,
    ln2_gain,
    ln2_bias,
    fc1_weight,
    fc1_bias,
    fc2_weight,
    fc2_bias,
):
    low, full = jnp.bfloat16, jnp.float32
    tensor_count = lax.axis_size("tensor")
    tensor_rank = lax.axis_index("tensor")
    slots, length, wide = images.shape
    count = slots // tensor_count
    rows = ceil_to(length, 32)
    half = rows // 2
    width = q_weight.shape[1]
    units = fc1_weight.shape[1]
    qvk_width = ceil_to(3 * width, WINDOW)
    o_width = ceil_to(width + SHIFT, WINDOW)
    unit_width = ceil_to(units, WINDOW)
    unit_width = ceil_to(unit_width, o_width)
    ranks = range(tensor_count)
    all_rows = count * rows
    heads = width // HEAD
    group = next(size for size in (8, 4, 2, 1) if heads % size == 0)
    blocks = all_rows // half
    scalars = jnp.concatenate(
        [
            jnp.stack([tensor_rank * count] + [tensor_rank ^ rank for rank in ranks]).astype(jnp.int32),
            lax.dynamic_slice_in_dim(live, tensor_rank * count, count, 0),
        ]
    )
    live_at = 1 + tensor_count

    def columns(parts, ahead, total):
        body_part = jnp.concatenate(parts, axis=1)
        return jnp.pad(body_part, ((0, 0), (ahead, total - ahead - body_part.shape[1])))

    def row(vector):
        return vector.reshape(1, -1)

    def slots_spec(first=0):
        return pl.BlockSpec((1, half, wide), lambda i, s: (s[0] + first + i // 2, i % 2, 0))

    def rows_spec(size, first=0):
        return pl.BlockSpec((half, size), lambda i, s: (2 * first + i, 0))

    def vector_spec():
        return pl.BlockSpec((1, wide), lambda i, s: (0, 0))

    def sums_spec():
        return pl.BlockSpec((8, wide), lambda i, s: (0, 0))

    def real_rows(values):
        at = lax.broadcasted_iota(jnp.int32, (half, 1), 0) + pl.program_id(0) % 2 * half
        return jnp.where(at < length, values.astype(full), 0.0)

    def live_slot(scalars_ref, first=0):
        return scalars_ref[live_at + first + pl.program_id(0) // 2].astype(full)

    def add_sums(sums_ref, *terms):
        @pl.when(pl.program_id(0) == 0)
        def _():
            sums_ref[...] = jnp.zeros_like(sums_ref)

        for at, term in enumerate(terms):
            sums_ref[at : at + 1] += jnp.sum(term, axis=0, keepdims=True)

    def product(part_refs, weight_refs):
        total = matmul_nt(part_refs[0][...], weight_refs[0][...])
        for part_ref, weight_ref in zip(part_refs[1:], weight_refs[1:]):
            total = total + matmul_nt(part_ref[...], weight_ref[...])
        return total

    qvk_shard = columns([w.astype(low) for w in (q_weight, v_weight, k_weight)], 0, qvk_width)
    parts = from_lines(qvk_shard)

    def first_kernel(scalars_ref, images_ref, cot_ref, gain_ref, shift_ref, first_ref, grad_ref, sums_ref):
        normed, _ = norm_parts(real_rows(images_ref[0]))
        first_ref[...] = (normed * gain_ref[...] + shift_ref[...]).astype(low)
        grad = real_rows(cot_ref[0]) * live_slot(scalars_ref)
        grad_ref[...] = grad.astype(low)
        add_sums(sums_ref, grad)

    first, out_grad, first_sums = call(
        first_kernel,
        "first_norm",
        (blocks,),
        scalars,
        [(images, slots_spec()), (cotangent, slots_spec()), (row(ln1_gain), vector_spec()), (row(ln1_bias), vector_spec())],
        [
            ((all_rows, wide), low, rows_spec(wide)),
            ((all_rows, wide), low, rows_spec(wide)),
            ((8, wide), full, sums_spec()),
        ],
    )

    parts, first, out_grad = tie(parts, first, out_grad)
    up_o_shard = jnp.concatenate(
        [
            columns([fc1_weight.astype(low)], 0, unit_width),
            columns([o_weight.astype(low).T], SHIFT, o_width),
        ],
        axis=1,
    )
    down_shard = columns([fc2_weight.astype(low).T], 0, unit_width)
    up_o_shard, down_shard, parts = tie(up_o_shard, down_shard, parts)
    up_o_whole = gather_whole(up_o_shard)
    down_whole = gather_whole(down_shard)
    qvk_weights = [gather_own(qvk_shard, parts)]
    far_parts = [gather_far(parts, rank) for rank in ranks[1:]]

    def of_rank(vector, rank, size):
        return lax.dynamic_slice_in_dim(vector, (tensor_rank ^ rank) * size, size, 0)

    scale_row = jnp.where(jnp.arange(qvk_width) < width, HEAD ** (-0.5), 1.0)
    qvk, mixed, probs = [], [], []
    for rank in ranks:
        shift_row = jnp.pad(
            jnp.concatenate([of_rank(q_bias, rank, width), of_rank(v_bias, rank, width)]),
            (0, qvk_width - 2 * width),
        )
        qvk.append(((matmul(first, qvk_weights[rank]) + shift_row) * scale_row).astype(low))
        mixed_part, probs_part = attention(qvk[rank], length, rows, width, group)
        if rank == 0:
            mixed_part, first, far_parts = tie(mixed_part, first, far_parts)
            qvk_weights += [finish_far(found) for found in far_parts]
        mixed.append(mixed_part)
        probs.append(probs_part)

    def o_spec(rank):
        return fixed((wide, o_width), lambda i, s: (s[1 + rank], unit_width // o_width))

    def middle_kernel(scalars_ref, *refs):
        images_ref, bias_ref, gain_ref, shift_ref, middle_ref, second_ref = refs[2 * tensor_count :]
        total = product(refs[:tensor_count], refs[tensor_count : 2 * tensor_count])
        middle = real_rows(images_ref[0]) + (total + bias_ref[...])
        middle_ref[...] = middle
        normed, _ = norm_parts(middle)
        second_ref[...] = (normed * gain_ref[...] + shift_ref[...]).astype(low)

    middle, second = call(
        middle_kernel,
        "middle_norm",
        (blocks,),
        scalars,
        [(part, rows_spec(o_width)) for part in mixed]
        + [(up_o_whole, o_spec(rank)) for rank in ranks]
        + [
            (images, slots_spec()),
            (row(o_bias), vector_spec()),
            (row(ln2_gain), vector_spec()),
            (row(ln2_bias), vector_spec()),
        ],
        [((all_rows, wide), full, rows_spec(wide)), ((all_rows, wide), low, rows_spec(wide))],
        flops=2 * all_rows * wide * o_width * tensor_count,
    )

    chunk = o_width

    def unit_rows():
        return pl.BlockSpec((half, unit_width), lambda t, i, s: (i, t))

    def unit_weights():
        return pl.BlockSpec((wide, unit_width), lambda t, i, s: (t, 0))

    def hidden_kernel(scalars_ref, second_ref, weight_ref, shift_ref, hidden_ref, slope_ref):
        for start in range(0, unit_width, chunk):
            at = slice(start, start + chunk)
            upper = matmul(second_ref[...], weight_ref[:, at]) + shift_ref[:, at]
            square = upper * upper
            share = 0.5 + 0.5 * jnp.tanh(upper * (GELU + GELU * 0.044715 * square))
            hidden = upper * share
            slope = share + (hidden - hidden * share) * (2 * GELU + 6 * GELU * 0.044715 * square)
            hidden_ref[:, at] = hidden.astype(low)
            slope_ref[:, at] = slope.astype(low)

    unit_shift = jnp.pad(
        fc1_bias.reshape(tensor_count, units), ((0, 0), (0, unit_width - units))
    ).reshape(1, -1)
    hidden, slopes = call(
        hidden_kernel,
        "hidden",
        (tensor_count, blocks),
        scalars,
        [
            (second, pl.BlockSpec((half, wide), lambda t, i, s: (i, 0))),
            (up_o_whole, unit_weights()),
            (unit_shift, pl.BlockSpec((1, unit_width), lambda t, i, s: (0, t))),
        ],
        [((all_rows, tensor_count * unit_width), low, unit_rows())] * 2,
        flops=2 * all_rows * wide * unit_width * tensor_count,
    )
    down_terms = outer_sum(out_grad, hidden, tensor_count, chunk)
    down_terms, hidden = tie(down_terms, hidden)
    down_share = lax.psum_scatter(down_terms, EVERY, scatter_dimension=0, tiled=True)

    def weight_spec(rank):
        return fixed((wide, unit_width), lambda i, s: (rank, 0))

    def unit_spec(rank):
        return pl.BlockSpec((half, unit_width), lambda i, s: (i, rank))

    def output_kernel(scalars_ref, *refs):
        middle_ref, bias_ref, output_ref, whole_ref = refs[2 * tensor_count :]
        total = product(refs[:tensor_count], refs[tensor_count : 2 * tensor_count])
        result = middle_ref[...] + (total + bias_ref[...])
        output_ref[0] = (result * live_slot(scalars_ref)).astype(low)
        whole_ref[0] = output_ref[0]

    output, out_whole = call(
        output_kernel,
        "output",
        (blocks,),
        scalars,
        [(hidden, unit_spec(rank)) for rank in ranks]
        + [(down_whole, weight_spec(rank)) for rank in ranks]
        + [(middle, rows_spec(wide)), (row(fc2_bias), vector_spec())],
        [
            ((count, length, wide), low, pl.BlockSpec((1, half, wide), lambda i, s: (i // 2, i % 2, 0))),
            ((slots, length, wide), low, slots_spec()),
        ],
        flops=2 * all_rows * wide * unit_width * tensor_count,
    )

    def trade(part):
        return [swap(part, "tensor", rank) for rank in ranks[1:]]

    def trade_halves(part):
        return [trade(piece) for piece in part]

    def lay_halves(whole, parts, first):
        for rank, *pieces in zip(ranks[1:], *parts):
            for at, piece in enumerate(pieces):
                start = ((tensor_rank ^ rank) * count + first, at * half, 0)
                whole = lax.dynamic_update_slice(whole, piece, start)
        return whole

    def lay(whole, parts, first):
        for rank, part in zip(ranks[1:], parts):
            whole = lax.dynamic_update_slice_in_dim(whole, part, (tensor_rank ^ rank) * count + first, 0)
        return whole

    output, out_grad = tie(output, out_grad)
    out_parts = trade(output)

    def hidden_back_kernel(scalars_ref, grad_ref, weight_ref, slope_ref, upper_ref, sums_ref):
        @pl.when(pl.program_id(1) == 0)
        def _():
            sums_ref[...] = jnp.zeros_like(sums_ref)

        for start in range(0, unit_width, chunk):
            at = slice(start, start + chunk)
            upper = matmul(grad_ref[...], weight_ref[:, at]) * slope_ref[:, at].astype(full)
            rounded = upper.astype(low)
            upper_ref[:, at] = rounded
            sums_ref[0:1, at] += jnp.sum(rounded.astype(full), axis=0, keepdims=True)

    upper_grads, upper_sums = call(
        hidden_back_kernel,
        "hidden_back",
        (tensor_count, blocks),
        scalars,
        [
            (out_grad, pl.BlockSpec((half, wide), lambda t, i, s: (i, 0))),
            (down_whole, unit_weights()),
            (slopes, unit_rows()),
        ],
        [
            ((all_rows, tensor_count * unit_width), low, unit_rows()),
            ((8, tensor_count * unit_width), full, pl.BlockSpec((8, unit_width), lambda t, i, s: (0, t))),
        ],
        flops=2 * all_rows * wide * unit_width * tensor_count,
    )
    up_terms = outer_sum(second, upper_grads, tensor_count, o_width, unit_width + o_width)
    up_terms, upper_grads = tie(up_terms, upper_grads)

    def middle_back_kernel(scalars_ref, *refs):
        middle_ref, grad_ref, gain_ref, *o_refs = refs[2 * tensor_count : 3 * tensor_count + 3]
        middle_grad_ref, low_ref, sums_ref, *mixed_grad_refs = refs[3 * tensor_count + 3 :]
        total = product(refs[:tensor_count], refs[tensor_count : 2 * tensor_count])
        normed, scale_inv = norm_parts(middle_ref[...])
        middle_grad = grad_ref[...].astype(full) + norm_backward(total, normed, scale_inv, gain_ref[...])
        middle_grad_ref[...] = middle_grad
        rounded = middle_grad.astype(low)
        low_ref[...] = rounded
        for o_ref, mixed_grad_ref in zip(o_refs, mixed_grad_refs):
            mixed_grad_ref[...] = matmul(rounded, o_ref[...]).astype(low)
        add_sums(sums_ref, total * normed, total, rounded.astype(full))

    middle_grad, middle_low, second_sums, *mixed_grads = call(
        middle_back_kernel,
        "middle_back",
        (blocks,),
        scalars,
        [(upper_grads, unit_spec(rank)) for rank in ranks]
        + [(up_o_whole, weight_spec(rank)) for rank in ranks]
        + [(middle, rows_spec(wide)), (out_grad, rows_spec(wide)), (row(ln2_gain), vector_spec())]
        + [(up_o_whole, o_spec(rank)) for rank in ranks],
        [
            ((all_rows, wide), full, rows_spec(wide)),
            ((all_rows, wide), low, rows_spec(wide)),
            ((8, wide), full, sums_spec()),
        ]
        + [((all_rows, o_width), low, rows_spec(o_width)) for rank in ranks],
        flops=2 * all_rows * wide * (unit_width + o_width) * tensor_count,
    )

    for rank in ranks:
        up_terms = outer_sum(
            middle_low,
            mixed[rank],
            1,
            o_width,
            unit_width + o_width,
            up_terms,
            (1 + rank, unit_width // o_width),
            scalars,
        )
    up_terms, mixed_grads[-1], out_parts = tie(up_terms, mixed_grads[-1], out_parts)
    up_share = lax.psum_scatter(up_terms, EVERY, scatter_dimension=0, tiled=True)
    bits = replica_bits()[::-1]

    def back(rank, which, kept):
        return attention_back(
            qvk[rank], mixed[rank], mixed_grads[rank], probs[rank], which, kept, rows, width, group
        )

    def first_back_kernel(scalars_ref, *refs):
        images_ref, grad_ref, gain_ref = refs[2 * tensor_count : 2 * tensor_count + 3]
        upper_ref, lower_ref, whole_ref, sums_ref = refs[-4:]
        total = product(refs[:tensor_count], refs[tensor_count : 2 * tensor_count])
        normed, scale_inv = norm_parts(real_rows(images_ref[0]))
        grad = grad_ref[...] + norm_backward(total, normed, scale_inv, gain_ref[...])
        whole_ref[0] = grad.astype(low)

        @pl.when(pl.program_id(0) == 0)
        def _():
            upper_ref[...] = whole_ref[...]

        @pl.when(pl.program_id(0) == 1)
        def _():
            lower_ref[...] = whole_ref[:, : length - half]

        add_sums(sums_ref, total * normed, total)

    qvk_grads, qvk_sums = [None] * tensor_count, [0.0] * tensor_count
    input_whole = None
    third_sums = 0.0
    in_parts = []

    def attend(rank, which):
        qvk_grads[rank], sums = back(rank, which, qvk_grads[rank])
        qvk_sums[rank] = qvk_sums[rank] + sums

    def first_back(slot, whole):
        ahead = [] if whole is None else [(whole, pl.BlockSpec(memory_space=pl.ANY))]
        upper, lower, whole, sums = call(
            first_back_kernel,
            "first_back",
            (2,),
            scalars,
            [(grads, rows_spec(qvk_width, slot)) for grads in qvk_grads]
            + [(weight, fixed((wide, qvk_width), lambda i, s: (0, 0))) for weight in qvk_weights]
            + [(images, slots_spec(slot)), (middle_grad, rows_spec(wide, slot)), (row(ln1_gain), vector_spec())]
            + ahead,
            [
                ((1, half, wide), low, pl.BlockSpec((1, half, wide), lambda i, s: (0, 0, 0))),
                ((1, length - half, wide), low, pl.BlockSpec((1, length - half, wide), lambda i, s: (0, 0, 0))),
                ((slots, length, wide), low, slots_spec(slot)),
                ((8, wide), full, sums_spec()),
            ],
            aliases={2 * tensor_count + 4: 2} if ahead else None,
            flops=2 * rows * wide * qvk_width * tensor_count,
        )
        return (upper, lower), whole, sums

    last = count - 1

    def halve_all(terms, which):
        for bit in which:
            terms = [halve(term, bit) for term in terms]
        return terms

    def join_on(found, which):
        for bit in which:
            found = swap_found(found, bit)
        return found

    far_bits, far_bit = replica_bits()[:-1], replica_bits()[-1:]

    down_found = join_on({0: down_share[None]}, far_bits)
    for rank in ranks[1:]:
        attend(rank, range(count))
    qvk_grads[1:], mixed_grads[0], down_found, first = tie(qvk_grads[1:], mixed_grads[0], down_found, first)
    far = [by_lines(outer_sum(first, grads, 1, qvk_width // 2)) for grads in qvk_grads[1:]]
    down_grads = place_found(join_on(down_found, far_bit))
    far, mixed_grads[0], down_grads = tie(far, mixed_grads[0], down_grads)
    far_done = 0
    for slot in range(last):
        if slot > 0:
            in_parts.append(trade_halves(input_grad))
        attend(0, range(slot, slot + 1))
        if slot == 0:
            far = halve_all(far, bits[:1])
            far, qvk_grads[0] = tie(far, qvk_grads[0])
        elif far_done == 1:
            far = halve_all(far, bits[1:])
        far_done += 1
        input_grad, input_whole, sums = first_back(slot, input_whole)
        third_sums = third_sums + sums
        far, input_grad, mixed_grads[0] = tie(far, input_grad, mixed_grads[0])
        if slot > 0:
            in_parts[-1][0], input_grad, mixed_grads[0] = tie(in_parts[-1][0], input_grad, mixed_grads[0])
    if last > 0:
        in_parts.append(trade_halves(input_grad))
    attend(0, range(last, count))
    near = by_lines(outer_sum(first, qvk_grads[0], 1, qvk_width // 2))
    if far_done < 2:
        far = halve_all(far, bits[far_done:])
    near, far, in_parts[:-1], qvk_grads[0] = tie(near, far, in_parts[:-1], qvk_grads[0])
    if last > 0:
        in_parts[-1][0], near, qvk_grads[0] = tie(in_parts[-1][0], near, qvk_grads[0])
    near = halve_all([near], bits[:1])
    near, qvk_grads[0], far, up_share = tie(near, qvk_grads[0], far, up_share)
    input_grad, input_whole, sums = first_back(last, input_whole)
    near = halve_all(near, bits[1:])
    far = [sum_lines(held) for held in far]
    (
        near,
        far,
        input_grad,
        input_whole,
        sums,
        third_sums,
        qvk_sums,
        first_sums,
        second_sums,
        upper_sums,
        out_whole,
        out_parts,
        down_grads,
        up_share,
        in_parts,
    ) = tie(
        near,
        far,
        input_grad,
        input_whole,
        sums,
        third_sums,
        qvk_sums,
        first_sums,
        second_sums,
        upper_sums,
        out_whole,
        out_parts,
        down_grads,
        up_share,
        in_parts,
    )
    third_sums = third_sums + sums
    in_parts.append(trade_halves(input_grad))
    lower = in_parts[-1][1]
    out_whole = lay(out_whole, out_parts, 0)
    for slot in range(last - 1):
        input_whole = lay_halves(input_whole, in_parts[slot], slot)
    up_found = join_on({0: up_share[None]}, far_bits)
    near_total = add_low(
        sum_lines(near[0]), *(swap(term, "tensor", rank) for rank, term in zip(ranks[1:], far))
    )
    (
        near_total,
        in_parts,
        up_found,
        out_whole,
        input_whole,
        third_sums,
        qvk_sums,
        first_sums,
        second_sums,
        upper_sums,
        down_grads,
    ) = tie(
        near_total,
        [*in_parts[:-1], in_parts[-1][:1]],
        up_found,
        out_whole,
        input_whole,
        third_sums,
        qvk_sums,
        first_sums,
        second_sums,
        upper_sums,
        down_grads,
    )
    in_parts[-1].append(lower)
    for slot in range(max(last - 1, 0), last):
        input_whole = lay_halves(input_whole, in_parts[slot], slot)
    near_found = among_replicas(near_total)
    up_grads, o_grads = place_cuts(
        join_on(up_found, far_bit), [(0, units), (unit_width + SHIFT, width)]
    )

    def all_ranks(parts, size):
        whole = jnp.zeros((tensor_count * size,), full)
        for rank in ranks:
            whole = lax.dynamic_update_slice_in_dim(whole, parts[rank], (tensor_rank ^ rank) * size, 0)
        return whole

    vectors = [
        third_sums[0],
        third_sums[1],
        all_ranks([sums[:width] for sums in qvk_sums], width),
        all_ranks([sums[width : 2 * width] for sums in qvk_sums], width),
        second_sums[2],
        second_sums[0],
        second_sums[1],
        upper_sums[0].reshape(tensor_count, unit_width)[:, :units].reshape(-1),
        first_sums[0],
    ]
    sizes = [vector.shape[0] for vector in vectors]
    joined = jnp.concatenate(vectors)
    padded = ceil_to(joined.shape[0], 8 * LANES)
    summed = jnp.pad(joined, (0, padded - joined.shape[0])).reshape(-1, LANES)
    summed = sum_over(summed, "replica")
    near_found, summed = tie(near_found, summed)
    summed = sum_over(summed, "fsdp")
    summed, in_parts[-1][1] = tie(summed, in_parts[-1][1])
    summed = sum_over(summed, "tensor").reshape(-1)
    q_grads, v_grads, k_grads = place_cuts(near_found, [(at * width, width) for at in range(3)])
    input_whole = lay_halves(input_whole, in_parts[-1], last)
    ends, start = [], 0
    for size in sizes:
        share = size // tensor_count
        ends.append(lax.dynamic_slice_in_dim(summed, start + tensor_rank * share, share, 0))
        start += size
    gain_one, shift_one, q_sum, v_sum, o_sum, gain_two, shift_two, up_sum, down_sum = ends
    return (
        out_whole,
        input_whole,
        gain_one,
        shift_one,
        q_grads,
        q_sum,
        k_grads,
        v_grads,
        v_sum,
        o_grads.T,
        o_sum,
        gain_two,
        shift_two,
        up_grads,
        up_sum,
        down_grads[:, :units].astype(full).T,
        down_sum,
    )


def halves(size):
    return size & (size - 1) == 0


def by_images(mesh):
    return SLOTS * MB % mesh.shape["tensor"] == 0 and all(halves(size) for size in mesh.shape.values())


def solution(mesh):
    in_specs = (
        P(("replica", "fsdp"), None, None),
        P(("replica", "fsdp")),
        P(("replica", "fsdp"), None, None),
        P(),
        P(),
        P("fsdp", "tensor"),
        P(),
        P("fsdp", "tensor"),
        P("fsdp", "tensor"),
        P(),
        P("tensor", "fsdp"),
        P(),
        P(),
        P(),
        P("fsdp", "tensor"),
        P(),
        P("tensor", "fsdp"),
        P(),
    )
    out_specs = (
        P(("replica", "fsdp"), None, None),
        P(("replica", "fsdp"), None, None),
        P("tensor"),
        P("tensor"),
        P("fsdp", "tensor"),
        P("tensor"),
        P("fsdp", "tensor"),
        P("fsdp", "tensor"),
        P("tensor"),
        P("tensor", "fsdp"),
        P("tensor"),
        P("tensor"),
        P("tensor"),
        P("fsdp", "tensor"),
        P("tensor"),
        P("tensor", "fsdp"),
        P("tensor"),
    )
    body = image_body if by_images(mesh) else split_heads_body
    return jax.shard_map(body, mesh=mesh, in_specs=in_specs, out_specs=out_specs, check_vma=False)
```
